32 devices in a mesh: dp: 8 (over z, y), seq: 2 (over x), tensor: 2 (over core).
Axes of the slice: x: 2, y: 2, z: 4, core: 2. Of those that a mesh axis runs over, the one named last changes fastest.
Arguments:
- latents: bfloat16 [2, 8, 32, 32, 2240], P(None, 'dp', 'seq'), may hold values from -6 to 6
- text: bfloat16 [2, 8, 300, 2240], P(None, 'dp'), may hold values from -6 to 6
- timesteps: int32 [2, 8], P(None, 'dp'), may hold values from 0 to 999
- text_lengths: int32 [2, 8], P(None, 'dp'), may hold values from 1 to 300, as said below
- cotangent: bfloat16 [2, 8, 32, 32, 2240], P(None, 'dp', 'seq'), may hold values from -6 to 6
- table: float32 [6, 2240], replicated
- self_qkv: bfloat16 [3, 2240, 2240], P(None, ('dp', 'seq'), 'tensor')
- self_out: bfloat16 [2240, 2240], P('tensor', ('dp', 'seq')), may hold values from -0.75 to 0.75
- cross_q: bfloat16 [2240, 2240], P(('dp', 'seq'), 'tensor')
- cross_kv: bfloat16 [2, 2240, 2240], P(None, ('dp', 'seq'), 'tensor'), may hold values from -0.125 to 0.125
- cross_out: bfloat16 [2240, 2240], P('tensor', ('dp', 'seq')), may hold values from -0.5 to 0.5
- up_w: bfloat16 [2, 2240, 5600], P(None, ('dp', 'seq'), 'tensor')
- up_b: float32 [2, 5600], P(None, 'tensor'), may hold values from -3 to 3
- conv_w: float32 [9, 2, 5600], P(None, None, 'tensor'), may hold values from -2 to 2
- conv_b: float32 [2, 5600], P(None, 'tensor'), may hold values from -3 to 3
- down_w: bfloat16 [5600, 2240], P('tensor', ('dp', 'seq')), may hold values from -0.21875 to 0.21875
Outputs:
- output: bfloat16 [2, 8, 32, 32, 2240], P(None, 'dp', 'seq')
- latents_grad: float32 [2, 8, 32, 32, 2240], P(None, 'dp', 'seq')
- table_grad: float32 [6, 2240], replicated
- self_qkv_grad: float32 [3, 2240, 2240], P(None, ('dp', 'seq'), 'tensor')
- self_out_grad: float32 [2240, 2240], P('tensor', ('dp', 'seq'))
- cross_q_grad: float32 [2240, 2240], P(('dp', 'seq'), 'tensor')
- cross_kv_grad: float32 [2, 2240, 2240], P(None, ('dp', 'seq'), 'tensor')
- cross_out_grad: float32 [2240, 2240], P('tensor', ('dp', 'seq'))
- up_w_grad: float32 [2, 2240, 5600], P(None, ('dp', 'seq'), 'tensor')
- up_b_grad: float32 [2, 5600], P(None, 'tensor')
- conv_w_grad: float32 [9, 2, 5600], P(None, None, 'tensor')
- conv_b_grad: float32 [2, 5600], P(None, 'tensor')
- down_w_grad: float32 [5600, 2240], P('tensor', ('dp', 'seq'))
- cross_q_clipped: float32 [2240, 2240], P(('dp', 'seq'), 'tensor')
- cross_k_clipped: float32 [2240, 2240], P(('dp', 'seq'), 'tensor')
The draws below stay inside these ranges and needn't reach their ends.
Inputs may be any that keep to these rules, and one draw needn't show every extreme that they name: `text_lengths`: for each latent position, at least one of the 2 micro-batches has length 300.
All inputs are finite; a program needn't handle non-finite values.
Results may differ from the reference program's by a relative error of at most 0.03.
Values may be sent and summed in bfloat16 or wider, within the bound.
A program may use at most 536 MiB of HBM per device.

```python
import math
import jax
import jax.numpy as jnp
from jax import lax

D = 2240
HEADS = 70
FF = 5600
HEAD_DIM = 32
TXT = 300
ROWS = 32
COLS = 32
MICRO = 2
LATENTS = 8


def draw_text_lengths(key, part):
    key = jax.random.fold_in(key, 5)
    drawn = jax.random.randint(jax.random.fold_in(key, 1), (MICRO, LATENTS), 1, TXT + 1)
    chosen = jax.random.randint(jax.random.fold_in(key, 2), (LATENTS,), 0, MICRO)
    longest = jnp.arange(MICRO)[:, None] == chosen[None, :]
    return jnp.where(longest, TXT, drawn).astype(jnp.int32)


def draw_cross_q(key, part):
    key = jax.random.fold_in(key, 11)
    entries = jax.random.truncated_normal(jax.random.fold_in(key, 1), -4.0, 4.0, (D, D), jnp.float32)
    head_scale = jnp.exp(jax.random.uniform(jax.random.fold_in(key, 2), (HEADS,), jnp.float32, -0.75, 0.55))
    column_scale = jnp.repeat(head_scale, HEAD_DIM)
    return (entries * column_scale[None, :] * D ** (-0.5)).astype(jnp.bfloat16)


def draw_self_qkv(key, part):
    key = jax.random.fold_in(key, 13)
    entries = jax.random.truncated_normal(jax.random.fold_in(key, 1), -4.0, 4.0, (3, D, D), jnp.float32)
    head_scale = jnp.exp(jax.random.uniform(jax.random.fold_in(key, 2), (2, HEADS), jnp.float32, 0.69, 1.39))
    column_scale = jnp.repeat(head_scale, HEAD_DIM, axis=1)
    query_key = entries[:2] * column_scale[:, None, :]
    offset = jax.random.randint(jax.random.fold_in(key, 3), (HEADS,), 1, HEAD_DIM)
    within = (jnp.arange(HEAD_DIM)[None, :] + offset[:, None]) % HEAD_DIM
    source = (jnp.arange(HEADS)[:, None] * HEAD_DIM + within).reshape(D)
    signs = (2 * jax.random.randint(jax.random.fold_in(key, 4), (D,), 0, 2) - 1).astype(jnp.float32)
    paired = jnp.take(entries[1], source, axis=1) * signs[None, :]
    value_part = 0.8 * paired + 0.6 * entries[2]
    return (jnp.concatenate([query_key, value_part[None]], axis=0) * D ** (-0.5)).astype(jnp.bfloat16)


def draw_table(key, part):
    key = jax.random.fold_in(key, 17)
    entries = jax.random.truncated_normal(jax.random.fold_in(key, 1), -6.0, 6.0, (6, D), jnp.float32)
    row_scale = jnp.array([0.15, 0.5, 0.5, 0.5, 0.5, 1.0], jnp.float32)
    return entries * row_scale[:, None]


def draw_up_w(key, part):
    key = jax.random.fold_in(key, 19)
    entries = jax.random.truncated_normal(jax.random.fold_in(key, 1), -4.0, 4.0, (2, D, FF), jnp.float32)
    common = jax.random.truncated_normal(jax.random.fold_in(key, 2), -4.0, 4.0, (2, FF), jnp.float32)
    return ((entries + common[:, None, :]) * D ** (-0.5)).astype(jnp.bfloat16)


def touch_ends(values, stream_key, low, top_value):
    place = [jax.random.randint(jax.random.fold_in(stream_key, axis), (), 0, length) for axis, length in enumerate(values.shape)]
    widest = values.shape.index(max(values.shape))
    neighbour = place[:widest] + [(place[widest] + 1) % values.shape[widest]] + place[widest + 1:]
    return values.at[tuple(place)].set(low).at[tuple(neighbour)].set(top_value)


def steps_of(rng, extent, shards, low, top_value):
    factor_of, own = 1.0, jax.random.fold_in(rng, 6)
    for dim, shards_of in shards:
        steps = jnp.exp(jax.random.uniform(jax.random.fold_in(own, dim), (shards_of,), jnp.float32, low / len(shards), top_value / len(shards)))
        factor_of = factor_of * jnp.repeat(steps, extent[dim] // shards_of).reshape([-1 if axis == dim else 1 for axis in range(len(extent))])
    return factor_of


def bell_draw(rng, shape, scale, reach, cuts=(), held_as=jnp.bfloat16):
    factor_of = steps_of(rng, shape, cuts, -0.22, 0.18) if cuts else 1.0
    values = jax.random.normal(rng, shape, jnp.float32) * scale * factor_of
    return jnp.minimum(jnp.maximum(values, -reach), reach).astype(held_as)


def setup_inputs(seed: int = 0) -> dict:
    keys = jax.random.split(jax.random.key(seed), 17)
    latents = bell_draw(keys[0], (MICRO, LATENTS, ROWS, COLS, D), 1.0, 6.0, ((1, 8), (2, 2)))
    text = bell_draw(keys[1], (MICRO, LATENTS, TXT, D), 1.0, 6.0, ((1, 8),))
    timesteps = touch_ends(jax.random.randint(keys[2], (MICRO, LATENTS), 0, 1000), jax.random.fold_in(keys[2], 1), 0, 999).astype(jnp.int32)
    text_lengths = draw_text_lengths(jax.random.fold_in(keys[16], 71), 0)
    cotangent = bell_draw(keys[4], (MICRO, LATENTS, ROWS, COLS, D), 1.0, 6.0, ((1, 8), (2, 2)))
    table = draw_table(jax.random.fold_in(keys[16], 71), 0)
    self_qkv = draw_self_qkv(jax.random.fold_in(keys[16], 71), 0)
    self_out = bell_draw(keys[7], (D, D), (max(1, D // 32)) ** -0.5, 0.75, ((0, 2), (1, 16)))
    cross_q = draw_cross_q(jax.random.fold_in(keys[16], 71), 0)
    cross_kv = bell_draw(keys[9], (2, D, D), D ** -0.5, 0.125, ((1, 16), (2, 2)))
    cross_out = bell_draw(keys[10], (D, D), (max(1, D // 16)) ** -0.5, 0.5, ((0, 2), (1, 16)))
    up_w = draw_up_w(jax.random.fold_in(keys[16], 71), 0)
    up_b = bell_draw(keys[12], (2, FF), 0.5, 3.0, ((1, 2),), jnp.float32)
    conv_w = bell_draw(keys[13], (9, 2, FF), 9 ** -0.5, 2.0, ((2, 2),), jnp.float32)
    conv_b = bell_draw(keys[14], (2, FF), 0.5, 3.0, ((1, 2),), jnp.float32)
    down_w = bell_draw(keys[15], (FF, D), (max(1, FF // 8)) ** -0.5, 0.21875, ((0, 2), (1, 16)))
    return dict(latents=latents, text=text, timesteps=timesteps, text_lengths=text_lengths, cotangent=cotangent, table=table, self_qkv=self_qkv, self_out=self_out, cross_q=cross_q, cross_kv=cross_kv, cross_out=cross_out, up_w=up_w, up_b=up_b, conv_w=conv_w, conv_b=conv_b, down_w=down_w)


@jax.custom_vjp
def low(v):
    return lax.optimization_barrier(v.astype(jnp.bfloat16)).astype(jnp.float32)

@jax.custom_vjp
def low_back(v):
    return v

def low_keep(v):
    return (low(v), None)

def low_pass(kept, grad):
    return (grad,)

def back_keep(v):
    return (v, None)

def back_low(kept, grad):
    return (low(grad),)
low.defvjp(low_keep, low_pass)
low_back.defvjp(back_keep, back_low)
peak_logit = lax.Precision.HIGHEST
norm_eps = 1e-06
attn_eps = 1e-06
clip_tau = 3.5
masked_fill = -1e+30

def layer_norm(values):
    center = values - lax.optimization_barrier(jnp.mean(values, axis=-1, keepdims=True))
    spread = lax.optimization_barrier(jnp.mean(center * center, axis=-1, keepdims=True))
    return center * lax.rsqrt(spread + norm_eps)

def modulate(values, offset, stretch):
    return layer_norm(values) * (1.0 + stretch) + offset

def time_rows(timestep, features):
    channel = jnp.arange(features, dtype=jnp.float32)
    frequency = jnp.exp(-math.log(10000.0) * channel / features)
    phases = jnp.arange(6, dtype=jnp.float32)
    return 0.5 * jnp.sin(timestep.astype(jnp.float32) * frequency[None, :] + phases[:, None])

def sana_block(resid_in, caption, timestep, length, table, self_qkv, self_out, cross_q, cross_kv, cross_out, up_w, up_b, conv_w, conv_b, down_w):
    tokens = ROWS * COLS
    modulation = table + time_rows(timestep, D)
    normed = low(modulate(resid_in, modulation[0], modulation[1]))
    projected = low_back(jnp.einsum('td,jde->jte', normed, self_qkv, precision=peak_logit))
    query_rows = low(jax.nn.softplus(projected[0])).reshape(tokens, HEADS, HEAD_DIM)
    every_key = low(jax.nn.softplus(projected[1])).reshape(tokens, HEADS, HEAD_DIM)
    every_value = low(projected[2]).reshape(tokens, HEADS, HEAD_DIM)
    key_value_state = jnp.einsum('sug,suw->ugw', every_key, every_value, precision=peak_logit)
    key_total = lax.optimization_barrier(jnp.sum(every_key, axis=0))
    weighted_numerator = jnp.einsum('ruc,uci->rui', query_rows, key_value_state, precision=peak_logit)
    denominator = jnp.einsum('thk,hk->th', query_rows, key_total, precision=peak_logit) + attn_eps
    mixed_heads = low((weighted_numerator / denominator[:, :, None]).reshape(tokens, D))
    self_term = low_back(jnp.dot(mixed_heads, self_out, precision=peak_logit))
    resid_a = resid_in + modulation[2] * self_term
    cross_input = low(resid_a)
    cross_query = low(low_back(jnp.dot(cross_input, cross_q, precision=peak_logit))).reshape(tokens, HEADS, HEAD_DIM)
    text_proj = low_back(jnp.einsum('md,jde->jme', caption, cross_kv, precision=peak_logit))
    text_keys = low(text_proj[0]).reshape(TXT, HEADS, HEAD_DIM)
    text_values = low(text_proj[1]).reshape(TXT, HEADS, HEAD_DIM)
    scores = low_back(jnp.einsum('thk,mhk->htm', cross_query, text_keys, precision=peak_logit) * HEAD_DIM ** (-0.5))
    visible = jnp.arange(TXT) < length
    masked = jnp.where(visible[None, None, :], scores, masked_fill)
    row_max = lax.optimization_barrier(jnp.max(masked, axis=2, keepdims=True))
    exponent = jnp.exp(masked - row_max)
    probability = low(exponent / lax.optimization_barrier(jnp.sum(exponent, axis=2, keepdims=True)))
    attended = low(low_back(jnp.einsum('htm,mhk->thk', probability, text_values, precision=peak_logit))).reshape(tokens, D)
    cross_term = low_back(jnp.dot(attended, cross_out, precision=peak_logit))
    resid_b = resid_a + cross_term
    normed_ffn = low(modulate(resid_b, modulation[3], modulation[4]))
    up_proj = low_back(jnp.einsum('td,jde->jte', normed_ffn, up_w, precision=peak_logit)) + up_b[:, None, :]
    activated = low(jax.nn.silu(up_proj)).reshape(2, ROWS, COLS, FF)
    padded = jnp.pad(activated, ((0, 0), (1, 1), (1, 1), (0, 0)))
    convolved = jnp.zeros((2, ROWS, COLS, FF), jnp.float32) + conv_b[:, None, None, :]
    for row_tap in range(3):
        for col_tap in range(3):
            window = padded[:, row_tap:row_tap + ROWS, col_tap:col_tap + COLS, :]
            convolved = convolved + window * conv_w[3 * row_tap + col_tap][:, None, None, :]
    gated_units = low(convolved[0] * jax.nn.silu(convolved[1])).reshape(tokens, FF)
    ffn_out = low_back(jnp.dot(gated_units, down_w, precision=peak_logit))
    resid_c = resid_b + modulation[5] * ffn_out
    return (low(resid_c), lax.optimization_barrier(jnp.max(masked, axis=(1, 2))))

def reference(latents, text, timesteps, text_lengths, cotangent, table, self_qkv, self_out, cross_q, cross_kv, cross_out, up_w, up_b, conv_w, conv_b, down_w):
    parameters = tuple((weight.astype(jnp.float32) for weight in (table, self_qkv, self_out, cross_q, cross_kv, cross_out, up_w, up_b, conv_w, conv_b, down_w)))
    latent_count = MICRO * LATENTS
    tokens = ROWS * COLS
    samples = (latents.astype(jnp.float32).reshape(latent_count, tokens, D), text.astype(jnp.float32).reshape(latent_count, TXT, D), timesteps.reshape(latent_count), text_lengths.reshape(latent_count), cotangent.astype(jnp.float32).reshape(latent_count, tokens, D))

    def one_latent(running, sample):
        grad_sums, head_peaks = running
        resid_in, caption, timestep, length, incoming = sample

        def wrapped(residual, *weights):
            return sana_block(residual, caption, timestep, length, *weights)
        output, pullback, peak_now = jax.vjp(wrapped, resid_in, *parameters, has_aux=True)
        gradients = pullback(incoming)
        grad_sums = tuple((running_sum + new_grad for running_sum, new_grad in zip(grad_sums, gradients[1:])))
        return ((grad_sums, jnp.maximum(head_peaks, peak_now)), (output, gradients[0]))
    zeros_init = tuple((jnp.zeros(weight.shape, jnp.float32) for weight in parameters))
    start_peak = jnp.full((HEADS,), masked_fill, jnp.float32)
    (grad_sums, head_peaks), (outputs, input_grads) = lax.scan(one_latent, (zeros_init, start_peak), samples)
    factor = jnp.repeat(jnp.sqrt(clip_tau / jnp.maximum(head_peaks, clip_tau)), HEAD_DIM)
    clipped_q = parameters[3] * factor[None, :]
    clipped_k = parameters[4][0] * factor[None, :]
    out_shape = (MICRO, LATENTS, ROWS, COLS, D)
    return (outputs.reshape(out_shape).astype(jnp.bfloat16), input_grads.reshape(out_shape), grad_sums[0], grad_sums[1], grad_sums[2], grad_sums[3], grad_sums[4], grad_sums[5], grad_sums[6], grad_sums[7], grad_sums[8], grad_sums[9], grad_sums[10], clipped_q, clipped_k)
```

```python
import functools
import math

import jax
import jax.numpy as jnp
from jax import lax
from jax.experimental import pallas as pl
from jax.experimental.pallas import tpu as pltpu
from jax.sharding import PartitionSpec as P

DP, SEQ, TP = "dp", "seq", "tensor"
HEAD_DIM = 32
LANES = 128
NORM_EPS = 1e-06
ATTN_EPS = 1e-06
CLIP_TAU = 3.5
MASKED_FILL = -1e30
F32, BF16 = jnp.float32, jnp.bfloat16
VMEM_LIMIT = 48 * 1024 * 1024


def up_to(value, step):
    return -(-value // step) * step


def dot(left, right, left_dim, right_dim):
    return lax.dot_general(
        left, right, (((left_dim,), (right_dim,)), ((), ())), preferred_element_type=F32
    )


def split(values):
    high = values.astype(BF16)
    return high, (values - high.astype(F32)).astype(BF16)


def ring_of(axis):
    size = lax.axis_size(axis)
    if axis == DP and size % 2 == 0:
        return list(range(0, size, 2)) + list(range(size - 1, 0, -2))
    return list(range(size))


def ring_place(axis):
    size, index = lax.axis_size(axis), lax.axis_index(axis)
    if axis == DP and size % 2 == 0:
        return jnp.where(index % 2 == 0, index // 2, size - 1 - index // 2)
    return index


def ring_member(axis, place):
    size = lax.axis_size(axis)
    if axis == DP and size % 2 == 0:
        return jnp.where(place < size // 2, 2 * place, 2 * (size - 1 - place) + 1)
    return place


def shift(values, axis, step):
    cycle = ring_of(axis)
    size = len(cycle)
    return lax.ppermute(values, axis, [(cycle[i], cycle[(i + step) % size]) for i in range(size)])


def ring_gather(own, axis, flip):
    size = lax.axis_size(axis)
    pieces = [own] + [None] * (size - 1)
    ahead = size // 2 if not flip else size - 1 - size // 2
    for a in range(1, ahead + 1):
        pieces[a] = shift(pieces[a - 1], axis, 1)
    for a in range(size - 1, ahead, -1):
        pieces[a] = shift(pieces[(a + 1) % size], axis, -1)
    return pieces


def ring_scatter(blocks, axis, flip):
    size = lax.axis_size(axis)
    ahead = size // 2 if not flip else size - 1 - size // 2
    total = blocks[0]().astype(F32)
    if ahead > 0:
        running = blocks[ahead]().astype(BF16)
        for a in range(ahead - 1, 0, -1):
            running = (shift(running, axis, -1).astype(F32) + blocks[a]()).astype(BF16)
        total = total + shift(running, axis, -1).astype(F32)
    if ahead < size - 1:
        running = blocks[ahead + 1]().astype(BF16)
        for a in range(ahead + 2, size):
            running = (shift(running, axis, 1).astype(F32) + blocks[a]()).astype(BF16)
        total = total + shift(running, axis, 1).astype(F32)
    return total


def gather_rows(shard, long_first, flip):
    if long_first:
        near = jnp.concatenate(ring_gather(shard, DP, flip), axis=0)
        return jnp.concatenate(ring_gather(near, SEQ, False), axis=0)
    pair = jnp.stack(ring_gather(shard, SEQ, False))
    pieces = ring_gather(pair, DP, flip)
    return jnp.concatenate([piece[b] for b in range(pair.shape[0]) for piece in pieces], axis=0)


def scatter_rows(parts, long_first, flip):
    dp_size = lax.axis_size(DP)
    parts = [part.reshape(dp_size, part.shape[0] // dp_size, part.shape[1]) for part in parts]
    if long_first:
        near = ring_scatter([lambda b=b: parts[b].astype(F32) for b in range(len(parts))], SEQ, False)
        return ring_scatter([lambda a=a: near[a] for a in range(dp_size)], DP, flip)
    far = [
        ring_scatter([lambda a=a, part=part: part[a].astype(F32) for a in range(dp_size)], DP, flip)
        for part in parts
    ]
    return ring_scatter([lambda b=b: far[b] for b in range(len(far))], SEQ, False)


def butterfly(values, axes, combine):
    for axis in axes:
        size = lax.axis_size(axis)
        bit = 1
        while bit < size:
            values = combine(values, lax.ppermute(values, axis, [(i, i ^ bit) for i in range(size)]))
            bit *= 2
    return values


def other_core(values):
    return lax.ppermute(values, TP, [(0, 1), (1, 0)])


def head_block():
    row = lax.broadcasted_iota(jnp.int32, (LANES, LANES), 0) // HEAD_DIM
    col = lax.broadcasted_iota(jnp.int32, (LANES, LANES), 1) // HEAD_DIM
    return row == col


def fold(state, total):
    state = jnp.where(head_block(), state, 0.0)
    rows = sum(state[i * HEAD_DIM : (i + 1) * HEAD_DIM] for i in range(LANES // HEAD_DIM))
    return jnp.concatenate([rows, total, jnp.zeros((7, LANES), F32)], axis=0)


def unfold(folded):
    state = jnp.concatenate([folded[:HEAD_DIM]] * (LANES // HEAD_DIM), axis=0)
    return jnp.where(head_block(), state, 0.0), folded[HEAD_DIM : HEAD_DIM + 1]


def softplus(values):
    return jnp.maximum(values, 0.0) + jnp.log1p(jnp.exp(-jnp.abs(values)))


def head_sum(values):
    ones = jnp.where(head_block(), 1.0, 0.0).astype(BF16)
    high, low = split(values)
    return dot(high, ones, 1, 0) + dot(low, ones, 1, 0)


def state_kernel(key_ref, value_ref, state_ref):
    key = softplus(key_ref[...]).astype(BF16)
    value = value_ref[...].astype(BF16)
    total = jnp.sum(key.astype(F32), axis=0, keepdims=True)
    state_ref[0, 0] = fold(dot(key, value, 0, 0), total)


def ratio_parts(query_ref, state_ref):
    query = softplus(query_ref[...]).astype(BF16)
    state, total = unfold(state_ref[0, 0])
    high, low = split(state)
    numerator = dot(query, high, 1, 0) + dot(query, low, 1, 0)
    denominator = head_sum(query.astype(F32) * total) + ATTN_EPS
    return query, high, low, total, numerator, denominator


def mix_kernel(query_ref, state_ref, mixed_ref):
    query, high, low, total, numerator, denominator = ratio_parts(query_ref, state_ref)
    mixed_ref[...] = (numerator / denominator).astype(BF16)


def mix_back_kernel(query_ref, state_ref, grad_ref, query_grad_ref, state_grad_ref):
    query, high, low, total, numerator, denominator = ratio_parts(query_ref, state_ref)
    mixed_grad = grad_ref[...]
    numer_grad = mixed_grad / denominator
    denom_grad = -head_sum(mixed_grad * numerator) / (denominator * denominator)
    up, down = split(numer_grad)
    state_grad = dot(query, up, 0, 0) + dot(query, down, 0, 0)
    total_grad = jnp.sum(query.astype(F32) * denom_grad, axis=0, keepdims=True)
    state_grad_ref[0, 0] = fold(state_grad, total_grad)
    side = dot(up, high, 1, 1) + dot(up, low, 1, 1) + dot(down, high, 1, 1) + denom_grad * total
    query_grad_ref[...] = (side * jax.nn.sigmoid(query_ref[...])).astype(BF16)


def state_back_kernel(key_ref, value_ref, state_ref, out_ref):
    state, total = unfold(state_ref[0, 0])
    high, low = split(state)

    @pl.when(pl.program_id(0) == 0)
    def _():
        value = value_ref[...].astype(BF16)
        side = dot(value, high, 1, 1) + dot(value, low, 1, 1) + total
        out_ref[...] = (side * jax.nn.sigmoid(key_ref[...])).astype(BF16)

    @pl.when(pl.program_id(0) == 1)
    def _():
        key = softplus(key_ref[...]).astype(BF16)
        out_ref[...] = (dot(key, high, 1, 0) + dot(key, low, 1, 0)).astype(BF16)


def head_of(values, head):
    lane = lax.broadcasted_iota(jnp.int32, values.shape, 1) // HEAD_DIM
    return jnp.where(lane == head, values, jnp.zeros_like(values))


def weigh(key_head, query, visible):
    scores = dot(key_head, query, 1, 1) * HEAD_DIM ** (-0.5)
    masked = jnp.where(visible, scores, MASKED_FILL)
    top = jnp.max(masked, axis=0, keepdims=True)
    exponent = jnp.exp(masked - top)
    return exponent * (1.0 / jnp.sum(exponent, axis=0, keepdims=True)), top


def cross_kernel(length_ref, query_ref, key_ref, value_ref, out_ref, peak_ref):
    query, key, value = query_ref[...], key_ref[...], value_ref[...]
    tokens, slots = query.shape[0], key.shape[0]
    visible = lax.broadcasted_iota(jnp.int32, (slots, tokens), 0) < length_ref[pl.program_id(0)]
    total = jnp.zeros((LANES, tokens), F32)
    peak_ref[0, 0] = jnp.zeros((8, LANES), F32)
    for head in range(LANES // HEAD_DIM):
        probability, top = weigh(head_of(key, head), query, visible)
        total = total + dot(head_of(value, head), probability.astype(BF16), 0, 0)
        peak_ref[0, 0, head : head + 1] = jnp.broadcast_to(jnp.max(top, axis=1, keepdims=True), (1, LANES))
    out_ref[...] = total.T.astype(BF16)


def cross_back_kernel(length_ref, query_ref, key_ref, value_ref, grad_ref, query_grad_ref, key_grad_ref, value_grad_ref):
    query, key, value, grad = query_ref[...], key_ref[...], value_ref[...], grad_ref[...]
    tokens, slots = query.shape[0], key.shape[0]
    visible = lax.broadcasted_iota(jnp.int32, (slots, tokens), 0) < length_ref[pl.program_id(0)]
    query_grad = jnp.zeros((LANES, tokens), F32)
    key_grad = jnp.zeros((slots, LANES), F32)
    value_grad = jnp.zeros((slots, LANES), F32)
    for head in range(LANES // HEAD_DIM):
        key_head = head_of(key, head)
        probability, top = weigh(key_head, query, visible)
        prob_grad = dot(head_of(value, head), grad, 1, 1)
        value_grad = value_grad + head_of(dot(probability.astype(BF16), grad, 1, 0), head)
        mean = jnp.sum(probability * prob_grad, axis=0, keepdims=True)
        score_grad = (probability * (prob_grad - mean)).astype(BF16)
        key_grad = key_grad + head_of(dot(score_grad, query, 1, 0), head)
        query_grad = query_grad + dot(key_head, score_grad, 0, 0)
    scale = HEAD_DIM ** (-0.5)
    query_grad_ref[...] = (query_grad * scale).T.astype(BF16)
    key_grad_ref[...] = (key_grad * scale).astype(BF16)
    value_grad_ref[...] = value_grad.astype(BF16)


def silu(values):
    return values * jax.nn.sigmoid(values)


def silu_slope(values):
    sigma = jax.nn.sigmoid(values)
    return sigma * (1.0 + values * (1.0 - sigma))


def columns_of(values, cols):
    place = lax.broadcasted_iota(jnp.int32, values.shape, 0) % cols
    count = values.shape[0]
    left = jnp.where(place == 0, 0.0, pltpu.roll(values, 1, 0))
    right = jnp.where(place == cols - 1, 0.0, pltpu.roll(values, count - 1, 0))
    return left, values, right


def strips_of(tokens, cols):
    size = 4 * cols if tokens % (4 * cols) == 0 else cols
    return [(at, size) for at in range(0, tokens, size)]


def stage_columns(scratch, top, middle, bottom, cols):
    tokens = middle.shape[0]
    full = jnp.concatenate([top.astype(F32), middle, bottom.astype(F32)], axis=0)
    for place, part in enumerate(columns_of(full, cols)):
        scratch[place] = part


def taps(scratch, weight, at, size, cols, mirror):
    result = None
    for row_tap in range(3):
        for col_tap in range(3):
            row_at = 2 - row_tap if mirror else row_tap
            col_at = 2 - col_tap if mirror else col_tap
            tap = 3 * row_tap + col_tap
            term = scratch[col_at, at + row_at * cols : at + row_at * cols + size] * weight[tap : tap + 1]
            result = term if result is None else result + term
    return result


def conv_kernel(cols, z0, z1, top0, top1, bottom0, bottom1, w_ref, b_ref, out_ref, s0, s1):
    tokens = z0.shape[0]
    for z, top, bottom, scratch in ((z0, top0, bottom0, s0), (z1, top1, bottom1, s1)):
        stage_columns(scratch, top[0], silu(z[...]).astype(BF16).astype(F32), bottom[0], cols)
    for at, size in strips_of(tokens, cols):
        first = taps(s0, w_ref[0], at, size, cols, False) + b_ref[0, 0:1]
        second = taps(s1, w_ref[1], at, size, cols, False) + b_ref[1, 0:1]
        out_ref[at : at + size] = (first * silu(second)).astype(BF16)


def conv_back_kernel(cols, z0, z1, top0, top1, bottom0, bottom1, grad_ref, w_ref, b_ref, out0, out1, small_ref, s0, s1):
    tokens = z0.shape[0]
    for z, top, bottom, scratch in ((z0, top0, bottom0, s0), (z1, top1, bottom1, s1)):
        stage_columns(scratch, top[0], silu(z[...]).astype(BF16).astype(F32), bottom[0], cols)
    sums = [jnp.zeros((8, LANES), F32) for _ in range(20)]
    for at, size in strips_of(tokens, cols):
        first = taps(s0, w_ref[0], at, size, cols, False) + b_ref[0, 0:1]
        second = taps(s1, w_ref[1], at, size, cols, False) + b_ref[1, 0:1]
        grad = grad_ref[at : at + size]
        sigma = jax.nn.sigmoid(second)
        slope = sigma * (1.0 + second * (1.0 - sigma))
        for j, (part, scratch, out) in enumerate(
            ((grad * second * sigma, s0, out0), (grad * first * slope, s1, out1))
        ):
            out[at : at + size] = part.astype(BF16)
            for row_tap in range(3):
                for col_tap in range(3):
                    start = at + row_tap * cols
                    product = part * scratch[col_tap, start : start + size]
                    place = 9 * j + 3 * row_tap + col_tap
                    sums[place] = sums[place] + jnp.sum(product.reshape(size // 8, 8, LANES), axis=0)
            sums[18 + j] = sums[18 + j] + jnp.sum(part.reshape(size // 8, 8, LANES), axis=0)
    for place in range(20):
        small_ref[0, place : place + 1] = jnp.sum(sums[place], axis=0, keepdims=True)
    small_ref[0, 20:24] = jnp.zeros((4, LANES), F32)


def act_back_kernel(cols, z_ref, grad_ref, top, bottom, w_ref, out_ref, bias_ref, scratch):
    tokens = z_ref.shape[0]
    stage_columns(scratch, top[0], grad_ref[...].astype(F32), bottom[0], cols)
    total = jnp.zeros((8, LANES), F32)
    for at, size in strips_of(tokens, cols):
        part = taps(scratch, w_ref[0], at, size, cols, True) * silu_slope(z_ref[at : at + size])
        out_ref[at : at + size] = part.astype(BF16)
        total = total + jnp.sum(part.reshape(size // 8, 8, LANES), axis=0)
    bias_ref[0] = jnp.broadcast_to(jnp.sum(total, axis=0, keepdims=True), (8, LANES))


def call(kernel, grid, in_specs, out_specs, out_shape, flops, moved, scratch=(), **extra):
    return pl.pallas_call(
        kernel,
        grid=grid,
        in_specs=in_specs,
        out_specs=out_specs,
        out_shape=out_shape,
        scratch_shapes=list(scratch),
        compiler_params=pltpu.CompilerParams(vmem_limit_bytes=VMEM_LIMIT),
        cost_estimate=pl.CostEstimate(flops=int(flops), bytes_accessed=int(moved), transcendentals=0),
        **extra,
    )


def struct(shape, dtype):
    return jax.ShapeDtypeStruct(shape, dtype)


class Kernels:
    def __init__(self, micro, tokens, cols, width, hidden, slots):
        self.micro, self.tokens, self.cols = micro, tokens, cols
        self.width, self.hidden, self.slots = width, hidden, slots
        self.groups, self.units = width // LANES, hidden // LANES

    def tile(self, offset=0):
        return pl.BlockSpec((self.tokens, LANES), lambda m, g: (m, g + offset))

    def folded(self):
        return pl.BlockSpec((1, 1, HEAD_DIM + 8, LANES), lambda m, g: (m, g, 0, 0))

    def folded_shape(self):
        return struct((self.micro, self.groups, HEAD_DIM + 8, LANES), F32)

    def states(self, keys_values):
        size = self.micro * self.tokens * self.width
        return call(
            state_kernel, (self.micro, self.groups), [self.tile(), self.tile(self.groups)],
            self.folded(), self.folded_shape(), size * 600, size * 8,
        )(keys_values, keys_values)

    def mix(self, queries, states):
        size = self.micro * self.tokens * self.width
        return call(
            mix_kernel, (self.micro, self.groups), [self.tile(), self.folded()],
            self.tile(), struct(queries.shape, BF16), size * 1500, size * 6,
        )(queries, states)

    def mix_back(self, queries, states, mixed_grad):
        size = self.micro * self.tokens * self.width
        return call(
            mix_back_kernel, (self.micro, self.groups), [self.tile(), self.folded(), self.tile()],
            [self.tile(), self.folded()], [struct(queries.shape, BF16), self.folded_shape()],
            size * 4000, size * 10,
        )(queries, states, mixed_grad)

    def states_back(self, keys_values, state_grad):
        groups = self.groups
        size = self.micro * self.tokens * self.width
        tile = lambda offset: pl.BlockSpec((self.tokens, LANES), lambda j, m, g: (m, g + offset))
        return call(
            state_back_kernel, (2, self.micro, groups),
            [tile(0), tile(groups), pl.BlockSpec((1, 1, HEAD_DIM + 8, LANES), lambda j, m, g: (m, g, 0, 0))],
            pl.BlockSpec((self.tokens, LANES), lambda j, m, g: (m, g + j * groups)),
            struct(keys_values.shape, BF16), size * 1500, size * 20,
        )(keys_values, keys_values, state_grad)

    def text_tile(self, offset):
        return pl.BlockSpec((self.slots, LANES), lambda m, g: (m, g + offset))

    def cross(self, lengths, queries, text):
        size = self.micro * self.tokens * self.width
        smem = pl.BlockSpec(memory_space=pltpu.SMEM)
        peak = pl.BlockSpec((1, 1, 8, LANES), lambda m, g: (m, g, 0, 0))
        return call(
            cross_kernel, (self.micro, self.groups),
            [smem, self.tile(), self.text_tile(0), self.text_tile(self.groups)],
            [self.tile(), peak],
            [struct(queries.shape, BF16), struct((self.micro, self.groups, 8, LANES), F32)],
            size * 20000, size * 6,
        )(lengths, queries, text, text)

    def cross_back(self, lengths, queries, text, attended_grad):
        size = self.micro * self.tokens * self.width
        smem = pl.BlockSpec(memory_space=pltpu.SMEM)
        return call(
            cross_back_kernel, (self.micro, self.groups),
            [smem, self.tile(), self.text_tile(0), self.text_tile(self.groups), self.tile()],
            [self.tile(), self.text_tile(0), self.text_tile(0)],
            [struct(queries.shape, BF16), struct((text.shape[0], self.width), BF16), struct((text.shape[0], self.width), BF16)],
            size * 50000, size * 6,
        )(lengths, queries, text, text, attended_grad)

    def edge(self, offset=0):
        return pl.BlockSpec((1, self.cols, LANES), lambda m, g: (m, 0, g + offset))

    def scratch(self):
        return pltpu.VMEM((3, self.tokens + 2 * self.cols, LANES), F32)

    def conv_specs(self):
        units = self.units
        return (
            [self.tile(), self.tile(units), self.edge(), self.edge(units), self.edge(), self.edge(units)],
            [
                pl.BlockSpec((2, 9, LANES), lambda m, g: (0, 0, g)),
                pl.BlockSpec((2, 1, LANES), lambda m, g: (0, 0, g)),
            ],
        )

    def conv(self, pre, top, bottom, conv_w, conv_b):
        size = self.micro * self.tokens * self.hidden
        data, weights = self.conv_specs()
        return call(
            functools.partial(conv_kernel, self.cols), (self.micro, self.units), data + weights,
            self.tile(), struct((pre.shape[0], self.hidden), BF16), size * 20000, size * 10,
            [self.scratch(), self.scratch()],
        )(pre, pre, top, top, bottom, bottom, conv_w, conv_b)

    def conv_back(self, pre, top, bottom, grad, conv_w, conv_b):
        size = self.micro * self.tokens * self.hidden
        data, weights = self.conv_specs()
        one = struct((pre.shape[0], self.hidden), BF16)
        return call(
            functools.partial(conv_back_kernel, self.cols), (self.micro, self.units),
            data + [self.tile()] + weights,
            [self.tile(), self.tile(), pl.BlockSpec((1, 24, LANES), lambda m, g: (m, 0, g))],
            [one, one, struct((self.micro, 24, self.hidden), F32)], size * 40000, size * 16,
            [self.scratch(), self.scratch()],
        )(pre, pre, top, top, bottom, bottom, grad, conv_w, conv_b)

    def act_back(self, pre, grad, top, bottom, conv_w):
        size = self.micro * self.tokens * self.hidden
        units = self.units
        return call(
            functools.partial(act_back_kernel, self.cols), (self.micro, 2 * units),
            [
                self.tile(), self.tile(), self.edge(), self.edge(),
                pl.BlockSpec((1, 9, LANES), lambda m, g: (g // units, 0, g % units)),
            ],
            [self.tile(), pl.BlockSpec((1, 8, LANES), lambda m, g: (m, 0, g))],
            [struct(pre.shape, BF16), struct((self.micro, 8, pre.shape[1]), F32)], size * 20000, size * 16,
            [self.scratch()],
        )(pre, grad, top, bottom, conv_w)


def pad_to(values, *sizes):
    return jnp.pad(values, [(0, size - now) for size, now in zip(sizes, values.shape)])


def side_by_side(parts, width):
    return jnp.concatenate([pad_to(part, part.shape[0], width) for part in parts], axis=1)


def halos(rows, cols):
    size = lax.axis_size(SEQ)
    up = [(i, i + 1) for i in range(size - 1)]
    down = [(j, i) for i, j in up]
    return (
        lax.ppermute(rows[:, -cols:], SEQ, up),
        lax.ppermute(rows[:, :cols], SEQ, down),
    )


def shards(latents, text, timesteps, text_lengths, cotangent, table, self_qkv, self_out, cross_q, cross_kv,
           cross_out, up_w, up_b, conv_w, conv_b, down_w):
    micro, _, row_count, cols, features = latents.shape
    tokens = row_count * cols
    own_rows, heads_width = cross_q.shape
    hidden_width = up_b.shape[1]
    text_len = text.shape[2]
    width, hidden, slots = up_to(heads_width, LANES), up_to(hidden_width, LANES), up_to(text_len, 16)
    rows = up_to(own_rows, 16)
    dp_size, seq_size = lax.axis_size(DP), lax.axis_size(SEQ)
    near = dp_size * rows
    wide = seq_size * near
    core = lax.axis_index(TP)
    kernels = Kernels(micro, tokens, cols, width, hidden, slots)

    packed = (
        (pad_to(self_qkv[0], rows, width), False),
        (pad_to(side_by_side([self_qkv[1], self_qkv[2]], width), rows, 2 * width), True),
        (pad_to(self_out.T, rows, width), False),
        (pad_to(cross_q, rows, width), False),
        (pad_to(side_by_side([cross_kv[0], cross_kv[1]], width), rows, 2 * width), True),
        (pad_to(cross_out.T, rows, width), False),
        (pad_to(side_by_side([up_w[0], up_w[1]], hidden), rows, 2 * hidden), True),
        (pad_to(down_w.T, rows, hidden), False),
    )
    flips = (False, True, True, False, False, True, False, True)
    full = []
    for place, ((shard, long_first), flip) in enumerate(zip(packed, flips)):
        full.append(gather_rows(shard, long_first, flip))
    w_q, w_kv, w_so, w_cq, w_ckv, w_co, w_up, w_down = full

    slot = jnp.arange(wide)
    block, row = slot // rows, slot % rows
    back_seq, back_dp = block // dp_size, block % dp_size
    from_seq = (lax.axis_index(SEQ) - back_seq) % seq_size
    from_dp = ring_member(DP, (ring_place(DP) - back_dp) % dp_size)
    valid = row < own_rows
    channel = jnp.where(valid, (from_dp * seq_size + from_seq) * own_rows + row, -1)
    pick = (jnp.arange(features)[:, None] == channel[None, :]).astype(BF16)

    def relative(values):
        return jnp.where(core == 0, values, jnp.flip(values, axis=0))

    lengths = relative(text_lengths[:, 0])
    caption = jnp.pad(relative(text[:, 0]), ((0, 0), (0, slots - text_len), (0, 0))).reshape(micro * slots, features)
    caption = dot(caption, pick, 1, 0).astype(BF16)
    resid_in = dot(lax.dynamic_index_in_dim(latents, core, 0, False).reshape(tokens, features), pick, 1, 0)
    grad_out = dot(lax.dynamic_index_in_dim(cotangent, core, 0, False).reshape(tokens, features), pick, 1, 0)

    frequency = jnp.exp(-math.log(10000.0) * channel.astype(F32) / features)
    time = lax.dynamic_index_in_dim(timesteps[:, 0], core, 0, False).astype(F32)
    waves = 0.5 * jnp.sin(time * frequency[None, :] + jnp.arange(6, dtype=F32)[:, None])
    mod_table = jnp.dot(table, pick.astype(F32), precision=lax.Precision.HIGHEST)
    modulation = jnp.where(valid[None, :], mod_table + waves, 0.0)
    shift_a, scale_a, gate_a, shift_f, scale_f, gate_f = [modulation[i] for i in range(6)]

    def normalise(values):
        center = jnp.where(valid[None, :], values - jnp.sum(values, axis=1, keepdims=True) / features, 0.0)
        spread = jnp.sum(center * center, axis=1, keepdims=True) / features
        inverse = lax.rsqrt(spread + NORM_EPS)
        return center * inverse, inverse

    def normalise_back(values, grad, stretch):
        unit, inverse = normalise(values)
        shift_grad = jnp.sum(grad, axis=0)
        scale_grad = jnp.sum(grad * unit, axis=0)
        scaled = grad * (1.0 + stretch)
        mean = jnp.sum(scaled, axis=1, keepdims=True) / features
        along = jnp.sum(scaled * unit, axis=1, keepdims=True) / features
        return jnp.where(valid[None, :], inverse * (scaled - mean - unit * along), 0.0), shift_grad, scale_grad

    def both(own):
        return jnp.concatenate([own, other_core(own)], axis=0)

    def core_total(parts):
        def product(at):
            return sum(dot(left[at : at + tokens], right, 1, dim) for left, right, dim in parts)

        return other_core(product(tokens).astype(BF16)).astype(F32) + product(0)

    ffn_grad = both((gate_f * grad_out).astype(BF16))

    unit_a, _ = normalise(resid_in)
    normed = both((unit_a * (1.0 + scale_a) + shift_a).astype(BF16))
    queries = dot(normed, w_q, 1, 0)
    keys_values = dot(normed, w_kv, 1, 0)
    states = butterfly(kernels.states(keys_values), (SEQ,), jnp.add)
    mixed = kernels.mix(queries, states)
    self_term = core_total([(mixed, w_so, 1)])
    resid_a = resid_in + gate_a * self_term
    cross_input = both(resid_a.astype(BF16))
    cross_query = dot(cross_input, w_cq, 1, 0).astype(BF16)
    text_proj = dot(caption, w_ckv, 1, 0).astype(BF16)
    attended, peaks = kernels.cross(lengths, cross_query, text_proj)
    resid_b = resid_a + core_total([(attended, w_co, 1)])
    unit_f, _ = normalise(resid_b)
    normed_ffn = both((unit_f * (1.0 + scale_f) + shift_f).astype(BF16))
    bias = side_by_side([up_b[0:1], up_b[1:2]], hidden)
    pre = dot(normed_ffn, w_up, 1, 0) + bias
    edges = jnp.concatenate(
        [pre.reshape(micro, tokens, 2 * hidden)[:, :cols], pre.reshape(micro, tokens, 2 * hidden)[:, -cols:]], axis=1
    )
    top, bottom = halos(silu(edges).astype(BF16), cols)
    filters = pad_to(conv_w.transpose(1, 0, 2), 2, 9, hidden)
    filter_bias = pad_to(conv_b, 2, hidden)[:, None]
    gated = kernels.conv(pre, top, bottom, filters, filter_bias)
    ffn_out = core_total([(gated, w_down, 1)])
    resid_c = resid_b + gate_f * ffn_out
    gate_f_grad = jnp.sum(grad_out * ffn_out, axis=0)

    def weight_grad(activation, grad, long_first, flip):
        parts = [
            dot(activation[:, b * near : (b + 1) * near], grad, 0, 0).astype(BF16) for b in range(seq_size)
        ]
        return scatter_rows(parts, long_first, flip)

    down_grad = weight_grad(ffn_grad, gated, False, True)
    gated_grad = dot(ffn_grad, w_down, 1, 0)
    conv_grad0, conv_grad1, small = kernels.conv_back(pre, top, bottom, gated_grad, filters, filter_bias)
    conv_grad = jnp.concatenate([conv_grad0, conv_grad1], axis=1)
    top_grad, bottom_grad = halos(conv_grad.reshape(micro, tokens, 2 * hidden), cols)
    up_low, bias_grad = kernels.act_back(pre, conv_grad, top_grad, bottom_grad, filters)
    small = butterfly(
        jnp.concatenate([jnp.sum(small, axis=0)[:20], jnp.sum(bias_grad, axis=0)[:1].reshape(2, hidden)], axis=0),
        (SEQ, DP), jnp.add,
    )
    up_grad = weight_grad(normed_ffn, up_low, True, False)
    normed_ffn_grad = core_total([(up_low, w_up, 1)])
    resid_b_part, shift_f_grad, scale_f_grad = normalise_back(resid_b, normed_ffn_grad, scale_f)
    resid_b_grad = grad_out + resid_b_part
    cross_grad = both(resid_b_grad.astype(BF16))
    attended_grad = dot(cross_grad, w_co, 1, 0).astype(BF16)
    cross_out_grad = weight_grad(cross_grad, attended, False, True)
    query_grad, key_grad, value_grad = kernels.cross_back(lengths, cross_query, text_proj, attended_grad)
    cross_kv_grad = weight_grad(caption, jnp.concatenate([key_grad, value_grad], axis=1), True, False)
    resid_a_grad = resid_b_grad + core_total([(query_grad, w_cq, 1)])
    cross_q_grad = weight_grad(cross_input, query_grad, False, False)
    gate_a_grad = jnp.sum(resid_a_grad * self_term, axis=0)
    self_grad = both((gate_a * resid_a_grad).astype(BF16))
    mixed_grad = dot(self_grad, w_so, 1, 0)
    self_out_grad = weight_grad(self_grad, mixed, False, True)
    q_low, state_grad = kernels.mix_back(queries, states, mixed_grad)
    state_grad = butterfly(state_grad, (SEQ,), jnp.add)
    kv_low = kernels.states_back(keys_values, state_grad)
    q_grad = weight_grad(normed, q_low, False, False)
    kv_grad = weight_grad(normed, kv_low, True, True)
    normed_grad = core_total([(q_low, w_q, 1), (kv_low, w_kv, 1)])
    resid_part, shift_a_grad, scale_a_grad = normalise_back(resid_in, normed_grad, scale_a)
    latent_grad = resid_a_grad + resid_part

    def whole(own):
        other = other_core(own)
        pair = jnp.where(core == 0, jnp.stack([own, other]), jnp.stack([other, own]))
        return pair.reshape(micro, 1, row_count, cols, features)

    high, low = split(latent_grad)
    output = whole(dot(resid_c.astype(BF16), pick, 1, 1).astype(BF16))
    latents_grad = whole(dot(high, pick, 1, 1) + dot(low, pick, 1, 1))
    mod_grad = jnp.stack([shift_a_grad, scale_a_grad, gate_a_grad, shift_f_grad, scale_f_grad, gate_f_grad])
    mod_grad = lax.dot_general(
        mod_grad, pick.astype(F32), (((1,), (1,)), ((), ())), precision=lax.Precision.HIGHEST
    )
    table_grad = butterfly(mod_grad, (TP, SEQ, DP), jnp.add)

    head_count = heads_width // HEAD_DIM
    head_peaks = jnp.max(peaks[:, :, : LANES // HEAD_DIM, 0], axis=0).reshape(-1)[:head_count]
    head_peaks = butterfly(head_peaks, (SEQ, DP), jnp.maximum)
    factor = jnp.repeat(jnp.sqrt(CLIP_TAU / jnp.maximum(head_peaks, CLIP_TAU)), HEAD_DIM)

    def cut(grad, count, each, size):
        grad = grad[:own_rows].reshape(own_rows, count, each)[:, :, :size]
        return grad.transpose(1, 0, 2)

    def heads(grad):
        return grad[:own_rows, :heads_width]

    taps_grad = small[:18].reshape(2, 9, hidden)[:, :, :hidden_width].transpose(1, 0, 2)
    return (
        output,
        latents_grad,
        table_grad,
        jnp.concatenate([heads(q_grad)[None], cut(kv_grad, 2, width, heads_width)], axis=0),
        heads(self_out_grad).T,
        heads(cross_q_grad),
        cut(cross_kv_grad, 2, width, heads_width),
        heads(cross_out_grad).T,
        cut(up_grad, 2, hidden, hidden_width),
        small[20:22, :hidden_width],
        taps_grad,
        small[18:20, :hidden_width],
        down_grad[:own_rows, :hidden_width].T,
        cross_q.astype(F32) * factor[None, :],
        cross_kv[0].astype(F32) * factor[None, :],
    )


def solution(mesh):
    tokens = P(None, DP, SEQ, None, None)
    stacked, by_column, by_row = P(None, (DP, SEQ), TP), P(TP, (DP, SEQ)), P((DP, SEQ), TP)
    return jax.shard_map(
        shards,
        mesh=mesh,
        in_specs=(
            tokens, P(None, DP, None, None), P(None, DP), P(None, DP), tokens, P(), stacked, by_column, by_row,
            stacked, by_column, stacked, P(None, TP), P(None, None, TP), P(None, TP), by_column,
        ),
        out_specs=(
            tokens, tokens, P(), stacked, by_column, by_row, stacked, by_column, stacked, P(None, TP),
            P(None, None, TP), P(None, TP), by_column, by_row, by_row,
        ),
        check_vma=False,
    )
```

```python
import functools
import math

import jax
import jax.numpy as jnp
from jax import lax
from jax.experimental import pallas as pl
from jax.experimental.pallas import tpu as pltpu
from jax.sharding import PartitionSpec as P

DP, SEQ, TP = "dp", "seq", "tensor"
HEAD_DIM = 32
LANES = 128
NORM_EPS = 1e-06
ATTN_EPS = 1e-06
CLIP_TAU = 3.5
MASKED_FILL = -1e30
F32, BF16 = jnp.float32, jnp.bfloat16
VMEM_LIMIT = 48 * 1024 * 1024


def up_to(value, step):
    return -(-value // step) * step


def dot(left, right, left_dim, right_dim):
    return lax.dot_general(
        left, right, (((left_dim,), (right_dim,)), ((), ())), preferred_element_type=F32
    )


def split(values):
    high = values.astype(BF16)
    return high, (values - high.astype(F32)).astype(BF16)


def ring_of(axis):
    size = lax.axis_size(axis)
    if axis == DP and size % 2 == 0:
        return list(range(0, size, 2)) + list(range(size - 1, 0, -2))
    return list(range(size))


def ring_place(axis):
    size, index = lax.axis_size(axis), lax.axis_index(axis)
    if axis == DP and size % 2 == 0:
        return jnp.where(index % 2 == 0, index // 2, size - 1 - index // 2)
    return index


def ring_member(axis, place):
    size = lax.axis_size(axis)
    if axis == DP and size % 2 == 0:
        return jnp.where(place < size // 2, 2 * place, 2 * (size - 1 - place) + 1)
    return place


def shift(values, axis, step):
    if isinstance(step, list):
        return lax.ppermute(values, axis, step)
    cycle = ring_of(axis)
    size = len(cycle)
    return lax.ppermute(values, axis, [(cycle[i], cycle[(i + step) % size]) for i in range(size)])


def ring_gather(own, axis, flip):
    size = lax.axis_size(axis)
    pieces = [own] + [None] * (size - 1)
    ahead = size // 2 if not flip else size - 1 - size // 2
    for a in range(1, ahead + 1):
        pieces[a] = shift(pieces[a - 1], axis, 1)
    for a in range(size - 1, ahead, -1):
        pieces[a] = shift(pieces[(a + 1) % size], axis, -1)
    return pieces


def ring_scatter(blocks, axis, flip):
    size = lax.axis_size(axis)
    ahead = size // 2 if not flip else size - 1 - size // 2
    total = blocks[0]().astype(F32)
    if ahead > 0:
        running = blocks[ahead]().astype(BF16)
        for a in range(ahead - 1, 0, -1):
            running = (shift(running, axis, -1).astype(F32) + blocks[a]()).astype(BF16)
        total = total + shift(running, axis, -1).astype(F32)
    if ahead < size - 1:
        running = blocks[ahead + 1]().astype(BF16)
        for a in range(ahead + 2, size):
            running = (shift(running, axis, 1).astype(F32) + blocks[a]()).astype(BF16)
        total = total + shift(running, axis, 1).astype(F32)
    return total


def slot_order(size):
    ahead = size // 2
    order = []
    for step in range(ahead):
        order.append(ahead - step)
        if ahead + 1 + step < size:
            order.append(ahead + 1 + step)
    return order + [0]


def in_slots(pieces):
    return [pieces[a] for a in slot_order(len(pieces))]


class Wire:
    def __init__(self):
        self.running, self.queue, self.last = [], [], ()
        self.stride, self.since = lax.axis_size(DP) // 2, lax.axis_size(DP)

    def join(self, phases):
        self.running.append((phases, next(phases)))

    def push(self, phases):
        self.queue.append(phases)

    def round(self):
        if self.queue and self.since >= self.stride:
            self.join(self.queue.pop(0))
            self.since = 0
        if not self.running:
            return
        self.since += 1
        sends = [send for _, pending in self.running for send in pending]
        values = tuple(value for value, _, _ in sends)
        if self.last:
            values, _ = lax.optimization_barrier((values, self.last))
        arrived = tuple(shift(value, axis, step) for value, (_, axis, step) in zip(values, sends))
        self.last = arrived
        running, at = [], 0
        for phases, pending in self.running:
            mine = arrived[at : at + len(pending)]
            at += len(pending)
            try:
                running.append((phases, phases.send(mine)))
            except StopIteration:
                pass
        self.running = running

    def step(self, value):
        before = self.last
        self.round()
        return lax.optimization_barrier((value, before))[0] if before else value

    def need(self, done):
        while not done:
            self.round()
        return done

    def finish(self):
        while self.running or self.queue:
            self.round()


def butterfly_phases(values, axes, combine, done):
    for axis in axes:
        size = lax.axis_size(axis)
        bit = 1
        while bit < size:
            (arrived,) = yield [(values, axis, [(i, i ^ bit) for i in range(size)])]
            values = combine(values, arrived)
            bit *= 2
    done.append(values)


def columns(values, widths):
    at, parts = 0, []
    for width in widths:
        parts.append(values[:, at : at + width])
        at += width
    return parts


def gather_phases(first, second, done):
    size = lax.axis_size(DP)
    ahead = size // 2
    widths_a, widths_b = [w.shape[1] for w in first], [w.shape[1] for w in second]
    shard_a, shard_b = jnp.concatenate(first, axis=1), jnp.concatenate(second, axis=1)
    n_a, n_b = shard_a.shape[1], shard_b.shape[1]
    rows = shard_a.shape[0]
    (far_b,) = yield [(shard_b, SEQ, 1)]
    pieces = [jnp.concatenate([shard_a, shard_b, far_b], axis=1)] + [None] * (size - 1)
    far = [None] * size
    fresh = [0]
    for hop in range(1, ahead + 2):
        sends, places = [], []
        if hop <= ahead:
            sends.append((pieces[hop - 1], DP, 1))
            places.append(hop)
        if size - hop > ahead:
            sends.append((pieces[(size - hop + 1) % size], DP, -1))
            places.append(size - hop)
        across = [pieces[a][:, :n_a] for a in fresh]
        sends.append((jnp.concatenate(across, axis=0) if len(across) > 1 else across[0], SEQ, 1))
        arrived = yield sends
        for i, a in enumerate(fresh):
            far[a] = arrived[-1][i * rows : (i + 1) * rows]
        for a, piece in zip(places, arrived):
            pieces[a] = piece
        fresh = places
    full = []
    at = 0
    for width in widths_a:
        blocks = [p[:, at : at + width] for p in in_slots(pieces)] + [p[:, at : at + width] for p in in_slots(far)]
        full.append(jnp.concatenate(blocks, axis=0))
        at += width
    for width in widths_b:
        blocks = [p[:, at : at + width] for p in in_slots(pieces)]
        blocks += [p[:, at + n_b : at + n_b + width] for p in in_slots(pieces)]
        full.append(jnp.concatenate(blocks, axis=0))
        at += width
    done.extend(full)


def gather_slow(shard):
    near = jnp.concatenate(in_slots(ring_gather(shard, DP, False)), axis=0)
    return jnp.concatenate(ring_gather(near, SEQ, False), axis=0)


def gather(wire, first, second):
    done = []
    if lax.axis_size(SEQ) == 2:
        wire.push(gather_phases(first, second, done))
    else:
        done.extend(gather_slow(shard) for shard in first + second)
    return done


def scatter_slow(parts):
    dp_size = lax.axis_size(DP)
    order = slot_order(dp_size)
    parts = [part.reshape(dp_size, part.shape[0] // dp_size, part.shape[1]) for part in parts]
    near = ring_scatter([lambda b=b: parts[b].astype(F32) for b in range(len(parts))], SEQ, False)
    return ring_scatter([lambda a=a: near[order.index(a)] for a in range(dp_size)], DP, False)


def scatter_phases(first, second, done):
    size = lax.axis_size(DP)
    ahead = size // 2
    order = slot_order(size)
    rows = first[0][0].shape[0] // size
    widths = [parts[0].shape[1] for parts in first + second]
    n_a = sum(parts[0].shape[1] for parts in first)
    n_b = sum(parts[0].shape[1] for parts in second)

    def block(array, start, count=1):
        return array[start * rows : (start + count) * rows]

    def across(start, count):
        blocks = [block(parts[1], start, count) for parts in first]
        return (jnp.concatenate(blocks, axis=1) if len(blocks) > 1 else blocks[0], SEQ, 1)

    def value(a, far):
        slot = order.index(a)
        near = [block(parts[0], slot) for parts in first]
        near = jnp.concatenate(near, axis=1) if len(near) > 1 else near[0]
        terms = [near.astype(F32) + far[a].astype(F32)]
        for b in range(2):
            terms += [block(parts[b], slot).astype(F32) for parts in second]
        return jnp.concatenate(terms, axis=1)

    def take(far, arrived, start):
        for i in range(arrived.shape[0] // rows):
            far[order[start + i]] = arrived[i * rows : (i + 1) * rows]

    far = {}
    (arrived,) = yield [across(0, 2)]
    take(far, arrived, 0)
    back = forth = None
    for step in range(ahead):
        sends = []
        here = value(ahead - step, far)
        back = here if back is None else back.astype(F32) + here
        sends.append((back.astype(BF16), DP, -1))
        place = ahead + 1 + step
        if place < size:
            here = value(place, far)
            forth = here if forth is None else forth.astype(F32) + here
            sends.append((forth.astype(BF16), DP, 1))
        start = 2 * step + 2
        if start < size:
            sends.append(across(start, min(2, size - start)))
        arrived = yield sends
        back = arrived[0]
        if place < size:
            forth = arrived[1]
        if start < size:
            take(far, arrived[-1], start)
    total = value(0, far) + back.astype(F32) + forth.astype(F32)
    (other,) = yield [(total[:, n_a + n_b :].astype(BF16), SEQ, 1)]
    mine = total[:, n_a : n_a + n_b] + other.astype(F32)
    done.extend(columns(total[:, :n_a], widths[: len(first)]) + columns(mine, widths[len(first) :]))


def scatter(wire, first, second):
    done = []
    if lax.axis_size(SEQ) == 2:
        wire.push(scatter_phases(first, second, done))
    else:
        done.extend(scatter_slow(parts) for parts in first + second)
    return done


def butterfly(values, axes, combine):
    for axis in axes:
        size = lax.axis_size(axis)
        bit = 1
        while bit < size:
            values = combine(values, lax.ppermute(values, axis, [(i, i ^ bit) for i in range(size)]))
            bit *= 2
    return values


def other_core(values):
    return lax.ppermute(values, TP, [(0, 1), (1, 0)])


def head_block():
    row = lax.broadcasted_iota(jnp.int32, (LANES, LANES), 0) // HEAD_DIM
    col = lax.broadcasted_iota(jnp.int32, (LANES, LANES), 1) // HEAD_DIM
    return row == col


def fold(state, total):
    state = jnp.where(head_block(), state, 0.0)
    rows = sum(state[i * HEAD_DIM : (i + 1) * HEAD_DIM] for i in range(LANES // HEAD_DIM))
    return jnp.concatenate([rows, total, jnp.zeros((7, LANES), F32)], axis=0)


def unfold(folded):
    state = jnp.concatenate([folded[:HEAD_DIM]] * (LANES // HEAD_DIM), axis=0)
    return jnp.where(head_block(), state, 0.0), folded[HEAD_DIM : HEAD_DIM + 1]


def softplus(values):
    return jnp.maximum(values, 0.0) + jnp.log1p(jnp.exp(-jnp.abs(values)))


def head_sum(values):
    ones = jnp.where(head_block(), 1.0, 0.0).astype(BF16)
    high, low = split(values)
    return dot(high, ones, 1, 0) + dot(low, ones, 1, 0)


def state_kernel(key_ref, value_ref, state_ref):
    key = softplus(key_ref[...]).astype(BF16)
    value = value_ref[...].astype(BF16)
    total = jnp.sum(key.astype(F32), axis=0, keepdims=True)
    state_ref[0, 0] = fold(dot(key, value, 0, 0), total)


def ratio_parts(query_ref, state_ref):
    query = softplus(query_ref[...]).astype(BF16)
    state, total = unfold(state_ref[0, 0])
    high, low = split(state)
    numerator = dot(query, high, 1, 0) + dot(query, low, 1, 0)
    denominator = head_sum(query.astype(F32) * total) + ATTN_EPS
    return query, high, low, total, numerator, denominator


def mix_kernel(query_ref, state_ref, mixed_ref):
    query, high, low, total, numerator, denominator = ratio_parts(query_ref, state_ref)
    mixed_ref[...] = (numerator / denominator).astype(BF16)


def mix_back_kernel(query_ref, state_ref, grad_ref, query_grad_ref, state_grad_ref):
    query, high, low, total, numerator, denominator = ratio_parts(query_ref, state_ref)
    mixed_grad = grad_ref[...]
    numer_grad = mixed_grad / denominator
    denom_grad = -head_sum(mixed_grad * numerator) / (denominator * denominator)
    up, down = split(numer_grad)
    state_grad = dot(query, up, 0, 0) + dot(query, down, 0, 0)
    total_grad = jnp.sum(query.astype(F32) * denom_grad, axis=0, keepdims=True)
    state_grad_ref[0, 0] = fold(state_grad, total_grad)
    side = dot(up, high, 1, 1) + dot(up, low, 1, 1) + dot(down, high, 1, 1) + denom_grad * total
    query_grad_ref[...] = (side * jax.nn.sigmoid(query_ref[...])).astype(BF16)


def state_back_kernel(key_ref, value_ref, state_ref, out_ref):
    state, total = unfold(state_ref[0, 0])
    high, low = split(state)

    @pl.when(pl.program_id(0) == 0)
    def _():
        value = value_ref[...].astype(BF16)
        side = dot(value, high, 1, 1) + dot(value, low, 1, 1) + total
        out_ref[...] = (side * jax.nn.sigmoid(key_ref[...])).astype(BF16)

    @pl.when(pl.program_id(0) == 1)
    def _():
        key = softplus(key_ref[...]).astype(BF16)
        out_ref[...] = (dot(key, high, 1, 0) + dot(key, low, 1, 0)).astype(BF16)


def head_of(values, head):
    lane = lax.broadcasted_iota(jnp.int32, values.shape, 1) // HEAD_DIM
    return jnp.where(lane == head, values, jnp.zeros_like(values))


def weigh(key_head, query, visible):
    scores = dot(key_head, query, 1, 1) * HEAD_DIM ** (-0.5)
    masked = jnp.where(visible, scores, MASKED_FILL)
    top = jnp.max(masked, axis=0, keepdims=True)
    exponent = jnp.exp(masked - top)
    return exponent * (1.0 / jnp.sum(exponent, axis=0, keepdims=True)), top


def cross_kernel(length_ref, query_ref, key_ref, value_ref, out_ref, peak_ref):
    query, key, value = query_ref[...], key_ref[...], value_ref[...]
    tokens, slots = query.shape[0], key.shape[0]
    visible = lax.broadcasted_iota(jnp.int32, (slots, tokens), 0) < length_ref[pl.program_id(0)]
    total = jnp.zeros((LANES, tokens), F32)
    peak_ref[0, 0] = jnp.zeros((8, LANES), F32)
    for head in range(LANES // HEAD_DIM):
        probability, top = weigh(head_of(key, head), query, visible)
        total = total + dot(head_of(value, head), probability.astype(BF16), 0, 0)
        peak_ref[0, 0, head : head + 1] = jnp.broadcast_to(jnp.max(top, axis=1, keepdims=True), (1, LANES))
    out_ref[...] = total.T.astype(BF16)


def cross_back_kernel(length_ref, query_ref, key_ref, value_ref, grad_ref, query_grad_ref, key_grad_ref, value_grad_ref):
    query, key, value, grad = query_ref[...], key_ref[...], value_ref[...], grad_ref[...]
    tokens, slots = query.shape[0], key.shape[0]
    visible = lax.broadcasted_iota(jnp.int32, (slots, tokens), 0) < length_ref[pl.program_id(0)]
    query_grad = jnp.zeros((LANES, tokens), F32)
    key_grad = jnp.zeros((slots, LANES), F32)
    value_grad = jnp.zeros((slots, LANES), F32)
    for head in range(LANES // HEAD_DIM):
        key_head = head_of(key, head)
        probability, top = weigh(key_head, query, visible)
        prob_grad = dot(head_of(value, head), grad, 1, 1)
        value_grad = value_grad + head_of(dot(probability.astype(BF16), grad, 1, 0), head)
        mean = jnp.sum(probability * prob_grad, axis=0, keepdims=True)
        score_grad = (probability * (prob_grad - mean)).astype(BF16)
        key_grad = key_grad + head_of(dot(score_grad, query, 1, 0), head)
        query_grad = query_grad + dot(key_head, score_grad, 0, 0)
    scale = HEAD_DIM ** (-0.5)
    query_grad_ref[...] = (query_grad * scale).T.astype(BF16)
    key_grad_ref[...] = (key_grad * scale).astype(BF16)
    value_grad_ref[...] = value_grad.astype(BF16)


def silu(values):
    return values * jax.nn.sigmoid(values)


def silu_slope(values):
    sigma = jax.nn.sigmoid(values)
    return sigma * (1.0 + values * (1.0 - sigma))


def columns_of(values, cols):
    place = lax.broadcasted_iota(jnp.int32, values.shape, 0) % cols
    count = values.shape[0]
    left = jnp.where(place == 0, 0.0, pltpu.roll(values, 1, 0))
    right = jnp.where(place == cols - 1, 0.0, pltpu.roll(values, count - 1, 0))
    return left, values, right


def strips_of(tokens, cols):
    size = 4 * cols if tokens % (4 * cols) == 0 else cols
    return [(at, size) for at in range(0, tokens, size)]


def stage_columns(scratch, top, middle, bottom, cols):
    tokens = middle.shape[0]
    full = jnp.concatenate([top.astype(F32), middle, bottom.astype(F32)], axis=0)
    for place, part in enumerate(columns_of(full, cols)):
        scratch[place] = part


def taps(scratch, weight, at, size, cols, mirror):
    result = None
    for row_tap in range(3):
        for col_tap in range(3):
            row_at = 2 - row_tap if mirror else row_tap
            col_at = 2 - col_tap if mirror else col_tap
            tap = 3 * row_tap + col_tap
            term = scratch[col_at, at + row_at * cols : at + row_at * cols + size] * weight[tap : tap + 1]
            result = term if result is None else result + term
    return result


def conv_kernel(cols, z0, z1, top0, top1, bottom0, bottom1, w_ref, b_ref, out_ref, s0, s1):
    tokens = z0.shape[0]
    for z, top, bottom, scratch in ((z0, top0, bottom0, s0), (z1, top1, bottom1, s1)):
        stage_columns(scratch, top[0], silu(z[...]).astype(BF16).astype(F32), bottom[0], cols)
    for at, size in strips_of(tokens, cols):
        first = taps(s0, w_ref[0], at, size, cols, False) + b_ref[0, 0:1]
        second = taps(s1, w_ref[1], at, size, cols, False) + b_ref[1, 0:1]
        out_ref[at : at + size] = (first * silu(second)).astype(BF16)


def conv_back_kernel(cols, z0, z1, top0, top1, bottom0, bottom1, grad_ref, w_ref, b_ref, out0, out1, small_ref, s0, s1):
    tokens = z0.shape[0]
    for z, top, bottom, scratch in ((z0, top0, bottom0, s0), (z1, top1, bottom1, s1)):
        stage_columns(scratch, top[0], silu(z[...]).astype(BF16).astype(F32), bottom[0], cols)
    sums = [jnp.zeros((8, LANES), F32) for _ in range(20)]
    for at, size in strips_of(tokens, cols):
        first = taps(s0, w_ref[0], at, size, cols, False) + b_ref[0, 0:1]
        second = taps(s1, w_ref[1], at, size, cols, False) + b_ref[1, 0:1]
        grad = grad_ref[at : at + size]
        sigma = jax.nn.sigmoid(second)
        slope = sigma * (1.0 + second * (1.0 - sigma))
        for j, (part, scratch, out) in enumerate(
            ((grad * second * sigma, s0, out0), (grad * first * slope, s1, out1))
        ):
            out[at : at + size] = part.astype(BF16)
            for row_tap in range(3):
                for col_tap in range(3):
                    start = at + row_tap * cols
                    product = part * scratch[col_tap, start : start + size]
                    place = 9 * j + 3 * row_tap + col_tap
                    sums[place] = sums[place] + jnp.sum(product.reshape(size // 8, 8, LANES), axis=0)
            sums[18 + j] = sums[18 + j] + jnp.sum(part.reshape(size // 8, 8, LANES), axis=0)
    for place in range(20):
        small_ref[0, place : place + 1] = jnp.sum(sums[place], axis=0, keepdims=True)
    small_ref[0, 20:24] = jnp.zeros((4, LANES), F32)


def act_back_kernel(cols, z_ref, grad_ref, top, bottom, w_ref, out_ref, bias_ref, scratch):
    tokens = z_ref.shape[0]
    stage_columns(scratch, top[0], grad_ref[...].astype(F32), bottom[0], cols)
    total = jnp.zeros((8, LANES), F32)
    for at, size in strips_of(tokens, cols):
        part = taps(scratch, w_ref[0], at, size, cols, True) * silu_slope(z_ref[at : at + size])
        out_ref[at : at + size] = part.astype(BF16)
        total = total + jnp.sum(part.reshape(size // 8, 8, LANES), axis=0)
    bias_ref[0] = jnp.broadcast_to(jnp.sum(total, axis=0, keepdims=True), (8, LANES))


def call(kernel, grid, in_specs, out_specs, out_shape, flops, moved, scratch=(), **extra):
    return pl.pallas_call(
        kernel,
        grid=grid,
        in_specs=in_specs,
        out_specs=out_specs,
        out_shape=out_shape,
        scratch_shapes=list(scratch),
        compiler_params=pltpu.CompilerParams(vmem_limit_bytes=VMEM_LIMIT),
        cost_estimate=pl.CostEstimate(flops=int(flops), bytes_accessed=int(moved), transcendentals=0),
        **extra,
    )


def struct(shape, dtype):
    return jax.ShapeDtypeStruct(shape, dtype)


class Kernels:
    def __init__(self, micro, tokens, cols, width, hidden, slots):
        self.micro, self.tokens, self.cols = micro, tokens, cols
        self.width, self.hidden, self.slots = width, hidden, slots
        self.groups, self.units = width // LANES, hidden // LANES

    def tile(self, offset=0):
        return pl.BlockSpec((self.tokens, LANES), lambda m, g: (m, g + offset))

    def folded(self):
        return pl.BlockSpec((1, 1, HEAD_DIM + 8, LANES), lambda m, g: (m, g, 0, 0))

    def folded_shape(self):
        return struct((self.micro, self.groups, HEAD_DIM + 8, LANES), F32)

    def states(self, keys_values):
        size = self.micro * self.tokens * self.width
        return call(
            state_kernel, (self.micro, self.groups), [self.tile(), self.tile(self.groups)],
            self.folded(), self.folded_shape(), size * 600, size * 8,
        )(keys_values, keys_values)

    def mix(self, queries, states):
        size = self.micro * self.tokens * self.width
        return call(
            mix_kernel, (self.micro, self.groups), [self.tile(), self.folded()],
            self.tile(), struct(queries.shape, BF16), size * 1500, size * 6,
        )(queries, states)

    def mix_back(self, queries, states, mixed_grad):
        size = self.micro * self.tokens * self.width
        return call(
            mix_back_kernel, (self.micro, self.groups), [self.tile(), self.folded(), self.tile()],
            [self.tile(), self.folded()], [struct(queries.shape, BF16), self.folded_shape()],
            size * 4000, size * 10,
        )(queries, states, mixed_grad)

    def states_back(self, keys_values, state_grad):
        groups = self.groups
        size = self.micro * self.tokens * self.width
        tile = lambda offset: pl.BlockSpec((self.tokens, LANES), lambda j, m, g: (m, g + offset))
        return call(
            state_back_kernel, (2, self.micro, groups),
            [tile(0), tile(groups), pl.BlockSpec((1, 1, HEAD_DIM + 8, LANES), lambda j, m, g: (m, g, 0, 0))],
            pl.BlockSpec((self.tokens, LANES), lambda j, m, g: (m, g + j * groups)),
            struct(keys_values.shape, BF16), size * 1500, size * 20,
        )(keys_values, keys_values, state_grad)

    def text_tile(self, offset):
        return pl.BlockSpec((self.slots, LANES), lambda m, g: (m, g + offset))

    def cross(self, lengths, queries, text):
        size = self.micro * self.tokens * self.width
        smem = pl.BlockSpec(memory_space=pltpu.SMEM)
        peak = pl.BlockSpec((1, 1, 8, LANES), lambda m, g: (m, g, 0, 0))
        return call(
            cross_kernel, (self.micro, self.groups),
            [smem, self.tile(), self.text_tile(0), self.text_tile(self.groups)],
            [self.tile(), peak],
            [struct(queries.shape, BF16), struct((self.micro, self.groups, 8, LANES), F32)],
            size * 20000, size * 6,
        )(lengths, queries, text, text)

    def cross_back(self, lengths, queries, text, attended_grad):
        size = self.micro * self.tokens * self.width
        smem = pl.BlockSpec(memory_space=pltpu.SMEM)
        return call(
            cross_back_kernel, (self.micro, self.groups),
            [smem, self.tile(), self.text_tile(0), self.text_tile(self.groups), self.tile()],
            [self.tile(), self.text_tile(0), self.text_tile(0)],
            [struct(queries.shape, BF16), struct((text.shape[0], self.width), BF16), struct((text.shape[0], self.width), BF16)],
            size * 50000, size * 6,
        )(lengths, queries, text, text, attended_grad)

    def edge(self, offset=0):
        return pl.BlockSpec((1, self.cols, LANES), lambda m, g: (m, 0, g + offset))

    def scratch(self):
        return pltpu.VMEM((3, self.tokens + 2 * self.cols, LANES), F32)

    def conv_specs(self):
        units = self.units
        return (
            [self.tile(), self.tile(units), self.edge(), self.edge(units), self.edge(), self.edge(units)],
            [
                pl.BlockSpec((2, 9, LANES), lambda m, g: (0, 0, g)),
                pl.BlockSpec((2, 1, LANES), lambda m, g: (0, 0, g)),
            ],
        )

    def conv(self, pre, top, bottom, conv_w, conv_b):
        size = self.micro * self.tokens * self.hidden
        data, weights = self.conv_specs()
        return call(
            functools.partial(conv_kernel, self.cols), (self.micro, self.units), data + weights,
            self.tile(), struct((pre.shape[0], self.hidden), BF16), size * 20000, size * 10,
            [self.scratch(), self.scratch()],
        )(pre, pre, top, top, bottom, bottom, conv_w, conv_b)

    def conv_back(self, pre, top, bottom, grad, conv_w, conv_b):
        size = self.micro * self.tokens * self.hidden
        data, weights = self.conv_specs()
        one = struct((pre.shape[0], self.hidden), BF16)
        return call(
            functools.partial(conv_back_kernel, self.cols), (self.micro, self.units),
            data + [self.tile()] + weights,
            [self.tile(), self.tile(), pl.BlockSpec((1, 24, LANES), lambda m, g: (m, 0, g))],
            [one, one, struct((self.micro, 24, self.hidden), F32)], size * 40000, size * 16,
            [self.scratch(), self.scratch()],
        )(pre, pre, top, top, bottom, bottom, grad, conv_w, conv_b)

    def act_back(self, pre, grad, top, bottom, conv_w):
        size = self.micro * self.tokens * self.hidden
        units = self.units
        return call(
            functools.partial(act_back_kernel, self.cols), (self.micro, 2 * units),
            [
                self.tile(), self.tile(), self.edge(), self.edge(),
                pl.BlockSpec((1, 9, LANES), lambda m, g: (g // units, 0, g % units)),
            ],
            [self.tile(), pl.BlockSpec((1, 8, LANES), lambda m, g: (m, 0, g))],
            [struct(pre.shape, BF16), struct((self.micro, 8, pre.shape[1]), F32)], size * 20000, size * 16,
            [self.scratch()],
        )(pre, grad, top, bottom, conv_w)


def pad_to(values, *sizes):
    return jnp.pad(values, [(0, size - now) for size, now in zip(sizes, values.shape)])


def side_by_side(parts, width):
    return jnp.concatenate([pad_to(part, part.shape[0], width) for part in parts], axis=1)


def halos(rows, cols):
    size = lax.axis_size(SEQ)
    up = [(i, i + 1) for i in range(size - 1)]
    down = [(j, i) for i, j in up]
    return (
        lax.ppermute(rows[:, -cols:], SEQ, up),
        lax.ppermute(rows[:, :cols], SEQ, down),
    )


def shards(latents, text, timesteps, text_lengths, cotangent, table, self_qkv, self_out, cross_q, cross_kv,
           cross_out, up_w, up_b, conv_w, conv_b, down_w):
    micro, _, row_count, cols, features = latents.shape
    tokens = row_count * cols
    own_rows, heads_width = cross_q.shape
    hidden_width = up_b.shape[1]
    text_len = text.shape[2]
    width, hidden, slots = up_to(heads_width, LANES), up_to(hidden_width, 2 * LANES), up_to(text_len, 16)
    rows = up_to(own_rows, 16)
    dp_size, seq_size = lax.axis_size(DP), lax.axis_size(SEQ)
    near = dp_size * rows
    wide = seq_size * near
    core = lax.axis_index(TP)
    kernels = Kernels(micro, tokens, cols, width, hidden // 2, slots)

    half = hidden // 2

    def units(values, at):
        return pad_to(values[:, at * half : (at + 1) * half], values.shape[0], half)

    def heads_rows(*parts):
        return pad_to(side_by_side(parts, width), rows, len(parts) * width)

    def ffn_rows(at):
        up = jnp.concatenate([units(up_w[0], at), units(up_w[1], at)], axis=1)
        return [pad_to(up, rows, 2 * half)], [pad_to(units(down_w.T, at), rows, half)]

    wire = Wire()
    qkv_rows = gather(wire, [heads_rows(self_qkv[1], self_qkv[2])], [heads_rows(self_qkv[0])])
    token_rows = gather(wire, [heads_rows(cross_q)], [heads_rows(self_out.T)])
    text_rows = gather(wire, [heads_rows(cross_kv[0], cross_kv[1])], [heads_rows(cross_out.T)])
    unit_rows = [gather(wire, *ffn_rows(at)) for at in range(2)]

    slot = jnp.arange(wide)
    block, row = slot // rows, slot % rows
    back_seq = block // dp_size
    back_dp = sum(jnp.where(block % dp_size == k, a, 0) for k, a in enumerate(slot_order(dp_size)))
    from_seq = (lax.axis_index(SEQ) - back_seq) % seq_size
    from_dp = ring_member(DP, (ring_place(DP) - back_dp) % dp_size)
    valid = row < own_rows
    channel = jnp.where(valid, (from_dp * seq_size + from_seq) * own_rows + row, -1)
    pick = (jnp.arange(features)[:, None] == channel[None, :]).astype(BF16)

    def relative(values):
        return jnp.where(core == 0, values, jnp.flip(values, axis=0))

    lengths = relative(text_lengths[:, 0])
    caption = jnp.pad(relative(text[:, 0]), ((0, 0), (0, slots - text_len), (0, 0))).reshape(micro * slots, features)
    caption = dot(caption, pick, 1, 0).astype(BF16)
    resid_in = dot(lax.dynamic_index_in_dim(latents, core, 0, False).reshape(tokens, features), pick, 1, 0)
    grad_out = dot(lax.dynamic_index_in_dim(cotangent, core, 0, False).reshape(tokens, features), pick, 1, 0)

    frequency = jnp.exp(-math.log(10000.0) * channel.astype(F32) / features)
    time = lax.dynamic_index_in_dim(timesteps[:, 0], core, 0, False).astype(F32)
    waves = 0.5 * jnp.sin(time * frequency[None, :] + jnp.arange(6, dtype=F32)[:, None])
    mod_table = jnp.dot(table, pick.astype(F32), precision=lax.Precision.HIGHEST)
    modulation = jnp.where(valid[None, :], mod_table + waves, 0.0)
    shift_a, scale_a, gate_a, shift_f, scale_f, gate_f = [modulation[i] for i in range(6)]

    def normalise(values):
        center = jnp.where(valid[None, :], values - jnp.sum(values, axis=1, keepdims=True) / features, 0.0)
        spread = jnp.sum(center * center, axis=1, keepdims=True) / features
        inverse = lax.rsqrt(spread + NORM_EPS)
        return center * inverse, inverse

    def normalise_back(values, grad, stretch):
        unit, inverse = normalise(values)
        shift_grad = jnp.sum(grad, axis=0)
        scale_grad = jnp.sum(grad * unit, axis=0)
        scaled = grad * (1.0 + stretch)
        mean = jnp.sum(scaled, axis=1, keepdims=True) / features
        along = jnp.sum(scaled * unit, axis=1, keepdims=True) / features
        return jnp.where(valid[None, :], inverse * (scaled - mean - unit * along), 0.0), shift_grad, scale_grad

    def both(own):
        return jnp.concatenate([own, other_core(own)], axis=0)

    def core_total(parts):
        def product(at):
            return sum(dot(left[at : at + tokens], right, 1, dim) for left, right, dim in parts)

        return other_core(product(tokens).astype(BF16)).astype(F32) + product(0)

    ffn_out_grad = both((gate_f * grad_out).astype(BF16))

    def weight_grad(activation, grad):
        return [dot(activation[:, b * near : (b + 1) * near], grad, 0, 0).astype(BF16) for b in range(seq_size)]

    unit_a, _ = normalise(resid_in)
    normed = both((unit_a * (1.0 + scale_a) + shift_a).astype(BF16))
    w_kv, w_q = wire.need(qkv_rows)
    keys_values = dot(normed, w_kv, 1, 0)
    states = butterfly(kernels.states(keys_values), (SEQ,), jnp.add)
    queries = dot(wire.step(normed), w_q, 1, 0)
    mixed = kernels.mix(queries, wire.step(states))
    w_cq, w_so = wire.need(token_rows)
    self_term = core_total([(mixed, w_so, 1)])
    resid_a = resid_in + gate_a * self_term
    cross_input = both(resid_a.astype(BF16))
    cross_query = dot(cross_input, w_cq, 1, 0).astype(BF16)
    w_ckv, w_co = wire.need(text_rows)
    text_proj = dot(caption, w_ckv, 1, 0).astype(BF16)
    attended, peaks = kernels.cross(lengths, cross_query, wire.step(text_proj))
    resid_b = resid_a + core_total([(wire.step(attended), w_co, 1)])
    unit_f, _ = normalise(resid_b)
    normed_ffn = both((unit_f * (1.0 + scale_f) + shift_f).astype(BF16))

    ffn_terms, backs, smalls, ffn_grads = [], [], [], []
    for at in range(2):
        w_up, w_down = wire.need(unit_rows[at])
        bias = jnp.concatenate([units(up_b[0:1], at), units(up_b[1:2], at)], axis=1)
        filters = jnp.stack([units(conv_w[:, j], at) for j in range(2)])
        filter_bias = jnp.stack([units(conv_b[j : j + 1], at) for j in range(2)])
        pre = dot(wire.step(normed_ffn), w_up, 1, 0) + bias
        by_micro = pre.reshape(micro, tokens, 2 * half)
        edges = jnp.concatenate([by_micro[:, :cols], by_micro[:, -cols:]], axis=1)
        top, bottom = halos(silu(edges).astype(BF16), cols)
        gated_grad = dot(ffn_out_grad, w_down, 1, 0)
        pre, top, bottom = wire.step((pre, top, bottom))
        gated = kernels.conv(pre, top, bottom, filters, filter_bias)
        gated_grad = wire.step(gated_grad)
        conv_grad0, conv_grad1, small = kernels.conv_back(pre, top, bottom, gated_grad, filters, filter_bias)
        conv_grad = jnp.concatenate([conv_grad0, conv_grad1], axis=1)
        top_grad, bottom_grad = halos(conv_grad.reshape(micro, tokens, 2 * half), cols)
        down_parts = weight_grad(ffn_out_grad, gated)
        top_grad, bottom_grad = wire.step((top_grad, bottom_grad))
        up_low, bias_grad = kernels.act_back(pre, conv_grad, top_grad, bottom_grad, filters)
        smalls.append(
            jnp.concatenate([jnp.sum(small, axis=0)[:20], jnp.sum(bias_grad, axis=0)[:1].reshape(2, half)], axis=0)
        )
        up_low = wire.step(up_low)
        ffn_grads.append(scatter(wire, [weight_grad(normed_ffn, up_low)], [down_parts]))
        ffn_terms.append((gated, w_down, 1))
        backs.append((up_low, w_up, 1))
    small, head_peaks = [], []
    wire.join(butterfly_phases(jnp.concatenate(smalls, axis=1), (SEQ, DP), jnp.add, small))
    head_count = heads_width // HEAD_DIM
    own_peaks = jnp.max(peaks[:, :, : LANES // HEAD_DIM, 0], axis=0).reshape(-1)[:head_count]
    wire.join(butterfly_phases(own_peaks, (SEQ, DP), jnp.maximum, head_peaks))

    normed_ffn_grad = core_total(backs)
    ffn_out = core_total(ffn_terms)
    resid_c = resid_b + gate_f * ffn_out
    gate_f_grad = jnp.sum(grad_out * ffn_out, axis=0)
    resid_b_part, shift_f_grad, scale_f_grad = normalise_back(resid_b, wire.step(normed_ffn_grad), scale_f)
    resid_b_grad = grad_out + resid_b_part
    cross_grad = both(resid_b_grad.astype(BF16))
    attended_grad = dot(wire.step(cross_grad), w_co, 1, 0).astype(BF16)
    cross_out_parts = weight_grad(cross_grad, attended)
    query_grad, key_grad, value_grad = kernels.cross_back(lengths, cross_query, text_proj, wire.step(attended_grad))
    query_grad = wire.step(query_grad)
    cross_kv_parts = weight_grad(caption, jnp.concatenate([key_grad, value_grad], axis=1))
    text_grads = scatter(wire, [cross_kv_parts], [cross_out_parts])
    resid_a_grad = resid_b_grad + core_total([(query_grad, w_cq, 1)])
    cross_q_parts = weight_grad(cross_input, query_grad)
    gate_a_grad = jnp.sum(resid_a_grad * self_term, axis=0)
    self_grad = both((gate_a * wire.step(resid_a_grad)).astype(BF16))
    mixed_grad = dot(self_grad, w_so, 1, 0)
    q_low, state_grad = kernels.mix_back(queries, states, wire.step(mixed_grad))
    state_grad = butterfly(state_grad, (SEQ,), jnp.add)
    token_grads = scatter(wire, [cross_q_parts], [weight_grad(self_grad, mixed)])
    q_parts = weight_grad(normed, q_low)
    kv_low = kernels.states_back(keys_values, wire.step(state_grad))
    kv_low = wire.step(kv_low)
    qkv_grads = scatter(wire, [weight_grad(normed, kv_low)], [q_parts])
    normed_grad = core_total([(q_low, w_q, 1), (kv_low, w_kv, 1)])
    resid_part, shift_a_grad, scale_a_grad = normalise_back(resid_in, normed_grad, scale_a)
    latent_grad = resid_a_grad + resid_part

    def whole(own):
        other = other_core(own)
        pair = jnp.where(core == 0, jnp.stack([own, other]), jnp.stack([other, own]))
        return pair.reshape(micro, 1, row_count, cols, features)

    high, low = split(latent_grad)
    output = whole(dot(resid_c.astype(BF16), pick, 1, 1).astype(BF16))
    latents_grad = whole(dot(high, pick, 1, 1) + dot(low, pick, 1, 1))
    mod_grad = jnp.stack([shift_a_grad, scale_a_grad, gate_a_grad, shift_f_grad, scale_f_grad, gate_f_grad])
    mod_grad = lax.dot_general(
        mod_grad, pick.astype(F32), (((1,), (1,)), ((), ())), precision=lax.Precision.HIGHEST
    )
    table_grads = []
    wire.join(butterfly_phases(butterfly(mod_grad, (TP,), jnp.add), (SEQ, DP), jnp.add, table_grads))
    wire.finish()
    (table_grad,), (head_peaks,), (small,) = table_grads, head_peaks, small
    down_grad = jnp.concatenate([down for _, down in ffn_grads], axis=1)
    up_grad = jnp.concatenate(
        [up[:, j * half : (j + 1) * half] for j in range(2) for up, _ in ffn_grads], axis=1
    )
    (cross_kv_grad, cross_out_grad), (cross_q_grad, self_out_grad) = text_grads, token_grads
    kv_grad, q_grad = qkv_grads

    factor = jnp.repeat(jnp.sqrt(CLIP_TAU / jnp.maximum(head_peaks, CLIP_TAU)), HEAD_DIM)

    def cut(grad, count, each, size):
        grad = grad[:own_rows].reshape(own_rows, count, each)[:, :, :size]
        return grad.transpose(1, 0, 2)

    def heads(grad):
        return grad[:own_rows, :heads_width]

    taps_grad = small[:18].reshape(2, 9, hidden)[:, :, :hidden_width].transpose(1, 0, 2)
    return (
        output,
        latents_grad,
        table_grad,
        jnp.concatenate([heads(q_grad)[None], cut(kv_grad, 2, width, heads_width)], axis=0),
        heads(self_out_grad).T,
        heads(cross_q_grad),
        cut(cross_kv_grad, 2, width, heads_width),
        heads(cross_out_grad).T,
        cut(up_grad, 2, hidden, hidden_width),
        small[20:22, :hidden_width],
        taps_grad,
        small[18:20, :hidden_width],
        down_grad[:own_rows, :hidden_width].T,
        cross_q.astype(F32) * factor[None, :],
        cross_kv[0].astype(F32) * factor[None, :],
    )


def solution(mesh):
    tokens = P(None, DP, SEQ, None, None)
    stacked, by_column, by_row = P(None, (DP, SEQ), TP), P(TP, (DP, SEQ)), P((DP, SEQ), TP)
    return jax.shard_map(
        shards,
        mesh=mesh,
        in_specs=(
            tokens, P(None, DP, None, None), P(None, DP), P(None, DP), tokens, P(), stacked, by_column, by_row,
            stacked, by_column, stacked, P(None, TP), P(None, None, TP), P(None, TP), by_column,
        ),
        out_specs=(
            tokens, tokens, P(), stacked, by_column, by_row, stacked, by_column, stacked, P(None, TP),
            P(None, None, TP), P(None, TP), by_column, by_row, by_row,
        ),
        check_vma=False,
    )
```

```python
import functools
import math

import jax
import jax.numpy as jnp
from jax import lax
from jax.experimental import pallas as pl
from jax.experimental.pallas import tpu as pltpu
from jax.sharding import PartitionSpec as P

DP, SEQ, TP = "dp", "seq", "tensor"
HEAD_DIM = 32
LANES = 128
NORM_EPS = 1e-06
ATTN_EPS = 1e-06
CLIP_TAU = 3.5
MASKED_FILL = -1e30
F32, BF16 = jnp.float32, jnp.bfloat16
VMEM_LIMIT = 48 * 1024 * 1024


def up_to(value, step):
    return -(-value // step) * step


def dot(left, right, left_dim, right_dim):
    return lax.dot_general(
        left, right, (((left_dim,), (right_dim,)), ((), ())), preferred_element_type=F32
    )


def split(values):
    high = values.astype(BF16)
    return high, (values - high.astype(F32)).astype(BF16)


def ring_of(axis):
    size = lax.axis_size(axis)
    if axis == DP and size % 2 == 0:
        return list(range(0, size, 2)) + list(range(size - 1, 0, -2))
    return list(range(size))


def ring_place(axis):
    size, index = lax.axis_size(axis), lax.axis_index(axis)
    if axis == DP and size % 2 == 0:
        return jnp.where(index % 2 == 0, index // 2, size - 1 - index // 2)
    return index


def ring_member(axis, place):
    size = lax.axis_size(axis)
    if axis == DP and size % 2 == 0:
        return jnp.where(place < size // 2, 2 * place, 2 * (size - 1 - place) + 1)
    return place


def shift(values, axis, step):
    if isinstance(step, list):
        return lax.ppermute(values, axis, step)
    cycle = ring_of(axis)
    size = len(cycle)
    return lax.ppermute(values, axis, [(cycle[i], cycle[(i + step) % size]) for i in range(size)])


def slot_order(size):
    ahead = size // 2
    order = []
    for step in range(ahead):
        order.append(ahead - step)
        if ahead + 1 + step < size:
            order.append(ahead + 1 + step)
    return order + [0]


def chip_back(back_dp, back_seq):
    dp_size, seq_size = lax.axis_size(DP), lax.axis_size(SEQ)
    from_dp = ring_member(DP, (ring_place(DP) - back_dp) % dp_size)
    return from_dp * seq_size + (lax.axis_index(SEQ) - back_seq) % seq_size


class Wire:
    def __init__(self):
        self.running, self.queue, self.last, self.before, self.patient = [], [], (), (), False
        self.stride, self.since = lax.axis_size(DP) // 2, lax.axis_size(DP)

    def join(self, phases):
        self.running.append((phases, next(phases)))

    def push(self, phases, patient):
        self.queue.append((phases, patient))

    def round(self, hurry=False):
        if self.queue and self.since >= self.stride:
            phases, self.patient = self.queue.pop(0)
            self.join(phases)
            self.since = 0
        elif self.patient and self.since >= self.stride and not hurry:
            return
        if not self.running:
            return
        self.since += 1
        sends = [send for _, pending in self.running for send in pending]
        values = tuple(value for value, _, _ in sends)
        if self.last:
            values, _ = lax.optimization_barrier((values, self.last))
        arrived = tuple(shift(value, axis, step) for value, (_, axis, step) in zip(values, sends))
        self.before, self.last = self.last, arrived
        running, at = [], 0
        for phases, pending in self.running:
            mine = arrived[at : at + len(pending)]
            at += len(pending)
            try:
                running.append((phases, phases.send(mine)))
            except StopIteration:
                pass
        self.running = running

    def after(self, value):
        return lax.optimization_barrier((value, self.last))[0] if self.last else value

    def step(self, value, slack=False):
        value = lax.optimization_barrier((value, self.before))[0] if slack else self.after(value)
        self.round()
        return value

    def need(self, done):
        while not done:
            self.round(True)
        return done

    def finish(self):
        while self.running or self.queue:
            self.round(True)


def butterfly_phases(values, axes, combine, done):
    for axis in axes:
        size = lax.axis_size(axis)
        bit = 1
        while bit < size:
            (arrived,) = yield [(values, axis, [(i, i ^ bit) for i in range(size)])]
            values = combine(values, arrived)
            bit *= 2
    done.append(values)


def columns(values, widths):
    at, parts = 0, []
    for width in widths:
        parts.append(values[:, at : at + width])
        at += width
    return parts


def gather_phases(first, second, done):
    size = lax.axis_size(DP)
    ahead = size // 2
    widths_a, widths_b = [w.shape[1] for w in first], [w.shape[1] for w in second]
    shard_a, shard_b = jnp.concatenate(first, axis=1), jnp.concatenate(second, axis=1)
    n_a, n_b = shard_a.shape[1], shard_b.shape[1]
    rows = shard_a.shape[0]
    (far_b,) = yield [(shard_b, SEQ, 1)]
    pieces = [jnp.concatenate([shard_a, shard_b, far_b], axis=1)] + [None] * (size - 1)
    far = [None] * size
    fresh = [0]
    for hop in range(1, ahead + 2):
        sends, places = [], []
        if hop <= ahead:
            sends.append((pieces[hop - 1], DP, 1))
            places.append(hop)
        if size - hop > ahead:
            sends.append((pieces[(size - hop + 1) % size], DP, -1))
            places.append(size - hop)
        across = [pieces[a][:, :n_a] for a in fresh]
        sends.append((jnp.concatenate(across, axis=0) if len(across) > 1 else across[0], SEQ, 1))
        arrived = yield sends
        for i, a in enumerate(fresh):
            far[a] = (arrived[-1], i * rows)
        for a, piece in zip(places, arrived):
            pieces[a] = piece
        fresh = places
    arrays, moves = [], []

    def source(array):
        for place, known in enumerate(arrays):
            if known is array:
                return place
        arrays.append(array)
        return len(arrays) - 1

    for a in range(size):
        near, (across, start) = source(pieces[a]), far[a]
        across = source(across)
        at = 0
        for weight, width in enumerate(widths_a):
            moves.append((weight, a, near, 0, at, width))
            moves.append((weight, size + a, across, start, at, width))
            at += width
        for weight, width in enumerate(widths_b):
            moves.append((len(widths_a) + weight, a, near, 0, at, width))
            moves.append((len(widths_a) + weight, size + a, near, 0, at + n_b, width))
            at += width
    place = jnp.stack([chip_back(a, b).astype(jnp.int32) for b in range(2) for a in range(size)])
    done.extend(assemble(place, arrays, moves, rows, widths_a + widths_b))


def assemble_kernel(moves, rows, count, place_ref, *refs):
    sources, outs = refs[:count], refs[count:]
    for slot in range(place_ref.shape[0]):

        @pl.when(pl.program_id(0) == slot)
        def _(slot=slot):
            for weight, to, array, start, at, width in moves:
                if to == slot:
                    outs[weight][...] = sources[array][start : start + rows, at : at + width]


def assemble(place, arrays, moves, rows, widths):
    slots = place.shape[0]
    return pl.pallas_call(
        functools.partial(assemble_kernel, moves, rows, len(arrays)),
        grid_spec=pltpu.PrefetchScalarGridSpec(
            num_scalar_prefetch=1,
            grid=(slots,),
            in_specs=[
                pl.BlockSpec(array.shape, lambda i, place_ref: (0, 0), pipeline_mode=pl.Buffered(1)) for array in arrays
            ],
            out_specs=[pl.BlockSpec((rows, width), lambda i, place_ref: (place_ref[i], 0)) for width in widths],
        ),
        out_shape=[struct((slots * rows, width), BF16) for width in widths],
        compiler_params=pltpu.CompilerParams(vmem_limit_bytes=VMEM_LIMIT),
        cost_estimate=pl.CostEstimate(flops=0, bytes_accessed=slots * rows * sum(widths) * 4, transcendentals=0),
    )(place, *arrays)


def gather(wire, first, second, gate=None):
    done = []
    if wire is not None and lax.axis_size(SEQ) == 2:
        wire.push(gather_phases(first, second, done), False)
    else:
        shard = jnp.concatenate(first + second, axis=1)
        if gate is not None:
            shard, _ = lax.optimization_barrier((shard, gate))
        full = lax.all_gather(shard, (DP, SEQ), axis=0, tiled=False).reshape(-1, shard.shape[1])
        done.extend(columns(full, [w.shape[1] for w in first + second]))
    return done


def combine_kernel(near_count, flat_count, index_ref, *refs):
    near, flat, far = refs[:near_count], refs[near_count : near_count + flat_count], refs[near_count + flat_count]
    running, out = refs[near_count + flat_count + 1 : -1], refs[-1]
    at = 0
    for place, ref in enumerate(near + flat):
        width = ref.shape[1]
        part = ref[...].astype(F32)
        if place < near_count:
            part = part + far[:, at : at + width].astype(F32)
        for other in running:
            part = part + other[:, at : at + width].astype(F32)
        out[:, at : at + width] = part.astype(out.dtype)
        at += width


def combine(blocks, near_count, far, running, rows, dtype):
    steps = 3 if rows % 48 == 0 else 1
    size = rows // steps
    width = sum(array.shape[1] for array, _ in blocks)
    sources = blocks + [far] + [(array, 0) for array in running]
    index = jnp.stack([jnp.asarray(at, jnp.int32) for _, at in sources])

    def spec(place, array):
        return pl.BlockSpec((size, array.shape[1]), lambda i, index_ref: (index_ref[place] * steps + i, 0))

    return pl.pallas_call(
        functools.partial(combine_kernel, near_count, len(blocks) - near_count),
        grid_spec=pltpu.PrefetchScalarGridSpec(
            num_scalar_prefetch=1,
            grid=(steps,),
            in_specs=[spec(place, array) for place, (array, _) in enumerate(sources)],
            out_specs=pl.BlockSpec((size, width), lambda i, index_ref: (i, 0)),
        ),
        out_shape=struct((rows, width), dtype),
        compiler_params=pltpu.CompilerParams(vmem_limit_bytes=VMEM_LIMIT),
        cost_estimate=pl.CostEstimate(flops=rows * width * 4, bytes_accessed=rows * width * 10, transcendentals=0),
    )(index, *[array for array, _ in sources])


def scatter_phases(first, second, done):
    size = lax.axis_size(DP)
    ahead = size // 2
    order = slot_order(size)
    rows = first[0].shape[0] // (2 * size)
    widths = [part.shape[1] for part in first + second]
    n_a = sum(part.shape[1] for part in first)
    n_b = sum(part.shape[1] for part in second)

    def across(start, count):
        blocks = [
            [lax.dynamic_slice_in_dim(part, chip_back(order[start + i], 1) * rows, rows, 0) for part in first]
            for i in range(count)
        ]
        blocks = [jnp.concatenate(each, axis=1) if len(each) > 1 else each[0] for each in blocks]
        return (jnp.concatenate(blocks, axis=0) if count > 1 else blocks[0], SEQ, 1)

    def value(a, far, running, dtype):
        blocks = [(part, chip_back(a, 0)) for part in first]
        blocks += [(part, chip_back(a, b)) for b in range(2) for part in second]
        return combine(blocks, len(first), far[a], running, rows, dtype)

    def take(far, arrived, start):
        for i in range(arrived.shape[0] // rows):
            far[order[start + i]] = (arrived, i)

    far = {}
    (arrived,) = yield [across(0, 2)]
    take(far, arrived, 0)
    back = forth = None
    for step in range(ahead):
        sends = []
        back = value(ahead - step, far, [] if back is None else [back], BF16)
        sends.append((back, DP, -1))
        place = ahead + 1 + step
        if place < size:
            forth = value(place, far, [] if forth is None else [forth], BF16)
            sends.append((forth, DP, 1))
        start = 2 * step + 2
        if start < size:
            sends.append(across(start, min(2, size - start)))
        arrived = yield sends
        back = arrived[0]
        if place < size:
            forth = arrived[1]
        if start < size:
            take(far, arrived[-1], start)
    total = value(0, far, [back, forth], F32)
    (other,) = yield [(total[:, n_a + n_b :].astype(BF16), SEQ, 1)]
    mine = total[:, n_a : n_a + n_b] + other.astype(F32)
    done.extend(columns(total[:, :n_a], widths[: len(first)]) + columns(mine, widths[len(first) :]))


def scatter(wire, first, second):
    done = []
    if wire is not None and lax.axis_size(SEQ) == 2:
        wire.push(scatter_phases(first, second, done), True)
    else:
        parts = jnp.concatenate(first + second, axis=1)
        devices = lax.axis_size(DP) * lax.axis_size(SEQ)
        parts = parts.reshape(devices, parts.shape[0] // devices, parts.shape[1])
        total = lax.psum_scatter(parts, (DP, SEQ), scatter_dimension=0, tiled=False)
        done.extend(columns(total.astype(F32), [w.shape[1] for w in first + second]))
    return done


def butterfly(values, axes, combine):
    for axis in axes:
        size = lax.axis_size(axis)
        bit = 1
        while bit < size:
            values = combine(values, lax.ppermute(values, axis, [(i, i ^ bit) for i in range(size)]))
            bit *= 2
    return values


def other_core(values):
    return lax.ppermute(values, TP, [(0, 1), (1, 0)])


def head_block():
    row = lax.broadcasted_iota(jnp.int32, (LANES, LANES), 0) // HEAD_DIM
    col = lax.broadcasted_iota(jnp.int32, (LANES, LANES), 1) // HEAD_DIM
    return row == col


def fold(state, total):
    state = jnp.where(head_block(), state, 0.0)
    rows = sum(state[i * HEAD_DIM : (i + 1) * HEAD_DIM] for i in range(LANES // HEAD_DIM))
    return jnp.concatenate([rows, total, jnp.zeros((7, LANES), F32)], axis=0)


def unfold(folded):
    state = jnp.concatenate([folded[:HEAD_DIM]] * (LANES // HEAD_DIM), axis=0)
    return jnp.where(head_block(), state, 0.0), folded[HEAD_DIM : HEAD_DIM + 1]


def softplus(values):
    return jnp.maximum(values, 0.0) + jnp.log1p(jnp.exp(-jnp.abs(values)))


def head_sum(values):
    ones = jnp.where(head_block(), 1.0, 0.0).astype(BF16)
    high, low = split(values)
    return dot(high, ones, 1, 0) + dot(low, ones, 1, 0)


def state_kernel(key_ref, value_ref, state_ref):
    key = softplus(key_ref[...]).astype(BF16)
    value = value_ref[...].astype(BF16)
    total = jnp.sum(key.astype(F32), axis=0, keepdims=True)
    state_ref[0, 0] = fold(dot(key, value, 0, 0), total)


def ratio_parts(query_ref, state_ref):
    query = softplus(query_ref[...]).astype(BF16)
    state, total = unfold(state_ref[0, 0])
    high, low = split(state)
    numerator = dot(query, high, 1, 0) + dot(query, low, 1, 0)
    denominator = head_sum(query.astype(F32) * total) + ATTN_EPS
    return query, high, low, total, numerator, denominator


def mix_kernel(query_ref, state_ref, mixed_ref):
    query, high, low, total, numerator, denominator = ratio_parts(query_ref, state_ref)
    mixed_ref[...] = (numerator / denominator).astype(BF16)


def mix_back_kernel(query_ref, state_ref, grad_ref, query_grad_ref, state_grad_ref):
    query, high, low, total, numerator, denominator = ratio_parts(query_ref, state_ref)
    mixed_grad = grad_ref[...]
    numer_grad = mixed_grad / denominator
    denom_grad = -head_sum(mixed_grad * numerator) / (denominator * denominator)
    up, down = split(numer_grad)
    state_grad = dot(query, up, 0, 0) + dot(query, down, 0, 0)
    total_grad = jnp.sum(query.astype(F32) * denom_grad, axis=0, keepdims=True)
    state_grad_ref[0, 0] = fold(state_grad, total_grad)
    side = dot(up, high, 1, 1) + dot(up, low, 1, 1) + dot(down, high, 1, 1) + denom_grad * total
    query_grad_ref[...] = (side * jax.nn.sigmoid(query_ref[...])).astype(BF16)


def state_back_kernel(key_ref, value_ref, state_ref, out_ref):
    state, total = unfold(state_ref[0, 0])
    high, low = split(state)

    @pl.when(pl.program_id(0) == 0)
    def _():
        value = value_ref[...].astype(BF16)
        side = dot(value, high, 1, 1) + dot(value, low, 1, 1) + total
        out_ref[...] = (side * jax.nn.sigmoid(key_ref[...])).astype(BF16)

    @pl.when(pl.program_id(0) == 1)
    def _():
        key = softplus(key_ref[...]).astype(BF16)
        out_ref[...] = (dot(key, high, 1, 0) + dot(key, low, 1, 0)).astype(BF16)


def head_of(values, head):
    lane = lax.broadcasted_iota(jnp.int32, values.shape, 1) // HEAD_DIM
    return jnp.where(lane == head, values, jnp.zeros_like(values))


def weigh(key_head, query, visible):
    scores = dot(key_head, query, 1, 1) * HEAD_DIM ** (-0.5)
    masked = jnp.where(visible, scores, MASKED_FILL)
    top = jnp.max(masked, axis=0, keepdims=True)
    exponent = jnp.exp(masked - top)
    return exponent * (1.0 / jnp.sum(exponent, axis=0, keepdims=True)), top


def cross_kernel(length_ref, query_ref, key_ref, value_ref, out_ref, peak_ref):
    query, key, value = query_ref[...], key_ref[...], value_ref[...]
    tokens, slots = query.shape[0], key.shape[0]
    visible = lax.broadcasted_iota(jnp.int32, (slots, tokens), 0) < length_ref[pl.program_id(0)]
    total = jnp.zeros((LANES, tokens), F32)
    peak_ref[0, 0] = jnp.zeros((8, LANES), F32)
    for head in range(LANES // HEAD_DIM):
        probability, top = weigh(head_of(key, head), query, visible)
        total = total + dot(head_of(value, head), probability.astype(BF16), 0, 0)
        peak_ref[0, 0, head : head + 1] = jnp.broadcast_to(jnp.max(top, axis=1, keepdims=True), (1, LANES))
    out_ref[...] = total.T.astype(BF16)


def cross_back_kernel(length_ref, query_ref, key_ref, value_ref, grad_ref, query_grad_ref, key_grad_ref, value_grad_ref):
    query, key, value, grad = query_ref[...], key_ref[...], value_ref[...], grad_ref[...]
    tokens, slots = query.shape[0], key.shape[0]
    visible = lax.broadcasted_iota(jnp.int32, (slots, tokens), 0) < length_ref[pl.program_id(0)]
    query_grad = jnp.zeros((LANES, tokens), F32)
    key_grad = jnp.zeros((slots, LANES), F32)
    value_grad = jnp.zeros((slots, LANES), F32)
    for head in range(LANES // HEAD_DIM):
        key_head = head_of(key, head)
        probability, top = weigh(key_head, query, visible)
        prob_grad = dot(head_of(value, head), grad, 1, 1)
        value_grad = value_grad + head_of(dot(probability.astype(BF16), grad, 1, 0), head)
        mean = jnp.sum(probability * prob_grad, axis=0, keepdims=True)
        score_grad = (probability * (prob_grad - mean)).astype(BF16)
        key_grad = key_grad + head_of(dot(score_grad, query, 1, 0), head)
        query_grad = query_grad + dot(key_head, score_grad, 0, 0)
    scale = HEAD_DIM ** (-0.5)
    query_grad_ref[...] = (query_grad * scale).T.astype(BF16)
    key_grad_ref[...] = (key_grad * scale).astype(BF16)
    value_grad_ref[...] = value_grad.astype(BF16)


def silu(values):
    return values * jax.nn.sigmoid(values)


def silu_slope(values):
    sigma = jax.nn.sigmoid(values)
    return sigma * (1.0 + values * (1.0 - sigma))


def columns_of(values, cols):
    place = lax.broadcasted_iota(jnp.int32, values.shape, 0) % cols
    count = values.shape[0]
    left = jnp.where(place == 0, 0.0, pltpu.roll(values, 1, 0))
    right = jnp.where(place == cols - 1, 0.0, pltpu.roll(values, count - 1, 0))
    return left, values, right


def strips_of(tokens, cols):
    size = 4 * cols if tokens % (4 * cols) == 0 else cols
    return [(at, size) for at in range(0, tokens, size)]


def stage_columns(scratch, top, middle, bottom, cols):
    tokens = middle.shape[0]
    full = jnp.concatenate([top.astype(F32), middle, bottom.astype(F32)], axis=0)
    for place, part in enumerate(columns_of(full, cols)):
        scratch[place] = part


def taps(scratch, weight, at, size, cols, mirror):
    result = None
    for row_tap in range(3):
        for col_tap in range(3):
            row_at = 2 - row_tap if mirror else row_tap
            col_at = 2 - col_tap if mirror else col_tap
            tap = 3 * row_tap + col_tap
            term = scratch[col_at, at + row_at * cols : at + row_at * cols + size] * weight[tap : tap + 1]
            result = term if result is None else result + term
    return result


def conv_kernel(cols, z0, z1, top0, top1, bottom0, bottom1, w_ref, b_ref, out_ref, s0, s1):
    tokens = z0.shape[0]
    for z, top, bottom, scratch in ((z0, top0, bottom0, s0), (z1, top1, bottom1, s1)):
        stage_columns(scratch, top[0], silu(z[...]).astype(BF16).astype(F32), bottom[0], cols)
    for at, size in strips_of(tokens, cols):
        first = taps(s0, w_ref[0], at, size, cols, False) + b_ref[0, 0:1]
        second = taps(s1, w_ref[1], at, size, cols, False) + b_ref[1, 0:1]
        out_ref[at : at + size] = (first * silu(second)).astype(BF16)


def conv_back_kernel(cols, z0, z1, top0, top1, bottom0, bottom1, grad_ref, w_ref, b_ref, out0, out1, small_ref, s0, s1):
    tokens = z0.shape[0]
    for z, top, bottom, scratch in ((z0, top0, bottom0, s0), (z1, top1, bottom1, s1)):
        stage_columns(scratch, top[0], silu(z[...]).astype(BF16).astype(F32), bottom[0], cols)
    sums = [jnp.zeros((8, LANES), F32) for _ in range(20)]
    for at, size in strips_of(tokens, cols):
        first = taps(s0, w_ref[0], at, size, cols, False) + b_ref[0, 0:1]
        second = taps(s1, w_ref[1], at, size, cols, False) + b_ref[1, 0:1]
        grad = grad_ref[at : at + size]
        sigma = jax.nn.sigmoid(second)
        slope = sigma * (1.0 + second * (1.0 - sigma))
        for j, (part, scratch, out) in enumerate(
            ((grad * second * sigma, s0, out0), (grad * first * slope, s1, out1))
        ):
            out[at : at + size] = part.astype(BF16)
            for row_tap in range(3):
                for col_tap in range(3):
                    start = at + row_tap * cols
                    product = part * scratch[col_tap, start : start + size]
                    place = 9 * j + 3 * row_tap + col_tap
                    sums[place] = sums[place] + jnp.sum(product.reshape(size // 8, 8, LANES), axis=0)
            sums[18 + j] = sums[18 + j] + jnp.sum(part.reshape(size // 8, 8, LANES), axis=0)
    for place in range(20):
        small_ref[0, place : place + 1] = jnp.sum(sums[place], axis=0, keepdims=True)
    small_ref[0, 20:24] = jnp.zeros((4, LANES), F32)


def act_back_kernel(cols, z0, z1, grad0, grad1, top0, top1, bottom0, bottom1, w_ref, out0, out1, bias_ref, s0, s1):
    tokens = z0.shape[0]
    for grad, top, bottom, scratch in ((grad0, top0, bottom0, s0), (grad1, top1, bottom1, s1)):
        stage_columns(scratch, top[0], grad[...].astype(F32), bottom[0], cols)
    for j, (z, scratch, out) in enumerate(((z0, s0, out0), (z1, s1, out1))):
        total = jnp.zeros((8, LANES), F32)
        for at, size in strips_of(tokens, cols):
            part = taps(scratch, w_ref[j], at, size, cols, True) * silu_slope(z[at : at + size])
            out[at : at + size] = part.astype(BF16)
            total = total + jnp.sum(part.reshape(size // 8, 8, LANES), axis=0)
        bias_ref[0, j : j + 1] = jnp.sum(total, axis=0, keepdims=True)
    bias_ref[0, 2:8] = jnp.zeros((6, LANES), F32)


def call(kernel, grid, in_specs, out_specs, out_shape, flops, moved, scratch=(), **extra):
    return pl.pallas_call(
        kernel,
        grid=grid,
        in_specs=in_specs,
        out_specs=out_specs,
        out_shape=out_shape,
        scratch_shapes=list(scratch),
        compiler_params=pltpu.CompilerParams(vmem_limit_bytes=VMEM_LIMIT),
        cost_estimate=pl.CostEstimate(flops=int(flops), bytes_accessed=int(moved), transcendentals=0),
        **extra,
    )


def struct(shape, dtype):
    return jax.ShapeDtypeStruct(shape, dtype)


class Kernels:
    def __init__(self, micro, tokens, cols, width, hidden, slots):
        self.micro, self.tokens, self.cols = micro, tokens, cols
        self.width, self.hidden, self.slots = width, hidden, slots
        self.groups, self.units = width // LANES, hidden // LANES

    def tile(self, offset=0):
        return pl.BlockSpec((self.tokens, LANES), lambda m, g: (m, g + offset))

    def folded(self):
        return pl.BlockSpec((1, 1, HEAD_DIM + 8, LANES), lambda m, g: (m, g, 0, 0))

    def folded_shape(self):
        return struct((self.micro, self.groups, HEAD_DIM + 8, LANES), F32)

    def states(self, keys_values):
        size = self.micro * self.tokens * self.width
        return call(
            state_kernel, (self.micro, self.groups), [self.tile(), self.tile(self.groups)],
            self.folded(), self.folded_shape(), size * 600, size * 8,
        )(keys_values, keys_values)

    def mix(self, queries, states):
        size = self.micro * self.tokens * self.width
        return call(
            mix_kernel, (self.micro, self.groups), [self.tile(), self.folded()],
            self.tile(), struct(queries.shape, BF16), size * 1500, size * 6,
        )(queries, states)

    def mix_back(self, queries, states, mixed_grad):
        size = self.micro * self.tokens * self.width
        return call(
            mix_back_kernel, (self.micro, self.groups), [self.tile(), self.folded(), self.tile()],
            [self.tile(), self.folded()], [struct(queries.shape, BF16), self.folded_shape()],
            size * 4000, size * 10,
        )(queries, states, mixed_grad)

    def states_back(self, keys_values, state_grad):
        groups = self.groups
        size = self.micro * self.tokens * self.width
        tile = lambda offset: pl.BlockSpec((self.tokens, LANES), lambda j, m, g: (m, g + offset))
        return call(
            state_back_kernel, (2, self.micro, groups),
            [tile(0), tile(groups), pl.BlockSpec((1, 1, HEAD_DIM + 8, LANES), lambda j, m, g: (m, g, 0, 0))],
            pl.BlockSpec((self.tokens, LANES), lambda j, m, g: (m, g + j * groups)),
            struct(keys_values.shape, BF16), size * 1500, size * 20,
        )(keys_values, keys_values, state_grad)

    def text_tile(self, offset):
        return pl.BlockSpec((self.slots, LANES), lambda m, g: (m, g + offset))

    def cross(self, lengths, queries, text):
        size = self.micro * self.tokens * self.width
        smem = pl.BlockSpec(memory_space=pltpu.SMEM)
        peak = pl.BlockSpec((1, 1, 8, LANES), lambda m, g: (m, g, 0, 0))
        return call(
            cross_kernel, (self.micro, self.groups),
            [smem, self.tile(), self.text_tile(0), self.text_tile(self.groups)],
            [self.tile(), peak],
            [struct(queries.shape, BF16), struct((self.micro, self.groups, 8, LANES), F32)],
            size * 20000, size * 6,
        )(lengths, queries, text, text)

    def cross_back(self, lengths, queries, text, attended_grad):
        size = self.micro * self.tokens * self.width
        smem = pl.BlockSpec(memory_space=pltpu.SMEM)
        return call(
            cross_back_kernel, (self.micro, self.groups),
            [smem, self.tile(), self.text_tile(0), self.text_tile(self.groups), self.tile()],
            [self.tile(), self.text_tile(0), self.text_tile(0)],
            [struct(queries.shape, BF16), struct((text.shape[0], self.width), BF16), struct((text.shape[0], self.width), BF16)],
            size * 50000, size * 6,
        )(lengths, queries, text, text, attended_grad)

    def edge(self, offset=0):
        return pl.BlockSpec((1, self.cols, LANES), lambda m, g: (m, 0, g + offset))

    def scratch(self):
        return pltpu.VMEM((3, self.tokens + 2 * self.cols, LANES), F32)

    def conv_specs(self):
        units = self.units
        return (
            [self.tile(), self.tile(units), self.edge(), self.edge(units), self.edge(), self.edge(units)],
            [
                pl.BlockSpec((2, 9, LANES), lambda m, g: (0, 0, g)),
                pl.BlockSpec((2, 1, LANES), lambda m, g: (0, 0, g)),
            ],
        )

    def conv(self, pre, top, bottom, conv_w, conv_b):
        size = self.micro * self.tokens * self.hidden
        data, weights = self.conv_specs()
        return call(
            functools.partial(conv_kernel, self.cols), (self.micro, self.units), data + weights,
            self.tile(), struct((pre.shape[0], self.hidden), BF16), size * 20000, size * 10,
            [self.scratch(), self.scratch()],
        )(pre, pre, top, top, bottom, bottom, conv_w, conv_b)

    def conv_back(self, pre, top, bottom, grad, conv_w, conv_b):
        size = self.micro * self.tokens * self.hidden
        data, weights = self.conv_specs()
        one = struct((pre.shape[0], self.hidden), BF16)
        return call(
            functools.partial(conv_back_kernel, self.cols), (self.micro, self.units),
            data + [self.tile()] + weights,
            [self.tile(), self.tile(), pl.BlockSpec((1, 24, LANES), lambda m, g: (m, 0, g))],
            [one, one, struct((self.micro, 24, self.hidden), F32)], size * 40000, size * 16,
            [self.scratch(), self.scratch()],
        )(pre, pre, top, top, bottom, bottom, grad, conv_w, conv_b)

    def act_back(self, pre, grads, tops, bottoms, conv_w):
        size = self.micro * self.tokens * self.hidden
        data, weights = self.conv_specs()
        one = struct((pre.shape[0], self.hidden), BF16)
        return call(
            functools.partial(act_back_kernel, self.cols), (self.micro, self.units),
            data[:2] + [self.tile(), self.tile()] + [self.edge()] * 4 + weights[:1],
            [self.tile(), self.tile(), pl.BlockSpec((1, 8, LANES), lambda m, g: (m, 0, g))],
            [one, one, struct((self.micro, 8, self.hidden), F32)], size * 40000, size * 20,
            [self.scratch(), self.scratch()],
        )(pre, pre, *grads, *tops, *bottoms, conv_w)


def pad_to(values, *sizes):
    return jnp.pad(values, [(0, size - now) for size, now in zip(sizes, values.shape)])


def side_by_side(parts, width):
    return jnp.concatenate([pad_to(part, part.shape[0], width) for part in parts], axis=1)


def halos(rows, cols):
    size = lax.axis_size(SEQ)
    up = [(i, i + 1) for i in range(size - 1)]
    down = [(j, i) for i, j in up]
    return (
        lax.ppermute(rows[:, -cols:], SEQ, up),
        lax.ppermute(rows[:, :cols], SEQ, down),
    )


def shards(latents, text, timesteps, text_lengths, cotangent, table, self_qkv, self_out, cross_q, cross_kv,
           cross_out, up_w, up_b, conv_w, conv_b, down_w):
    micro, _, row_count, cols, features = latents.shape
    tokens = row_count * cols
    own_rows, heads_width = cross_q.shape
    hidden_width = up_b.shape[1]
    text_len = text.shape[2]
    width, hidden, slots = up_to(heads_width, LANES), up_to(hidden_width, 2 * LANES), up_to(text_len, 16)
    rows = up_to(own_rows, 16)
    dp_size, seq_size = lax.axis_size(DP), lax.axis_size(SEQ)
    wide = dp_size * seq_size * rows
    core = lax.axis_index(TP)
    kernels = Kernels(micro, tokens, cols, width, hidden // 2, slots)

    half = hidden // 2

    def units(values, at):
        return pad_to(values[:, at * half : (at + 1) * half], values.shape[0], half)

    def heads_rows(*parts):
        return pad_to(side_by_side(parts, width), rows, len(parts) * width)

    def ffn_rows(at):
        up = jnp.concatenate([units(up_w[0], at), units(up_w[1], at)], axis=1)
        return [pad_to(up, rows, 2 * half)], [pad_to(units(down_w.T, at), rows, half)]

    wire = Wire()
    qkv_rows = gather(wire, [heads_rows(self_qkv[1], self_qkv[2])], [heads_rows(self_qkv[0])])
    token_rows = gather(wire, [heads_rows(cross_q)], [heads_rows(self_out.T)])
    text_rows = gather(wire, [heads_rows(cross_kv[0], cross_kv[1])], [heads_rows(cross_out.T)])

    unit_rows = [gather(wire, *ffn_rows(at)) for at in range(2)]

    slot = jnp.arange(wide)
    valid = slot % rows < own_rows
    channel = jnp.where(valid, slot // rows * own_rows + slot % rows, -1)
    pick = (jnp.arange(features)[:, None] == channel[None, :]).astype(BF16)

    def relative(values):
        return jnp.where(core == 0, values, jnp.flip(values, axis=0))

    lengths = relative(text_lengths[:, 0])
    caption = jnp.pad(relative(text[:, 0]), ((0, 0), (0, slots - text_len), (0, 0))).reshape(micro * slots, features)
    caption = dot(caption, pick, 1, 0).astype(BF16)
    resid_in = dot(lax.dynamic_index_in_dim(latents, core, 0, False).reshape(tokens, features), pick, 1, 0)
    grad_out = dot(lax.dynamic_index_in_dim(cotangent, core, 0, False).reshape(tokens, features), pick, 1, 0)

    frequency = jnp.exp(-math.log(10000.0) * channel.astype(F32) / features)
    time = lax.dynamic_index_in_dim(timesteps[:, 0], core, 0, False).astype(F32)
    waves = 0.5 * jnp.sin(time * frequency[None, :] + jnp.arange(6, dtype=F32)[:, None])
    mod_table = jnp.dot(table, pick.astype(F32), precision=lax.Precision.HIGHEST)
    modulation = jnp.where(valid[None, :], mod_table + waves, 0.0)
    shift_a, scale_a, gate_a, shift_f, scale_f, gate_f = [modulation[i] for i in range(6)]

    def normalise(values):
        center = jnp.where(valid[None, :], values - jnp.sum(values, axis=1, keepdims=True) / features, 0.0)
        spread = jnp.sum(center * center, axis=1, keepdims=True) / features
        inverse = lax.rsqrt(spread + NORM_EPS)
        return center * inverse, inverse

    def normalise_back(values, grad, stretch):
        unit, inverse = normalise(values)
        shift_grad = jnp.sum(grad, axis=0)
        scale_grad = jnp.sum(grad * unit, axis=0)
        scaled = grad * (1.0 + stretch)
        mean = jnp.sum(scaled, axis=1, keepdims=True) / features
        along = jnp.sum(scaled * unit, axis=1, keepdims=True) / features
        return jnp.where(valid[None, :], inverse * (scaled - mean - unit * along), 0.0), shift_grad, scale_grad

    def both(own):
        return jnp.concatenate([own, other_core(own)], axis=0)

    def core_total(parts):
        def product(at):
            return sum(dot(left[at : at + tokens], right, 1, dim) for left, right, dim in parts)

        return other_core(product(tokens).astype(BF16)).astype(F32) + product(0)

    ffn_out_grad = both((gate_f * grad_out).astype(BF16))

    def weight_grad(activation, grad):
        return dot(activation, grad, 0, 0).astype(BF16)

    unit_a, _ = normalise(resid_in)
    normed = both((unit_a * (1.0 + scale_a) + shift_a).astype(BF16))
    w_kv, w_q = wire.need(qkv_rows)
    keys_values = dot(normed, w_kv, 1, 0)
    states = butterfly(kernels.states(keys_values), (SEQ,), jnp.add)
    queries = dot(wire.step(normed), w_q, 1, 0)
    mixed = kernels.mix(queries, wire.step(states))
    w_cq, w_so = wire.need(token_rows)
    self_term = core_total([(mixed, w_so, 1)])
    resid_a = resid_in + gate_a * self_term
    cross_input = both(resid_a.astype(BF16))
    cross_query = dot(cross_input, w_cq, 1, 0).astype(BF16)
    w_ckv, w_co = wire.need(text_rows)
    text_proj = dot(caption, w_ckv, 1, 0).astype(BF16)
    attended, peaks = kernels.cross(lengths, cross_query, wire.step(text_proj))
    head_count = heads_width // HEAD_DIM
    head_peaks = []
    own_peaks = jnp.max(peaks[:, :, : LANES // HEAD_DIM, 0], axis=0).reshape(-1)[:head_count]
    wire.join(butterfly_phases(own_peaks, (SEQ, DP), jnp.maximum, head_peaks))
    resid_b = resid_a + core_total([(wire.step(attended), w_co, 1)])
    unit_f, _ = normalise(resid_b)
    normed_ffn = both((unit_f * (1.0 + scale_f) + shift_f).astype(BF16))

    ffn_terms, backs, smalls, ffn_grads = [], [], [], []
    for at in range(2):
        w_up, w_down = wire.need(unit_rows[at])
        bias = jnp.concatenate([units(up_b[0:1], at), units(up_b[1:2], at)], axis=1)
        filters = jnp.stack([units(conv_w[:, j], at) for j in range(2)])
        filter_bias = jnp.stack([units(conv_b[j : j + 1], at) for j in range(2)])
        pre = dot(wire.step(normed_ffn) if at == 0 else normed_ffn, w_up, 1, 0) + bias
        by_micro = pre.reshape(micro, tokens, 2 * half)
        edges = jnp.concatenate([by_micro[:, :cols], by_micro[:, -cols:]], axis=1)
        top, bottom = halos(silu(edges).astype(BF16), cols)
        gated_grad = dot(ffn_out_grad, w_down, 1, 0)
        if at == 0:
            pre, top, bottom = wire.step((pre, top, bottom))
        gated = kernels.conv(pre, top, bottom, filters, filter_bias)
        if at == 0:
            gated_grad = wire.step(gated_grad)
        conv_grad0, conv_grad1, small = kernels.conv_back(pre, top, bottom, gated_grad, filters, filter_bias)
        edges = [grad.reshape(micro, tokens, half) for grad in (conv_grad0, conv_grad1)]
        edges = jnp.concatenate(
            [jnp.concatenate([grad[:, :cols], grad[:, -cols:]], axis=1) for grad in edges], axis=2
        )
        top_grad, bottom_grad = halos(edges, cols)
        down_parts = weight_grad(ffn_out_grad, gated)
        down_sum = scatter(None, [down_parts], []) if at == 0 else []
        if at == 0:
            top_grad, bottom_grad = wire.step((top_grad, bottom_grad))
        up_low0, up_low1, bias_grad = kernels.act_back(
            pre, (conv_grad0, conv_grad1), [top_grad[:, :, :half], top_grad[:, :, half:]],
            [bottom_grad[:, :, :half], bottom_grad[:, :, half:]], filters,
        )
        smalls.append(jnp.concatenate([jnp.sum(small, axis=0)[:20], jnp.sum(bias_grad, axis=0)[:2]], axis=0))
        if at == 0:
            up_low0, up_low1 = wire.step((up_low0, up_low1))
        up_low = jnp.concatenate([up_low0, up_low1], axis=1)
        up_parts = weight_grad(normed_ffn, up_low)
        if at == 0:
            ffn_grads.append(scatter(None, [up_parts], []) + down_sum)
        else:
            ffn_grads.append(scatter(wire, [up_parts], [down_parts]))
        ffn_terms.append((gated, w_down, 1))
        backs.append((up_low, w_up, 1))
    small = []
    wire.join(butterfly_phases(jnp.concatenate(smalls, axis=1), (SEQ, DP), jnp.add, small))

    backs[1] = (wire.step(up_low, True), *backs[1][1:])
    normed_ffn_grad = core_total(backs)
    resid_b_part, shift_f_grad, scale_f_grad = normalise_back(resid_b, normed_ffn_grad, scale_f)
    resid_b_grad = grad_out + resid_b_part
    cross_grad = both(wire.step(resid_b_grad, True).astype(BF16))
    attended_grad = dot(cross_grad, w_co, 1, 0).astype(BF16)
    query_grad, key_grad, value_grad = kernels.cross_back(lengths, cross_query, text_proj, wire.step(attended_grad, True))
    (query_grad, key_grad, value_grad), _ = lax.optimization_barrier(((query_grad, key_grad, value_grad), ffn_grads[0]))
    query_grad, key_grad, value_grad = wire.step((query_grad, key_grad, value_grad), True)
    cross_out_parts = weight_grad(cross_grad, attended)
    cross_kv_parts = weight_grad(caption, jnp.concatenate([key_grad, value_grad], axis=1))
    text_grads = scatter(None, [cross_kv_parts], [])
    text_grads += scatter(None, [cross_out_parts], [])
    resid_a_grad = resid_b_grad + core_total([(wire.step(query_grad, True), w_cq, 1)])
    cross_q_parts = weight_grad(cross_input, query_grad)
    gate_a_grad = jnp.sum(resid_a_grad * self_term, axis=0)
    self_grad = both((gate_a * resid_a_grad).astype(BF16))
    mixed_grad = dot(wire.step(self_grad, True), w_so, 1, 0)
    q_low, state_grad = kernels.mix_back(queries, states, wire.step(mixed_grad, True))
    self_out_parts = weight_grad(self_grad, mixed)
    state_grad = butterfly(state_grad, (SEQ,), jnp.add)
    token_grads = scatter(wire, [cross_q_parts, weight_grad(normed, q_low)], [self_out_parts])
    kv_low = kernels.states_back(keys_values, wire.step(state_grad, True))
    key_parts, value_parts = [weight_grad(normed, kv_low[:, j * width : (j + 1) * width]) for j in range(2)]
    kv_grads = scatter(wire, [key_parts], [value_parts])
    kv_low, _ = lax.optimization_barrier((wire.step(kv_low, True), text_grads))
    normed_grad = core_total([(q_low, w_q, 1), (kv_low, w_kv, 1)])
    resid_part, shift_a_grad, scale_a_grad = normalise_back(resid_in, wire.step(normed_grad, True), scale_a)
    latent_grad = resid_a_grad + resid_part
    ffn_terms = wire.after([left for left, _, _ in ffn_terms])
    ffn_out = core_total([(left, rows_of[1], 1) for left, rows_of in zip(ffn_terms, unit_rows)])
    resid_c = resid_b + gate_f * ffn_out
    gate_f_grad = jnp.sum(grad_out * ffn_out, axis=0)

    def whole(own):
        other = other_core(own)
        pair = jnp.where(core == 0, jnp.stack([own, other]), jnp.stack([other, own]))
        return pair.reshape(micro, 1, row_count, cols, features)

    high, low = split(latent_grad)
    output = whole(dot(resid_c.astype(BF16), pick, 1, 1).astype(BF16))
    latents_grad = whole(dot(high, pick, 1, 1) + dot(low, pick, 1, 1))
    mod_grad = jnp.stack([shift_a_grad, scale_a_grad, gate_a_grad, shift_f_grad, scale_f_grad, gate_f_grad])
    mod_grad = lax.dot_general(
        mod_grad, pick.astype(F32), (((1,), (1,)), ((), ())), precision=lax.Precision.HIGHEST
    )
    table_grads = []
    wire.join(butterfly_phases(butterfly(mod_grad, (TP,), jnp.add), (SEQ, DP), jnp.add, table_grads))
    wire.finish()
    (table_grad,), (head_peaks,), (small,) = table_grads, head_peaks, small
    down_grad = jnp.concatenate([down for _, down in ffn_grads], axis=1)
    up_grad = jnp.concatenate(
        [up[:, j * half : (j + 1) * half] for j in range(2) for up, _ in ffn_grads], axis=1
    )
    (cross_kv_grad, cross_out_grad), (cross_q_grad, q_grad, self_out_grad) = text_grads, token_grads

    factor = jnp.repeat(jnp.sqrt(CLIP_TAU / jnp.maximum(head_peaks, CLIP_TAU)), HEAD_DIM)

    def cut(grad, count, each, size):
        grad = grad[:own_rows].reshape(own_rows, count, each)[:, :, :size]
        return grad.transpose(1, 0, 2)

    def heads(grad):
        return grad[:own_rows, :heads_width]

    taps_grad = small[:18].reshape(2, 9, hidden)[:, :, :hidden_width].transpose(1, 0, 2)
    return (
        output,
        latents_grad,
        table_grad,
        jnp.stack([heads(grad) for grad in [q_grad] + kv_grads]),
        heads(self_out_grad).T,
        heads(cross_q_grad),
        cut(cross_kv_grad, 2, width, heads_width),
        heads(cross_out_grad).T,
        cut(up_grad, 2, hidden, hidden_width),
        small[20:22, :hidden_width],
        taps_grad,
        small[18:20, :hidden_width],
        down_grad[:own_rows, :hidden_width].T,
        cross_q.astype(F32) * factor[None, :],
        cross_kv[0].astype(F32) * factor[None, :],
    )


def solution(mesh):
    tokens = P(None, DP, SEQ, None, None)
    stacked, by_column, by_row = P(None, (DP, SEQ), TP), P(TP, (DP, SEQ)), P((DP, SEQ), TP)
    return jax.shard_map(
        shards,
        mesh=mesh,
        in_specs=(
            tokens, P(None, DP, None, None), P(None, DP), P(None, DP), tokens, P(), stacked, by_column, by_row,
            stacked, by_column, stacked, P(None, TP), P(None, None, TP), P(None, TP), by_column,
        ),
        out_specs=(
            tokens, tokens, P(), stacked, by_column, by_row, stacked, by_column, stacked, P(None, TP),
            P(None, None, TP), P(None, TP), by_column, by_row, by_row,
        ),
        check_vma=False,
    )
```

```python
import functools
import math

import jax
import jax.numpy as jnp
from jax import lax
from jax.experimental import pallas as pl
from jax.experimental.pallas import tpu as pltpu
from jax.sharding import PartitionSpec as P

DP, SEQ, TP = "dp", "seq", "tensor"
HEAD_DIM = 32
LANES = 128
NORM_EPS = 1e-06
ATTN_EPS = 1e-06
CLIP_TAU = 3.5
MASKED_FILL = -1e30
F32, BF16 = jnp.float32, jnp.bfloat16
VMEM_LIMIT = 48 * 1024 * 1024


def up_to(value, step):
    return -(-value // step) * step


def dot(left, right, left_dim, right_dim):
    return lax.dot_general(
        left, right, (((left_dim,), (right_dim,)), ((), ())), preferred_element_type=F32
    )


def split(values):
    high = values.astype(BF16)
    return high, (values - high.astype(F32)).astype(BF16)


def ring_of(axis):
    size = lax.axis_size(axis)
    if axis == DP and size % 2 == 0:
        return list(range(0, size, 2)) + list(range(size - 1, 0, -2))
    return list(range(size))


def ring_place(axis):
    size, index = lax.axis_size(axis), lax.axis_index(axis)
    if axis == DP and size % 2 == 0:
        return jnp.where(index % 2 == 0, index // 2, size - 1 - index // 2)
    return index


def ring_member(axis, place):
    size = lax.axis_size(axis)
    if axis == DP and size % 2 == 0:
        return jnp.where(place < size // 2, 2 * place, 2 * (size - 1 - place) + 1)
    return place


def shift(values, axis, step):
    if isinstance(step, list):
        return lax.ppermute(values, axis, step)
    cycle = ring_of(axis)
    size = len(cycle)
    return lax.ppermute(values, axis, [(cycle[i], cycle[(i + step) % size]) for i in range(size)])


def slot_order(size):
    ahead = size // 2
    order = []
    for step in range(ahead):
        order.append(ahead - step)
        if ahead + 1 + step < size:
            order.append(ahead + 1 + step)
    return order + [0]


def chip_back(back_dp, back_seq):
    dp_size, seq_size = lax.axis_size(DP), lax.axis_size(SEQ)
    from_dp = ring_member(DP, (ring_place(DP) - back_dp) % dp_size)
    return from_dp * seq_size + (lax.axis_index(SEQ) - back_seq) % seq_size


class Wire:
    def __init__(self):
        self.running, self.queue, self.last, self.before, self.patient = [], [], (), (), False
        self.stride, self.since = lax.axis_size(DP) // 2, lax.axis_size(DP)

    def join(self, phases):
        self.running.append((phases, next(phases)))

    def push(self, phases, patient):
        self.queue.append((phases, patient))

    def round(self, hurry=False):
        if self.queue and self.since >= self.stride:
            phases, self.patient = self.queue.pop(0)
            self.join(phases)
            self.since = 0
        elif self.patient and self.since >= self.stride and not hurry:
            return
        if not self.running:
            return
        self.since += 1
        sends = [send for _, pending in self.running for send in pending]
        values = tuple(value for value, _, _ in sends)
        if self.last:
            values, _ = lax.optimization_barrier((values, self.last))
        arrived = tuple(shift(value, axis, step) for value, (_, axis, step) in zip(values, sends))
        self.before, self.last = self.last, arrived
        running, at = [], 0
        for phases, pending in self.running:
            mine = arrived[at : at + len(pending)]
            at += len(pending)
            try:
                running.append((phases, phases.send(mine)))
            except StopIteration:
                pass
        self.running = running

    def after(self, value):
        return lax.optimization_barrier((value, self.last))[0] if self.last else value

    def step(self, value, slack=False):
        value = lax.optimization_barrier((value, self.before))[0] if slack else self.after(value)
        self.round()
        return value

    def need(self, done):
        while not done:
            self.round(True)
        return done

    def finish(self):
        while self.running or self.queue:
            self.round(True)


def butterfly_phases(values, axes, combine, done):
    for axis in axes:
        size = lax.axis_size(axis)
        bit = 1
        while bit < size:
            (arrived,) = yield [(values, axis, [(i, i ^ bit) for i in range(size)])]
            values = combine(values, arrived)
            bit *= 2
    done.append(values)


def columns(values, widths):
    at, parts = 0, []
    for width in widths:
        parts.append(values[:, at : at + width])
        at += width
    return parts


def gather_phases(first, second, done):
    size = lax.axis_size(DP)
    ahead = size // 2
    widths_a, widths_b = [w.shape[1] for w in first], [w.shape[1] for w in second]
    shard_a, shard_b = jnp.concatenate(first, axis=1), jnp.concatenate(second, axis=1)
    n_a, n_b = shard_a.shape[1], shard_b.shape[1]
    rows = shard_a.shape[0]
    (far_b,) = yield [(shard_b, SEQ, 1)]
    pieces = [jnp.concatenate([shard_a, shard_b, far_b], axis=1)] + [None] * (size - 1)
    far = [None] * size
    fresh = [0]
    for hop in range(1, ahead + 2):
        sends, places = [], []
        if hop <= ahead:
            sends.append((pieces[hop - 1], DP, 1))
            places.append(hop)
        if size - hop > ahead:
            sends.append((pieces[(size - hop + 1) % size], DP, -1))
            places.append(size - hop)
        across = [pieces[a][:, :n_a] for a in fresh]
        sends.append((jnp.concatenate(across, axis=0) if len(across) > 1 else across[0], SEQ, 1))
        arrived = yield sends
        for i, a in enumerate(fresh):
            far[a] = (arrived[-1], i * rows)
        for a, piece in zip(places, arrived):
            pieces[a] = piece
        fresh = places
    arrays, moves = [], []

    def source(array):
        for place, known in enumerate(arrays):
            if known is array:
                return place
        arrays.append(array)
        return len(arrays) - 1

    for a in range(size):
        near, (across, start) = source(pieces[a]), far[a]
        across = source(across)
        at = 0
        for weight, width in enumerate(widths_a):
            moves.append((weight, a, near, 0, at, width))
            moves.append((weight, size + a, across, start, at, width))
            at += width
        for weight, width in enumerate(widths_b):
            moves.append((len(widths_a) + weight, a, near, 0, at, width))
            moves.append((len(widths_a) + weight, size + a, near, 0, at + n_b, width))
            at += width
    place = jnp.stack([chip_back(a, b).astype(jnp.int32) for b in range(2) for a in range(size)])
    done.extend(assemble(place, arrays, moves, rows, widths_a + widths_b))


def assemble_kernel(moves, rows, count, place_ref, *refs):
    sources, outs = refs[:count], refs[count:]
    for slot in range(place_ref.shape[0]):

        @pl.when(pl.program_id(0) == slot)
        def _(slot=slot):
            for weight, to, array, start, at, width in moves:
                if to == slot:
                    outs[weight][...] = sources[array][start : start + rows, at : at + width]


def assemble(place, arrays, moves, rows, widths):
    slots = place.shape[0]
    return pl.pallas_call(
        functools.partial(assemble_kernel, moves, rows, len(arrays)),
        grid_spec=pltpu.PrefetchScalarGridSpec(
            num_scalar_prefetch=1,
            grid=(slots,),
            in_specs=[
                pl.BlockSpec(array.shape, lambda i, place_ref: (0, 0), pipeline_mode=pl.Buffered(1)) for array in arrays
            ],
            out_specs=[pl.BlockSpec((rows, width), lambda i, place_ref: (place_ref[i], 0)) for width in widths],
        ),
        out_shape=[struct((slots * rows, width), BF16) for width in widths],
        compiler_params=pltpu.CompilerParams(vmem_limit_bytes=VMEM_LIMIT),
        cost_estimate=pl.CostEstimate(flops=0, bytes_accessed=slots * rows * sum(widths) * 4, transcendentals=0),
    )(place, *arrays)


def gather(wire, first, second, gate=None):
    done = []
    if wire is not None and lax.axis_size(SEQ) == 2:
        wire.push(gather_phases(first, second, done), False)
    else:
        shard = jnp.concatenate(first + second, axis=1)
        if gate is not None:
            shard, _ = lax.optimization_barrier((shard, gate))
        full = lax.all_gather(shard, (DP, SEQ), axis=0, tiled=False).reshape(-1, shard.shape[1])
        done.extend(columns(full, [w.shape[1] for w in first + second]))
    return done


def combine_kernel(near_count, flat_count, index_ref, *refs):
    near, flat, far = refs[:near_count], refs[near_count : near_count + flat_count], refs[near_count + flat_count]
    running, out = refs[near_count + flat_count + 1 : -1], refs[-1]
    at = 0
    for place, ref in enumerate(near + flat):
        width = ref.shape[1]
        part = ref[...].astype(F32)
        if place < near_count:
            part = part + far[:, at : at + width].astype(F32)
        for other in running:
            part = part + other[:, at : at + width].astype(F32)
        out[:, at : at + width] = part.astype(out.dtype)
        at += width


def combine(blocks, near_count, far, running, rows, dtype):
    steps = 3 if rows % 48 == 0 else 1
    size = rows // steps
    width = sum(array.shape[1] for array, _ in blocks)
    sources = blocks + [far] + [(array, 0) for array in running]
    index = jnp.stack([jnp.asarray(at, jnp.int32) for _, at in sources])

    def spec(place, array):
        return pl.BlockSpec((size, array.shape[1]), lambda i, index_ref: (index_ref[place] * steps + i, 0))

    return pl.pallas_call(
        functools.partial(combine_kernel, near_count, len(blocks) - near_count),
        grid_spec=pltpu.PrefetchScalarGridSpec(
            num_scalar_prefetch=1,
            grid=(steps,),
            in_specs=[spec(place, array) for place, (array, _) in enumerate(sources)],
            out_specs=pl.BlockSpec((size, width), lambda i, index_ref: (i, 0)),
        ),
        out_shape=struct((rows, width), dtype),
        compiler_params=pltpu.CompilerParams(vmem_limit_bytes=VMEM_LIMIT),
        cost_estimate=pl.CostEstimate(flops=rows * width * 4, bytes_accessed=rows * width * 10, transcendentals=0),
    )(index, *[array for array, _ in sources])


def pack_kernel(index_ref, *refs):
    out, at = refs[-1], 0
    for ref in refs[:-1]:
        out[:, at : at + ref.shape[1]] = ref[...]
        at += ref.shape[1]


def pack(index, parts, rows):
    count, width = index.shape[0], sum(part.shape[1] for part in parts)
    return pl.pallas_call(
        pack_kernel,
        grid_spec=pltpu.PrefetchScalarGridSpec(
            num_scalar_prefetch=1,
            grid=(count,),
            in_specs=[pl.BlockSpec((rows, part.shape[1]), lambda i, index_ref: (index_ref[i], 0)) for part in parts],
            out_specs=pl.BlockSpec((rows, width), lambda i, index_ref: (i, 0)),
        ),
        out_shape=struct((count * rows, width), BF16),
        compiler_params=pltpu.CompilerParams(vmem_limit_bytes=VMEM_LIMIT),
        cost_estimate=pl.CostEstimate(flops=0, bytes_accessed=count * rows * width * 4, transcendentals=0),
    )(index, *parts)


def scatter_phases(first, second, done):
    size = lax.axis_size(DP)
    ahead = size // 2
    order = slot_order(size)
    rows = first[0].shape[0] // (2 * size)
    widths = [part.shape[1] for part in first + second]
    n_a = sum(part.shape[1] for part in first)
    n_b = sum(part.shape[1] for part in second)

    def across(start, count):
        index = jnp.stack([chip_back(order[start + i], 1).astype(jnp.int32) for i in range(count)])
        return (pack(index, first, rows), SEQ, 1)

    def value(a, far, running, dtype):
        blocks = [(part, chip_back(a, 0)) for part in first]
        blocks += [(part, chip_back(a, b)) for b in range(2) for part in second]
        return combine(blocks, len(first), far[a], running, rows, dtype)

    def take(far, arrived, start):
        for i in range(arrived.shape[0] // rows):
            far[order[start + i]] = (arrived, i)

    far = {}
    (arrived,) = yield [across(0, 2)]
    take(far, arrived, 0)
    back = forth = None
    for step in range(ahead):
        sends = []
        back = value(ahead - step, far, [] if back is None else [back], BF16)
        sends.append((back, DP, -1))
        place = ahead + 1 + step
        if place < size:
            forth = value(place, far, [] if forth is None else [forth], BF16)
            sends.append((forth, DP, 1))
        start = 2 * step + 2
        if start < size:
            sends.append(across(start, min(2, size - start)))
        arrived = yield sends
        back = arrived[0]
        if place < size:
            forth = arrived[1]
        if start < size:
            take(far, arrived[-1], start)
    total = value(0, far, [back, forth], F32)
    (other,) = yield [(total[:, n_a + n_b :].astype(BF16), SEQ, 1)]
    mine = total[:, n_a : n_a + n_b] + other.astype(F32)
    done.extend(columns(total[:, :n_a], widths[: len(first)]) + columns(mine, widths[len(first) :]))


def scatter(wire, first, second):
    done = []
    if wire is not None and lax.axis_size(SEQ) == 2:
        wire.push(scatter_phases(first, second, done), True)
    else:
        parts = jnp.concatenate(first + second, axis=1)
        devices = lax.axis_size(DP) * lax.axis_size(SEQ)
        parts = parts.reshape(devices, parts.shape[0] // devices, parts.shape[1])
        total = lax.psum_scatter(parts, (DP, SEQ), scatter_dimension=0, tiled=False)
        done.extend(columns(total.astype(F32), [w.shape[1] for w in first + second]))
    return done


def butterfly(values, axes, combine):
    for axis in axes:
        size = lax.axis_size(axis)
        bit = 1
        while bit < size:
            values = combine(values, lax.ppermute(values, axis, [(i, i ^ bit) for i in range(size)]))
            bit *= 2
    return values


def other_core(values):
    return lax.ppermute(values, TP, [(0, 1), (1, 0)])


def head_block():
    row = lax.broadcasted_iota(jnp.int32, (LANES, LANES), 0) // HEAD_DIM
    col = lax.broadcasted_iota(jnp.int32, (LANES, LANES), 1) // HEAD_DIM
    return row == col


def fold(state, total):
    state = jnp.where(head_block(), state, 0.0)
    rows = sum(state[i * HEAD_DIM : (i + 1) * HEAD_DIM] for i in range(LANES // HEAD_DIM))
    return jnp.concatenate([rows, total, jnp.zeros((7, LANES), F32)], axis=0)


def unfold(folded):
    state = jnp.concatenate([folded[:HEAD_DIM]] * (LANES // HEAD_DIM), axis=0)
    return jnp.where(head_block(), state, 0.0), folded[HEAD_DIM : HEAD_DIM + 1]


def softplus(values):
    return jnp.maximum(values, 0.0) + jnp.log1p(jnp.exp(-jnp.abs(values)))


def head_sum(values):
    ones = jnp.where(head_block(), 1.0, 0.0).astype(BF16)
    high, low = split(values)
    return dot(high, ones, 1, 0) + dot(low, ones, 1, 0)


def state_kernel(key_ref, value_ref, state_ref):
    key = softplus(key_ref[...]).astype(BF16)
    value = value_ref[...].astype(BF16)
    total = jnp.sum(key.astype(F32), axis=0, keepdims=True)
    state_ref[0, 0] = fold(dot(key, value, 0, 0), total)


def ratio_parts(query_ref, state_ref):
    query = softplus(query_ref[...]).astype(BF16)
    state, total = unfold(state_ref[0, 0])
    high, low = split(state)
    numerator = dot(query, high, 1, 0) + dot(query, low, 1, 0)
    denominator = head_sum(query.astype(F32) * total) + ATTN_EPS
    return query, high, low, total, numerator, denominator


def mix_kernel(query_ref, state_ref, mixed_ref):
    query, high, low, total, numerator, denominator = ratio_parts(query_ref, state_ref)
    mixed_ref[...] = (numerator / denominator).astype(BF16)


def mix_back_kernel(query_ref, state_ref, grad_ref, query_grad_ref, state_grad_ref):
    query, high, low, total, numerator, denominator = ratio_parts(query_ref, state_ref)
    mixed_grad = grad_ref[...]
    numer_grad = mixed_grad / denominator
    denom_grad = -head_sum(mixed_grad * numerator) / (denominator * denominator)
    up, down = split(numer_grad)
    state_grad = dot(query, up, 0, 0) + dot(query, down, 0, 0)
    total_grad = jnp.sum(query.astype(F32) * denom_grad, axis=0, keepdims=True)
    state_grad_ref[0, 0] = fold(state_grad, total_grad)
    side = dot(up, high, 1, 1) + dot(up, low, 1, 1) + dot(down, high, 1, 1) + denom_grad * total
    query_grad_ref[...] = (side * jax.nn.sigmoid(query_ref[...])).astype(BF16)


def state_back_kernel(key_ref, value_ref, state_ref, out_ref):
    state, total = unfold(state_ref[0, 0])
    high, low = split(state)

    @pl.when(pl.program_id(0) == 0)
    def _():
        value = value_ref[...].astype(BF16)
        side = dot(value, high, 1, 1) + dot(value, low, 1, 1) + total
        out_ref[...] = (side * jax.nn.sigmoid(key_ref[...])).astype(BF16)

    @pl.when(pl.program_id(0) == 1)
    def _():
        key = softplus(key_ref[...]).astype(BF16)
        out_ref[...] = (dot(key, high, 1, 0) + dot(key, low, 1, 0)).astype(BF16)


def head_of(values, head):
    lane = lax.broadcasted_iota(jnp.int32, values.shape, 1) // HEAD_DIM
    return jnp.where(lane == head, values, jnp.zeros_like(values))


def weigh(key_head, query, visible):
    scores = dot(key_head, query, 1, 1) * HEAD_DIM ** (-0.5)
    masked = jnp.where(visible, scores, MASKED_FILL)
    top = jnp.max(masked, axis=0, keepdims=True)
    exponent = jnp.exp(masked - top)
    return exponent * (1.0 / jnp.sum(exponent, axis=0, keepdims=True)), top


def cross_kernel(length_ref, query_ref, key_ref, value_ref, out_ref, peak_ref):
    query, key, value = query_ref[...], key_ref[...], value_ref[...]
    tokens, slots = query.shape[0], key.shape[0]
    visible = lax.broadcasted_iota(jnp.int32, (slots, tokens), 0) < length_ref[pl.program_id(0)]
    total = jnp.zeros((LANES, tokens), F32)
    peak_ref[0, 0] = jnp.zeros((8, LANES), F32)
    for head in range(LANES // HEAD_DIM):
        probability, top = weigh(head_of(key, head), query, visible)
        total = total + dot(head_of(value, head), probability.astype(BF16), 0, 0)
        peak_ref[0, 0, head : head + 1] = jnp.broadcast_to(jnp.max(top, axis=1, keepdims=True), (1, LANES))
    out_ref[...] = total.T.astype(BF16)


def cross_back_kernel(length_ref, query_ref, key_ref, value_ref, grad_ref, query_grad_ref, key_grad_ref, value_grad_ref):
    query, key, value, grad = query_ref[...], key_ref[...], value_ref[...], grad_ref[...]
    tokens, slots = query.shape[0], key.shape[0]
    visible = lax.broadcasted_iota(jnp.int32, (slots, tokens), 0) < length_ref[pl.program_id(0)]
    query_grad = jnp.zeros((LANES, tokens), F32)
    key_grad = jnp.zeros((slots, LANES), F32)
    value_grad = jnp.zeros((slots, LANES), F32)
    for head in range(LANES // HEAD_DIM):
        key_head = head_of(key, head)
        probability, top = weigh(key_head, query, visible)
        prob_grad = dot(head_of(value, head), grad, 1, 1)
        value_grad = value_grad + head_of(dot(probability.astype(BF16), grad, 1, 0), head)
        mean = jnp.sum(probability * prob_grad, axis=0, keepdims=True)
        score_grad = (probability * (prob_grad - mean)).astype(BF16)
        key_grad = key_grad + head_of(dot(score_grad, query, 1, 0), head)
        query_grad = query_grad + dot(key_head, score_grad, 0, 0)
    scale = HEAD_DIM ** (-0.5)
    query_grad_ref[...] = (query_grad * scale).T.astype(BF16)
    key_grad_ref[...] = (key_grad * scale).astype(BF16)
    value_grad_ref[...] = value_grad.astype(BF16)


def silu(values):
    return values * jax.nn.sigmoid(values)


def silu_slope(values):
    sigma = jax.nn.sigmoid(values)
    return sigma * (1.0 + values * (1.0 - sigma))


def columns_of(values, cols):
    place = lax.broadcasted_iota(jnp.int32, values.shape, 0) % cols
    count = values.shape[0]
    left = jnp.where(place == 0, 0.0, pltpu.roll(values, 1, 0))
    right = jnp.where(place == cols - 1, 0.0, pltpu.roll(values, count - 1, 0))
    return left, values, right


def strips_of(tokens, cols):
    size = 4 * cols if tokens % (4 * cols) == 0 else cols
    return [(at, size) for at in range(0, tokens, size)]


def stage_columns(scratch, top, middle, bottom, cols):
    tokens = middle.shape[0]
    full = jnp.concatenate([top.astype(F32), middle, bottom.astype(F32)], axis=0)
    for place, part in enumerate(columns_of(full, cols)):
        scratch[place] = part


def taps(scratch, weight, at, size, cols, mirror):
    result = None
    for row_tap in range(3):
        for col_tap in range(3):
            row_at = 2 - row_tap if mirror else row_tap
            col_at = 2 - col_tap if mirror else col_tap
            tap = 3 * row_tap + col_tap
            term = scratch[col_at, at + row_at * cols : at + row_at * cols + size] * weight[tap : tap + 1]
            result = term if result is None else result + term
    return result


def conv_kernel(cols, z0, z1, top0, top1, bottom0, bottom1, grad_ref, w_ref, b_ref, gated_ref, out0, out1, small_ref, s0, s1):
    tokens = z0.shape[0]
    for z, top, bottom, scratch in ((z0, top0, bottom0, s0), (z1, top1, bottom1, s1)):
        stage_columns(scratch, top[0], silu(z[...]).astype(BF16).astype(F32), bottom[0], cols)
    sums = [jnp.zeros((8, LANES), F32) for _ in range(20)]
    for at, size in strips_of(tokens, cols):
        first = taps(s0, w_ref[0], at, size, cols, False) + b_ref[0, 0:1]
        second = taps(s1, w_ref[1], at, size, cols, False) + b_ref[1, 0:1]
        grad = grad_ref[at : at + size]
        sigma = jax.nn.sigmoid(second)
        gate = second * sigma
        gated_ref[at : at + size] = (first * gate).astype(BF16)
        slope = sigma + gate * (1.0 - sigma)
        for j, (part, scratch, out) in enumerate(
            ((grad * gate, s0, out0), (grad * first * slope, s1, out1))
        ):
            out[at : at + size] = part.astype(BF16)
            for row_tap in range(3):
                for col_tap in range(3):
                    start = at + row_tap * cols
                    product = part * scratch[col_tap, start : start + size]
                    place = 9 * j + 3 * row_tap + col_tap
                    sums[place] = sums[place] + jnp.sum(product.reshape(size // 8, 8, LANES), axis=0)
            sums[18 + j] = sums[18 + j] + jnp.sum(part.reshape(size // 8, 8, LANES), axis=0)
    for place in range(20):
        small_ref[0, place : place + 1] = jnp.sum(sums[place], axis=0, keepdims=True)
    small_ref[0, 20:24] = jnp.zeros((4, LANES), F32)


def act_back_kernel(cols, z0, z1, grad0, grad1, top0, top1, bottom0, bottom1, w_ref, out0, out1, bias_ref, s0, s1):
    tokens = z0.shape[0]
    for grad, top, bottom, scratch in ((grad0, top0, bottom0, s0), (grad1, top1, bottom1, s1)):
        stage_columns(scratch, top[0], grad[...].astype(F32), bottom[0], cols)
    for j, (z, scratch, out) in enumerate(((z0, s0, out0), (z1, s1, out1))):
        total = jnp.zeros((8, LANES), F32)
        for at, size in strips_of(tokens, cols):
            part = taps(scratch, w_ref[j], at, size, cols, True) * silu_slope(z[at : at + size])
            out[at : at + size] = part.astype(BF16)
            total = total + jnp.sum(part.reshape(size // 8, 8, LANES), axis=0)
        bias_ref[0, j : j + 1] = jnp.sum(total, axis=0, keepdims=True)
    bias_ref[0, 2:8] = jnp.zeros((6, LANES), F32)


def call(kernel, grid, in_specs, out_specs, out_shape, flops, moved, scratch=(), **extra):
    return pl.pallas_call(
        kernel,
        grid=grid,
        in_specs=in_specs,
        out_specs=out_specs,
        out_shape=out_shape,
        scratch_shapes=list(scratch),
        compiler_params=pltpu.CompilerParams(vmem_limit_bytes=VMEM_LIMIT),
        cost_estimate=pl.CostEstimate(flops=int(flops), bytes_accessed=int(moved), transcendentals=0),
        **extra,
    )


def struct(shape, dtype):
    return jax.ShapeDtypeStruct(shape, dtype)


class Kernels:
    def __init__(self, micro, tokens, cols, width, hidden, slots):
        self.micro, self.tokens, self.cols = micro, tokens, cols
        self.width, self.hidden, self.slots = width, hidden, slots
        self.groups, self.units = width // LANES, hidden // LANES

    def tile(self, offset=0):
        return pl.BlockSpec((self.tokens, LANES), lambda m, g: (m, g + offset))

    def folded(self):
        return pl.BlockSpec((1, 1, HEAD_DIM + 8, LANES), lambda m, g: (m, g, 0, 0))

    def folded_shape(self):
        return struct((self.micro, self.groups, HEAD_DIM + 8, LANES), F32)

    def states(self, keys_values):
        size = self.micro * self.tokens * self.width
        return call(
            state_kernel, (self.micro, self.groups), [self.tile(), self.tile(self.groups)],
            self.folded(), self.folded_shape(), size * 600, size * 8,
        )(keys_values, keys_values)

    def mix(self, queries, states):
        size = self.micro * self.tokens * self.width
        return call(
            mix_kernel, (self.micro, self.groups), [self.tile(), self.folded()],
            self.tile(), struct(queries.shape, BF16), size * 1500, size * 6,
        )(queries, states)

    def mix_back(self, queries, states, mixed_grad):
        size = self.micro * self.tokens * self.width
        return call(
            mix_back_kernel, (self.micro, self.groups), [self.tile(), self.folded(), self.tile()],
            [self.tile(), self.folded()], [struct(queries.shape, BF16), self.folded_shape()],
            size * 4000, size * 10,
        )(queries, states, mixed_grad)

    def states_back(self, keys_values, state_grad):
        groups = self.groups
        size = self.micro * self.tokens * self.width
        tile = lambda offset: pl.BlockSpec((self.tokens, LANES), lambda j, m, g: (m, g + offset))
        return call(
            state_back_kernel, (2, self.micro, groups),
            [tile(0), tile(groups), pl.BlockSpec((1, 1, HEAD_DIM + 8, LANES), lambda j, m, g: (m, g, 0, 0))],
            pl.BlockSpec((self.tokens, LANES), lambda j, m, g: (m, g + j * groups)),
            struct(keys_values.shape, BF16), size * 1500, size * 20,
        )(keys_values, keys_values, state_grad)

    def text_tile(self, offset):
        return pl.BlockSpec((self.slots, LANES), lambda m, g: (m, g + offset))

    def cross(self, lengths, queries, text):
        size = self.micro * self.tokens * self.width
        smem = pl.BlockSpec(memory_space=pltpu.SMEM)
        peak = pl.BlockSpec((1, 1, 8, LANES), lambda m, g: (m, g, 0, 0))
        return call(
            cross_kernel, (self.micro, self.groups),
            [smem, self.tile(), self.text_tile(0), self.text_tile(self.groups)],
            [self.tile(), peak],
            [struct(queries.shape, BF16), struct((self.micro, self.groups, 8, LANES), F32)],
            size * 20000, size * 6,
        )(lengths, queries, text, text)

    def cross_back(self, lengths, queries, text, attended_grad):
        size = self.micro * self.tokens * self.width
        smem = pl.BlockSpec(memory_space=pltpu.SMEM)
        return call(
            cross_back_kernel, (self.micro, self.groups),
            [smem, self.tile(), self.text_tile(0), self.text_tile(self.groups), self.tile()],
            [self.tile(), self.text_tile(0), self.text_tile(0)],
            [struct(queries.shape, BF16), struct((text.shape[0], self.width), BF16), struct((text.shape[0], self.width), BF16)],
            size * 50000, size * 6,
        )(lengths, queries, text, text, attended_grad)

    def edge(self, offset=0):
        return pl.BlockSpec((1, self.cols, LANES), lambda m, g: (m, 0, g + offset))

    def scratch(self):
        return pltpu.VMEM((3, self.tokens + 2 * self.cols, LANES), F32)

    def conv_specs(self):
        units = self.units
        return (
            [self.tile(), self.tile(units), self.edge(), self.edge(units), self.edge(), self.edge(units)],
            [
                pl.BlockSpec((2, 9, LANES), lambda m, g: (0, 0, g)),
                pl.BlockSpec((2, 1, LANES), lambda m, g: (0, 0, g)),
            ],
        )

    def conv(self, pre, top, bottom, grad, conv_w, conv_b):
        size = self.micro * self.tokens * self.hidden
        data, weights = self.conv_specs()
        one = struct((pre.shape[0], self.hidden), BF16)
        return call(
            functools.partial(conv_kernel, self.cols), (self.micro, self.units),
            data + [self.tile()] + weights,
            [self.tile()] * 3 + [pl.BlockSpec((1, 24, LANES), lambda m, g: (m, 0, g))],
            [one, one, one, struct((self.micro, 24, self.hidden), F32)], size * 40000, size * 16,
            [self.scratch(), self.scratch()],
        )(pre, pre, top, top, bottom, bottom, grad, conv_w, conv_b)

    def act_back(self, pre, grads, tops, bottoms, conv_w):
        size = self.micro * self.tokens * self.hidden
        data, weights = self.conv_specs()
        one = struct((pre.shape[0], self.hidden), BF16)
        return call(
            functools.partial(act_back_kernel, self.cols), (self.micro, self.units),
            data[:2] + [self.tile(), self.tile()] + [self.edge()] * 4 + weights[:1],
            [self.tile(), self.tile(), pl.BlockSpec((1, 8, LANES), lambda m, g: (m, 0, g))],
            [one, one, struct((self.micro, 8, self.hidden), F32)], size * 40000, size * 20,
            [self.scratch(), self.scratch()],
        )(pre, pre, *grads, *tops, *bottoms, conv_w)


def pad_to(values, *sizes):
    return jnp.pad(values, [(0, size - now) for size, now in zip(sizes, values.shape)])


def side_by_side(parts, width):
    return jnp.concatenate([pad_to(part, part.shape[0], width) for part in parts], axis=1)


def halos(rows, cols):
    size = lax.axis_size(SEQ)
    up = [(i, i + 1) for i in range(size - 1)]
    down = [(j, i) for i, j in up]
    return (
        lax.ppermute(rows[:, -cols:], SEQ, up),
        lax.ppermute(rows[:, :cols], SEQ, down),
    )


def shards(latents, text, timesteps, text_lengths, cotangent, table, self_qkv, self_out, cross_q, cross_kv,
           cross_out, up_w, up_b, conv_w, conv_b, down_w):
    micro, _, row_count, cols, features = latents.shape
    tokens = row_count * cols
    own_rows, heads_width = cross_q.shape
    hidden_width = up_b.shape[1]
    text_len = text.shape[2]
    width, hidden, slots = up_to(heads_width, LANES), up_to(hidden_width, 2 * LANES), up_to(text_len, 16)
    rows = up_to(own_rows, 16)
    dp_size, seq_size = lax.axis_size(DP), lax.axis_size(SEQ)
    wide = dp_size * seq_size * rows
    core = lax.axis_index(TP)
    kernels = Kernels(micro, tokens, cols, width, hidden // 2, slots)

    half = hidden // 2

    def units(values, at):
        return pad_to(values[:, at * half : (at + 1) * half], values.shape[0], half)

    def heads_rows(*parts):
        return pad_to(side_by_side(parts, width), rows, len(parts) * width)

    def ffn_rows(at):
        up = jnp.concatenate([units(up_w[0], at), units(up_w[1], at)], axis=1)
        return [pad_to(up, rows, 2 * half)], [pad_to(units(down_w.T, at), rows, half)]

    wire = Wire()
    qkv_rows = gather(wire, [heads_rows(self_qkv[1], self_qkv[2])], [heads_rows(self_qkv[0])])
    token_rows = gather(wire, [heads_rows(cross_q)], [heads_rows(self_out.T)])
    text_rows = gather(wire, [heads_rows(cross_kv[0], cross_kv[1])], [heads_rows(cross_out.T)])

    unit_rows = [gather(wire, *ffn_rows(at)) for at in range(2)]

    slot = jnp.arange(wide)
    valid = slot % rows < own_rows
    channel = jnp.where(valid, slot // rows * own_rows + slot % rows, -1)
    pick = (jnp.arange(features)[:, None] == channel[None, :]).astype(BF16)

    def relative(values):
        return jnp.where(core == 0, values, jnp.flip(values, axis=0))

    lengths = relative(text_lengths[:, 0])
    caption = jnp.pad(relative(text[:, 0]), ((0, 0), (0, slots - text_len), (0, 0))).reshape(micro * slots, features)
    caption = dot(caption, pick, 1, 0).astype(BF16)
    resid_in = dot(lax.dynamic_index_in_dim(latents, core, 0, False).reshape(tokens, features), pick, 1, 0)
    grad_out = dot(lax.dynamic_index_in_dim(cotangent, core, 0, False).reshape(tokens, features), pick, 1, 0)

    frequency = jnp.exp(-math.log(10000.0) * channel.astype(F32) / features)
    time = lax.dynamic_index_in_dim(timesteps[:, 0], core, 0, False).astype(F32)
    waves = 0.5 * jnp.sin(time * frequency[None, :] + jnp.arange(6, dtype=F32)[:, None])
    mod_table = jnp.dot(table, pick.astype(F32), precision=lax.Precision.HIGHEST)
    modulation = jnp.where(valid[None, :], mod_table + waves, 0.0)
    shift_a, scale_a, gate_a, shift_f, scale_f, gate_f = [modulation[i] for i in range(6)]

    def normalise(values):
        center = jnp.where(valid[None, :], values - jnp.sum(values, axis=1, keepdims=True) / features, 0.0)
        spread = jnp.sum(center * center, axis=1, keepdims=True) / features
        inverse = lax.rsqrt(spread + NORM_EPS)
        return center * inverse, inverse

    def normalise_back(values, grad, stretch):
        unit, inverse = normalise(values)
        shift_grad = jnp.sum(grad, axis=0)
        scale_grad = jnp.sum(grad * unit, axis=0)
        scaled = grad * (1.0 + stretch)
        mean = jnp.sum(scaled, axis=1, keepdims=True) / features
        along = jnp.sum(scaled * unit, axis=1, keepdims=True) / features
        return jnp.where(valid[None, :], inverse * (scaled - mean - unit * along), 0.0), shift_grad, scale_grad

    def both(own):
        return jnp.concatenate([own, other_core(own)], axis=0)

    def core_total(parts):
        def product(at):
            return sum(dot(left[at : at + tokens], right, 1, dim) for left, right, dim in parts)

        return other_core(product(tokens).astype(BF16)).astype(F32) + product(0)

    ffn_out_grad = both((gate_f * grad_out).astype(BF16))

    def weight_grad(activation, grad):
        return dot(activation, grad, 0, 0).astype(BF16)

    unit_a, _ = normalise(resid_in)
    normed = both((unit_a * (1.0 + scale_a) + shift_a).astype(BF16))
    w_kv, w_q = wire.need(qkv_rows)
    keys_values = dot(normed, w_kv, 1, 0)
    states = butterfly(kernels.states(keys_values), (SEQ,), jnp.add)
    queries = dot(wire.step(normed), w_q, 1, 0)
    mixed = kernels.mix(queries, wire.step(states))
    w_cq, w_so = wire.need(token_rows)
    self_term = core_total([(mixed, w_so, 1)])
    resid_a = resid_in + gate_a * self_term
    cross_input = both(resid_a.astype(BF16))
    cross_query = dot(cross_input, w_cq, 1, 0).astype(BF16)
    w_ckv, w_co = wire.need(text_rows)
    text_proj = dot(caption, w_ckv, 1, 0).astype(BF16)
    attended, peaks = kernels.cross(lengths, cross_query, wire.step(text_proj))
    head_count = heads_width // HEAD_DIM
    head_peaks = []
    own_peaks = jnp.max(peaks[:, :, : LANES // HEAD_DIM, 0], axis=0).reshape(-1)[:head_count]
    wire.join(butterfly_phases(own_peaks, (SEQ, DP), jnp.maximum, head_peaks))
    resid_b = resid_a + core_total([(wire.step(attended), w_co, 1)])
    unit_f, _ = normalise(resid_b)
    normed_ffn = both((unit_f * (1.0 + scale_f) + shift_f).astype(BF16))

    ffn_terms, backs, smalls, ffn_grads = [], [], [], []
    for at in range(2):
        w_up, w_down = wire.need(unit_rows[at])
        if at == 1:
            early, _ = lax.optimization_barrier((early, w_down))
            ffn_grads.append([part for parts in early for part in scatter(None, [parts], [])])
        bias = jnp.concatenate([units(up_b[0:1], at), units(up_b[1:2], at)], axis=1)
        filters = jnp.stack([units(conv_w[:, j], at) for j in range(2)])
        filter_bias = jnp.stack([units(conv_b[j : j + 1], at) for j in range(2)])
        pre = dot(wire.step(normed_ffn) if at == 0 else normed_ffn, w_up, 1, 0) + bias
        by_micro = pre.reshape(micro, tokens, 2 * half)
        edges = jnp.concatenate([by_micro[:, :cols], by_micro[:, -cols:]], axis=1)
        top, bottom = halos(silu(edges).astype(BF16), cols)
        gated_grad = dot(ffn_out_grad, w_down, 1, 0)
        if at == 0:
            pre, top, bottom = wire.step((pre, top, bottom))
        gated, conv_grad0, conv_grad1, small = kernels.conv(pre, top, bottom, gated_grad, filters, filter_bias)
        edges = [grad.reshape(micro, tokens, half) for grad in (conv_grad0, conv_grad1)]
        edges = jnp.concatenate(
            [jnp.concatenate([grad[:, :cols], grad[:, -cols:]], axis=1) for grad in edges], axis=2
        )
        top_grad, bottom_grad = halos(edges, cols)
        down_parts = weight_grad(ffn_out_grad, gated)
        if at == 0:
            top_grad, bottom_grad = wire.step((top_grad, bottom_grad))
        up_low0, up_low1, bias_grad = kernels.act_back(
            pre, (conv_grad0, conv_grad1), [top_grad[:, :, :half], top_grad[:, :, half:]],
            [bottom_grad[:, :, :half], bottom_grad[:, :, half:]], filters,
        )
        smalls.append(jnp.concatenate([jnp.sum(small, axis=0)[:20], jnp.sum(bias_grad, axis=0)[:2]], axis=0))
        if at == 0:
            up_low0, up_low1 = wire.step((up_low0, up_low1))
        up_low = jnp.concatenate([up_low0, up_low1], axis=1)
        up_parts = weight_grad(normed_ffn, up_low)
        if at == 0:
            early = (up_parts, down_parts)
            normed_ffn, _ = lax.optimization_barrier((normed_ffn, early))
        else:
            ffn_grads.append(scatter(wire, [up_parts], [down_parts]))
            up_low, _ = lax.optimization_barrier((up_low, (up_parts, down_parts)))
        ffn_terms.append((gated, w_down, 1))
        backs.append((up_low, w_up, 1))

    backs[1] = (wire.step(up_low, True), *backs[1][1:])
    normed_ffn_grad = core_total(backs)
    resid_b_part, shift_f_grad, scale_f_grad = normalise_back(resid_b, normed_ffn_grad, scale_f)
    resid_b_grad = grad_out + resid_b_part
    cross_grad = both(wire.step(resid_b_grad, True).astype(BF16))
    attended_grad = dot(cross_grad, w_co, 1, 0).astype(BF16)
    query_grad, key_grad, value_grad = kernels.cross_back(lengths, cross_query, text_proj, wire.step(attended_grad, True))
    (query_grad, key_grad, value_grad), _ = lax.optimization_barrier(((query_grad, key_grad, value_grad), ffn_grads[0][1]))
    query_grad, key_grad, value_grad = wire.step((query_grad, key_grad, value_grad), True)
    cross_out_parts = weight_grad(cross_grad, attended)
    cross_kv_parts = weight_grad(caption, jnp.concatenate([key_grad, value_grad], axis=1))
    text_grads = scatter(None, [cross_kv_parts], [])
    resid_a_grad = resid_b_grad + core_total([(wire.step(query_grad, True), w_cq, 1)])
    cross_q_parts = weight_grad(cross_input, query_grad)
    gate_a_grad = jnp.sum(resid_a_grad * self_term, axis=0)
    self_grad = both((gate_a * resid_a_grad).astype(BF16))
    mixed_grad = dot(wire.step(self_grad, True), w_so, 1, 0)
    mixed_grad, _ = lax.optimization_barrier((mixed_grad, ffn_grads[0][0]))
    q_low, state_grad = kernels.mix_back(queries, states, wire.step(mixed_grad, True))
    self_out_parts = weight_grad(self_grad, mixed)
    state_grad = butterfly(state_grad, (SEQ,), jnp.add)
    small = []
    wire.join(butterfly_phases(jnp.concatenate(smalls, axis=1), (SEQ, DP), jnp.add, small))
    token_grads = scatter(wire, [cross_q_parts, weight_grad(normed, q_low), cross_out_parts], [self_out_parts])
    kv_low = kernels.states_back(keys_values, wire.step(state_grad, True))
    kv_parts = weight_grad(normed, kv_low)
    kv_low, _ = lax.optimization_barrier((wire.step(kv_low, True), (text_grads, kv_parts)))
    kv_grads = scatter(None, [kv_parts], [])
    normed_grad = core_total([(q_low, w_q, 1), (kv_low, w_kv, 1)])
    resid_part, shift_a_grad, scale_a_grad = normalise_back(resid_in, wire.step(normed_grad, True), scale_a)
    latent_grad = resid_a_grad + resid_part
    ffn_terms = wire.after([left for left, _, _ in ffn_terms])
    ffn_out = core_total([(left, rows_of[1], 1) for left, rows_of in zip(ffn_terms, unit_rows)])
    resid_c = resid_b + gate_f * ffn_out
    gate_f_grad = jnp.sum(grad_out * ffn_out, axis=0)

    def whole(own):
        other = other_core(own)
        pair = jnp.where(core == 0, jnp.stack([own, other]), jnp.stack([other, own]))
        return pair.reshape(micro, 1, row_count, cols, features)

    high, low = split(latent_grad)
    output = whole(dot(resid_c.astype(BF16), pick, 1, 1).astype(BF16))
    latents_grad = whole(dot(high, pick, 1, 1) + dot(low, pick, 1, 1))
    mod_grad = jnp.stack([shift_a_grad, scale_a_grad, gate_a_grad, shift_f_grad, scale_f_grad, gate_f_grad])
    mod_grad = lax.dot_general(
        mod_grad, pick.astype(F32), (((1,), (1,)), ((), ())), precision=lax.Precision.HIGHEST
    )
    table_grad = butterfly(mod_grad, (TP, SEQ, DP), jnp.add)
    wire.finish()
    (head_peaks,), (small,) = head_peaks, small
    down_grad = jnp.concatenate([down for _, down in ffn_grads], axis=1)
    up_grad = jnp.concatenate(
        [up[:, j * half : (j + 1) * half] for j in range(2) for up, _ in ffn_grads], axis=1
    )
    (cross_kv_grad,), (cross_q_grad, q_grad, cross_out_grad, self_out_grad) = text_grads, token_grads

    factor = jnp.repeat(jnp.sqrt(CLIP_TAU / jnp.maximum(head_peaks, CLIP_TAU)), HEAD_DIM)

    def cut(grad, count, each, size):
        grad = grad[:own_rows].reshape(own_rows, count, each)[:, :, :size]
        return grad.transpose(1, 0, 2)

    def heads(grad):
        return grad[:own_rows, :heads_width]

    taps_grad = small[:18].reshape(2, 9, hidden)[:, :, :hidden_width].transpose(1, 0, 2)
    return (
        output,
        latents_grad,
        table_grad,
        jnp.concatenate([heads(q_grad)[None], cut(kv_grads[0], 2, width, heads_width)], axis=0),
        heads(self_out_grad).T,
        heads(cross_q_grad),
        cut(cross_kv_grad, 2, width, heads_width),
        heads(cross_out_grad).T,
        cut(up_grad, 2, hidden, hidden_width),
        small[20:22, :hidden_width],
        taps_grad,
        small[18:20, :hidden_width],
        down_grad[:own_rows, :hidden_width].T,
        cross_q.astype(F32) * factor[None, :],
        cross_kv[0].astype(F32) * factor[None, :],
    )


def solution(mesh):
    tokens = P(None, DP, SEQ, None, None)
    stacked, by_column, by_row = P(None, (DP, SEQ), TP), P(TP, (DP, SEQ)), P((DP, SEQ), TP)
    return jax.shard_map(
        shards,
        mesh=mesh,
        in_specs=(
            tokens, P(None, DP, None, None), P(None, DP), P(None, DP), tokens, P(), stacked, by_column, by_row,
            stacked, by_column, stacked, P(None, TP), P(None, None, TP), P(None, TP), by_column,
        ),
        out_specs=(
            tokens, tokens, P(), stacked, by_column, by_row, stacked, by_column, stacked, P(None, TP),
            P(None, None, TP), P(None, TP), by_column, by_row, by_row,
        ),
        check_vma=False,
    )
```

```python
import functools
import math

import jax
import jax.numpy as jnp
from jax import lax
from jax.experimental import pallas as pl
from jax.experimental.pallas import tpu as pltpu
from jax.sharding import PartitionSpec as P

DP, SEQ, TP = "dp", "seq", "tensor"
HEAD_DIM = 32
LANES = 128
NORM_EPS = 1e-06
ATTN_EPS = 1e-06
CLIP_TAU = 3.5
MASKED_FILL = -1e30
F32, BF16 = jnp.float32, jnp.bfloat16
VMEM_LIMIT = 48 * 1024 * 1024


def up_to(value, step):
    return -(-value // step) * step


def dot(left, right, left_dim, right_dim):
    return lax.dot_general(
        left, right, (((left_dim,), (right_dim,)), ((), ())), preferred_element_type=F32
    )


def split(values):
    high = values.astype(BF16)
    return high, (values - high.astype(F32)).astype(BF16)


def ring_of(axis):
    size = lax.axis_size(axis)
    if axis == DP and size % 2 == 0:
        return list(range(0, size, 2)) + list(range(size - 1, 0, -2))
    return list(range(size))


def ring_place(axis):
    size, index = lax.axis_size(axis), lax.axis_index(axis)
    if axis == DP and size % 2 == 0:
        return jnp.where(index % 2 == 0, index // 2, size - 1 - index // 2)
    return index


def ring_member(axis, place):
    size = lax.axis_size(axis)
    if axis == DP and size % 2 == 0:
        return jnp.where(place < size // 2, 2 * place, 2 * (size - 1 - place) + 1)
    return place


def shift(values, axis, step):
    if isinstance(step, list):
        return lax.ppermute(values, axis, step)
    cycle = ring_of(axis)
    size = len(cycle)
    return lax.ppermute(values, axis, [(cycle[i], cycle[(i + step) % size]) for i in range(size)])


def slot_order(size):
    ahead = size // 2
    order = []
    for step in range(ahead):
        order.append(ahead - step)
        if ahead + 1 + step < size:
            order.append(ahead + 1 + step)
    return order + [0]


def chip_back(back_dp, back_seq):
    dp_size, seq_size = lax.axis_size(DP), lax.axis_size(SEQ)
    from_dp = ring_member(DP, (ring_place(DP) - back_dp) % dp_size)
    return from_dp * seq_size + (lax.axis_index(SEQ) - back_seq) % seq_size


class Wire:
    def __init__(self):
        self.running, self.queue, self.last, self.before, self.patient = [], [], (), (), False
        self.stride, self.since = lax.axis_size(DP) // 2, lax.axis_size(DP)

    def join(self, phases):
        self.running.append((phases, next(phases)))

    def push(self, phases, patient):
        self.queue.append((phases, patient))

    def round(self, hurry=False):
        if self.queue and self.since >= self.stride:
            phases, self.patient = self.queue.pop(0)
            self.join(phases)
            self.since = 0
        elif self.patient and self.since >= self.stride and not hurry:
            return
        if not self.running:
            return
        self.since += 1
        sends = [send for _, pending in self.running for send in pending]
        values = tuple(value for value, _, _ in sends)
        if self.last:
            values, _ = lax.optimization_barrier((values, self.last))
        arrived = tuple(shift(value, axis, step) for value, (_, axis, step) in zip(values, sends))
        self.before, self.last = self.last, arrived
        running, at = [], 0
        for phases, pending in self.running:
            mine = arrived[at : at + len(pending)]
            at += len(pending)
            try:
                running.append((phases, phases.send(mine)))
            except StopIteration:
                pass
        self.running = running

    def after(self, value):
        return lax.optimization_barrier((value, self.last))[0] if self.last else value

    def step(self, value, slack=False):
        value = lax.optimization_barrier((value, self.before))[0] if slack else self.after(value)
        self.round()
        return value

    def need(self, done):
        while not done:
            self.round(True)
        return done

    def finish(self):
        while self.running or self.queue:
            self.round(True)


def butterfly_phases(values, axes, combine, done):
    for axis in axes:
        size = lax.axis_size(axis)
        bit = 1
        while bit < size:
            (arrived,) = yield [(values, axis, [(i, i ^ bit) for i in range(size)])]
            values = combine(values, arrived)
            bit *= 2
    done.append(values)


def columns(values, widths):
    at, parts = 0, []
    for width in widths:
        parts.append(values[:, at : at + width])
        at += width
    return parts


def gather_phases(first, second, done):
    size = lax.axis_size(DP)
    ahead = size // 2
    widths_a, widths_b = [w.shape[1] for w in first], [w.shape[1] for w in second]
    shard_a, shard_b = jnp.concatenate(first, axis=1), jnp.concatenate(second, axis=1)
    n_a, n_b = shard_a.shape[1], shard_b.shape[1]
    rows = shard_a.shape[0]
    (far_b,) = yield [(shard_b, SEQ, 1)]
    pieces = [jnp.concatenate([shard_a, shard_b, far_b], axis=1)] + [None] * (size - 1)
    far = [None] * size
    fresh = [0]
    for hop in range(1, ahead + 2):
        sends, places = [], []
        if hop <= ahead:
            sends.append((pieces[hop - 1], DP, 1))
            places.append(hop)
        if size - hop > ahead:
            sends.append((pieces[(size - hop + 1) % size], DP, -1))
            places.append(size - hop)
        across = [pieces[a][:, :n_a] for a in fresh]
        sends.append((jnp.concatenate(across, axis=0) if len(across) > 1 else across[0], SEQ, 1))
        arrived = yield sends
        for i, a in enumerate(fresh):
            far[a] = (arrived[-1], i * rows)
        for a, piece in zip(places, arrived):
            pieces[a] = piece
        fresh = places
    arrays, moves = [], []

    def source(array):
        for place, known in enumerate(arrays):
            if known is array:
                return place
        arrays.append(array)
        return len(arrays) - 1

    for a in range(size):
        near, (across, start) = source(pieces[a]), far[a]
        across = source(across)
        at = 0
        for weight, width in enumerate(widths_a):
            moves.append((weight, a, near, 0, at, width))
            moves.append((weight, size + a, across, start, at, width))
            at += width
        for weight, width in enumerate(widths_b):
            moves.append((len(widths_a) + weight, a, near, 0, at, width))
            moves.append((len(widths_a) + weight, size + a, near, 0, at + n_b, width))
            at += width
    place = jnp.stack([chip_back(a, b).astype(jnp.int32) for b in range(2) for a in range(size)])
    done.extend(assemble(place, arrays, moves, rows, widths_a + widths_b))


def assemble_kernel(moves, rows, count, place_ref, *refs):
    sources, outs = refs[:count], refs[count:]
    for slot in range(place_ref.shape[0]):

        @pl.when(pl.program_id(0) == slot)
        def _(slot=slot):
            for weight, to, array, start, at, width in moves:
                if to == slot:
                    outs[weight][...] = sources[array][start : start + rows, at : at + width]


def assemble(place, arrays, moves, rows, widths):
    slots = place.shape[0]
    return pl.pallas_call(
        functools.partial(assemble_kernel, moves, rows, len(arrays)),
        grid_spec=pltpu.PrefetchScalarGridSpec(
            num_scalar_prefetch=1,
            grid=(slots,),
            in_specs=[
                pl.BlockSpec(array.shape, lambda i, place_ref: (0, 0), pipeline_mode=pl.Buffered(1)) for array in arrays
            ],
            out_specs=[pl.BlockSpec((rows, width), lambda i, place_ref: (place_ref[i], 0)) for width in widths],
        ),
        out_shape=[struct((slots * rows, width), BF16) for width in widths],
        compiler_params=pltpu.CompilerParams(vmem_limit_bytes=VMEM_LIMIT),
        cost_estimate=pl.CostEstimate(flops=0, bytes_accessed=slots * rows * sum(widths) * 4, transcendentals=0),
    )(place, *arrays)


def gather(wire, first, second, gate=None):
    done = []
    if wire is not None and lax.axis_size(SEQ) == 2:
        wire.push(gather_phases(first, second, done), False)
    else:
        shard = jnp.concatenate(first + second, axis=1)
        if gate is not None:
            shard, _ = lax.optimization_barrier((shard, gate))
        full = lax.all_gather(shard, (DP, SEQ), axis=0, tiled=False).reshape(-1, shard.shape[1])
        done.extend(columns(full, [w.shape[1] for w in first + second]))
    return done


def combine_kernel(near_count, flat_count, index_ref, *refs):
    near, flat, far = refs[:near_count], refs[near_count : near_count + flat_count], refs[near_count + flat_count]
    running, out = refs[near_count + flat_count + 1 : -1], refs[-1]
    at = 0
    for place, ref in enumerate(near + flat):
        width = ref.shape[1]
        part = ref[...].astype(F32)
        if place < near_count:
            part = part + far[:, at : at + width].astype(F32)
        for other in running:
            part = part + other[:, at : at + width].astype(F32)
        out[:, at : at + width] = part.astype(out.dtype)
        at += width


def combine(blocks, near_count, far, running, rows, dtype):
    steps = 3 if rows % 48 == 0 else 1
    size = rows // steps
    width = sum(array.shape[1] for array, _ in blocks)
    sources = blocks + [far] + [(array, 0) for array in running]
    index = jnp.stack([jnp.asarray(at, jnp.int32) for _, at in sources])

    def spec(place, array):
        return pl.BlockSpec((size, array.shape[1]), lambda i, index_ref: (index_ref[place] * steps + i, 0))

    return pl.pallas_call(
        functools.partial(combine_kernel, near_count, len(blocks) - near_count),
        grid_spec=pltpu.PrefetchScalarGridSpec(
            num_scalar_prefetch=1,
            grid=(steps,),
            in_specs=[spec(place, array) for place, (array, _) in enumerate(sources)],
            out_specs=pl.BlockSpec((size, width), lambda i, index_ref: (i, 0)),
        ),
        out_shape=struct((rows, width), dtype),
        compiler_params=pltpu.CompilerParams(vmem_limit_bytes=VMEM_LIMIT),
        cost_estimate=pl.CostEstimate(flops=rows * width * 4, bytes_accessed=rows * width * 10, transcendentals=0),
    )(index, *[array for array, _ in sources])


def scatter_phases(first, second, done):
    size = lax.axis_size(DP)
    ahead = size // 2
    order = slot_order(size)
    rows = first[0].shape[0] // (2 * size)
    widths = [part.shape[1] for part in first + second]
    n_a = sum(part.shape[1] for part in first)
    n_b = sum(part.shape[1] for part in second)

    def across(start, count):
        blocks = [
            [lax.dynamic_slice_in_dim(part, chip_back(order[start + i], 1) * rows, rows, 0) for part in first]
            for i in range(count)
        ]
        blocks = [jnp.concatenate(each, axis=1) if len(each) > 1 else each[0] for each in blocks]
        return (jnp.concatenate(blocks, axis=0) if count > 1 else blocks[0], SEQ, 1)

    def value(a, far, running, dtype):
        blocks = [(part, chip_back(a, 0)) for part in first]
        blocks += [(part, chip_back(a, b)) for b in range(2) for part in second]
        return combine(blocks, len(first), far[a], running, rows, dtype)

    def take(far, arrived, start):
        for i in range(arrived.shape[0] // rows):
            far[order[start + i]] = (arrived, i)

    far = {}
    (arrived,) = yield [across(0, 2)]
    take(far, arrived, 0)
    back = forth = None
    for step in range(ahead):
        sends = []
        back = value(ahead - step, far, [] if back is None else [back], BF16)
        sends.append((back, DP, -1))
        place = ahead + 1 + step
        if place < size:
            forth = value(place, far, [] if forth is None else [forth], BF16)
            sends.append((forth, DP, 1))
        start = 2 * step + 2
        if start < size:
            sends.append(across(start, min(2, size - start)))
        arrived = yield sends
        back = arrived[0]
        if place < size:
            forth = arrived[1]
        if start < size:
            take(far, arrived[-1], start)
    total = value(0, far, [back, forth], F32)
    (other,) = yield [(total[:, n_a + n_b :].astype(BF16), SEQ, 1)]
    mine = total[:, n_a : n_a + n_b] + other.astype(F32)
    done.extend(columns(total[:, :n_a], widths[: len(first)]) + columns(mine, widths[len(first) :]))


def scatter(wire, first, second):
    done = []
    if wire is not None and lax.axis_size(SEQ) == 2:
        wire.push(scatter_phases(first, second, done), True)
    else:
        parts = jnp.concatenate(first + second, axis=1)
        devices = lax.axis_size(DP) * lax.axis_size(SEQ)
        parts = parts.reshape(devices, parts.shape[0] // devices, parts.shape[1])
        total = lax.psum_scatter(parts, (DP, SEQ), scatter_dimension=0, tiled=False)
        done.extend(columns(total.astype(F32), [w.shape[1] for w in first + second]))
    return done


def butterfly(values, axes, combine):
    for axis in axes:
        size = lax.axis_size(axis)
        bit = 1
        while bit < size:
            values = combine(values, lax.ppermute(values, axis, [(i, i ^ bit) for i in range(size)]))
            bit *= 2
    return values


def other_core(values):
    return lax.ppermute(values, TP, [(0, 1), (1, 0)])


def head_block():
    row = lax.broadcasted_iota(jnp.int32, (LANES, LANES), 0) // HEAD_DIM
    col = lax.broadcasted_iota(jnp.int32, (LANES, LANES), 1) // HEAD_DIM
    return row == col


def fold(state, total):
    state = jnp.where(head_block(), state, 0.0)
    rows = sum(state[i * HEAD_DIM : (i + 1) * HEAD_DIM] for i in range(LANES // HEAD_DIM))
    return jnp.concatenate([rows, total, jnp.zeros((7, LANES), F32)], axis=0)


def unfold(folded):
    state = jnp.concatenate([folded[:HEAD_DIM]] * (LANES // HEAD_DIM), axis=0)
    return jnp.where(head_block(), state, 0.0), folded[HEAD_DIM : HEAD_DIM + 1]


def softplus(values):
    return jnp.maximum(values, 0.0) + jnp.log1p(jnp.exp(-jnp.abs(values)))


def head_sum(values):
    ones = jnp.where(head_block(), 1.0, 0.0).astype(BF16)
    high, low = split(values)
    return dot(high, ones, 1, 0) + dot(low, ones, 1, 0)


def state_kernel(key_ref, value_ref, state_ref):
    key = softplus(key_ref[...]).astype(BF16)
    value = value_ref[...].astype(BF16)
    total = jnp.sum(key.astype(F32), axis=0, keepdims=True)
    state_ref[0, 0] = fold(dot(key, value, 0, 0), total)


def ratio_parts(query_ref, state_ref):
    query = softplus(query_ref[...]).astype(BF16)
    state, total = unfold(state_ref[0, 0])
    high, low = split(state)
    numerator = dot(query, high, 1, 0) + dot(query, low, 1, 0)
    denominator = head_sum(query.astype(F32) * total) + ATTN_EPS
    return query, high, low, total, numerator, denominator


def mix_kernel(query_ref, state_ref, mixed_ref):
    query, high, low, total, numerator, denominator = ratio_parts(query_ref, state_ref)
    mixed_ref[...] = (numerator / denominator).astype(BF16)


def mix_back_kernel(query_ref, state_ref, grad_ref, query_grad_ref, state_grad_ref):
    query, high, low, total, numerator, denominator = ratio_parts(query_ref, state_ref)
    mixed_grad = grad_ref[...]
    numer_grad = mixed_grad / denominator
    denom_grad = -head_sum(mixed_grad * numerator) / (denominator * denominator)
    up, down = split(numer_grad)
    state_grad = dot(query, up, 0, 0) + dot(query, down, 0, 0)
    total_grad = jnp.sum(query.astype(F32) * denom_grad, axis=0, keepdims=True)
    state_grad_ref[0, 0] = fold(state_grad, total_grad)
    side = dot(up, high, 1, 1) + dot(up, low, 1, 1) + dot(down, high, 1, 1) + denom_grad * total
    query_grad_ref[...] = (side * jax.nn.sigmoid(query_ref[...])).astype(BF16)


def state_back_kernel(key_ref, value_ref, state_ref, out_ref):
    state, total = unfold(state_ref[0, 0])
    high, low = split(state)

    @pl.when(pl.program_id(0) == 0)
    def _():
        value = value_ref[...].astype(BF16)
        side = dot(value, high, 1, 1) + dot(value, low, 1, 1) + total
        out_ref[...] = (side * jax.nn.sigmoid(key_ref[...])).astype(BF16)

    @pl.when(pl.program_id(0) == 1)
    def _():
        key = softplus(key_ref[...]).astype(BF16)
        out_ref[...] = (dot(key, high, 1, 0) + dot(key, low, 1, 0)).astype(BF16)


def head_of(values, head):
    lane = lax.broadcasted_iota(jnp.int32, values.shape, 1) // HEAD_DIM
    return jnp.where(lane == head, values, jnp.zeros_like(values))


def weigh(key_head, query, visible):
    scores = dot(key_head, query, 1, 1) * HEAD_DIM ** (-0.5)
    masked = jnp.where(visible, scores, MASKED_FILL)
    top = jnp.max(masked, axis=0, keepdims=True)
    exponent = jnp.exp(masked - top)
    return exponent * (1.0 / jnp.sum(exponent, axis=0, keepdims=True)), top


def cross_kernel(length_ref, query_ref, key_ref, value_ref, out_ref, peak_ref):
    query, key, value = query_ref[...], key_ref[...], value_ref[...]
    tokens, slots = query.shape[0], key.shape[0]
    visible = lax.broadcasted_iota(jnp.int32, (slots, tokens), 0) < length_ref[pl.program_id(0)]
    total = jnp.zeros((LANES, tokens), F32)
    peak_ref[0, 0] = jnp.zeros((8, LANES), F32)
    for head in range(LANES // HEAD_DIM):
        probability, top = weigh(head_of(key, head), query, visible)
        total = total + dot(head_of(value, head), probability.astype(BF16), 0, 0)
        peak_ref[0, 0, head : head + 1] = jnp.broadcast_to(jnp.max(top, axis=1, keepdims=True), (1, LANES))
    out_ref[...] = total.T.astype(BF16)


def cross_back_kernel(length_ref, query_ref, key_ref, value_ref, grad_ref, query_grad_ref, key_grad_ref, value_grad_ref):
    query, key, value, grad = query_ref[...], key_ref[...], value_ref[...], grad_ref[...]
    tokens, slots = query.shape[0], key.shape[0]
    visible = lax.broadcasted_iota(jnp.int32, (slots, tokens), 0) < length_ref[pl.program_id(0)]
    query_grad = jnp.zeros((LANES, tokens), F32)
    key_grad = jnp.zeros((slots, LANES), F32)
    value_grad = jnp.zeros((slots, LANES), F32)
    for head in range(LANES // HEAD_DIM):
        key_head = head_of(key, head)
        probability, top = weigh(key_head, query, visible)
        prob_grad = dot(head_of(value, head), grad, 1, 1)
        value_grad = value_grad + head_of(dot(probability.astype(BF16), grad, 1, 0), head)
        mean = jnp.sum(probability * prob_grad, axis=0, keepdims=True)
        score_grad = (probability * (prob_grad - mean)).astype(BF16)
        key_grad = key_grad + head_of(dot(score_grad, query, 1, 0), head)
        query_grad = query_grad + dot(key_head, score_grad, 0, 0)
    scale = HEAD_DIM ** (-0.5)
    query_grad_ref[...] = (query_grad * scale).T.astype(BF16)
    key_grad_ref[...] = (key_grad * scale).astype(BF16)
    value_grad_ref[...] = value_grad.astype(BF16)


def silu(values):
    return values * jax.nn.sigmoid(values)


def silu_slope(values):
    sigma = jax.nn.sigmoid(values)
    return sigma * (1.0 + values * (1.0 - sigma))


def columns_of(values, cols):
    place = lax.broadcasted_iota(jnp.int32, values.shape, 0) % cols
    count = values.shape[0]
    left = jnp.where(place == 0, 0.0, pltpu.roll(values, 1, 0))
    right = jnp.where(place == cols - 1, 0.0, pltpu.roll(values, count - 1, 0))
    return left, values, right


def strips_of(tokens, cols):
    size = 4 * cols if tokens % (4 * cols) == 0 else cols
    return [(at, size) for at in range(0, tokens, size)]


def stage_columns(scratch, top, middle, bottom, cols):
    tokens = middle.shape[0]
    full = jnp.concatenate([top.astype(F32), middle, bottom.astype(F32)], axis=0)
    for place, part in enumerate(columns_of(full, cols)):
        scratch[place] = part


def taps(scratch, weight, at, size, cols, mirror):
    result = None
    for row_tap in range(3):
        for col_tap in range(3):
            row_at = 2 - row_tap if mirror else row_tap
            col_at = 2 - col_tap if mirror else col_tap
            tap = 3 * row_tap + col_tap
            term = scratch[col_at, at + row_at * cols : at + row_at * cols + size] * weight[tap : tap + 1]
            result = term if result is None else result + term
    return result


def conv_kernel(cols, z0, z1, top0, top1, bottom0, bottom1, grad_ref, w_ref, b_ref, gated_ref, out0, out1, small_ref, s0, s1):
    tokens = z0.shape[0]
    for z, top, bottom, scratch in ((z0, top0, bottom0, s0), (z1, top1, bottom1, s1)):
        stage_columns(scratch, top[0], silu(z[...]).astype(BF16).astype(F32), bottom[0], cols)
    sums = [jnp.zeros((8, LANES), F32) for _ in range(20)]
    for at, size in strips_of(tokens, cols):
        first = taps(s0, w_ref[0], at, size, cols, False) + b_ref[0, 0:1]
        second = taps(s1, w_ref[1], at, size, cols, False) + b_ref[1, 0:1]
        grad = grad_ref[at : at + size]
        sigma = jax.nn.sigmoid(second)
        gate = second * sigma
        gated_ref[at : at + size] = (first * gate).astype(BF16)
        slope = sigma + gate * (1.0 - sigma)
        for j, (part, scratch, out) in enumerate(
            ((grad * gate, s0, out0), (grad * first * slope, s1, out1))
        ):
            out[at : at + size] = part.astype(BF16)
            for row_tap in range(3):
                for col_tap in range(3):
                    start = at + row_tap * cols
                    product = part * scratch[col_tap, start : start + size]
                    place = 9 * j + 3 * row_tap + col_tap
                    sums[place] = sums[place] + jnp.sum(product.reshape(size // 8, 8, LANES), axis=0)
            sums[18 + j] = sums[18 + j] + jnp.sum(part.reshape(size // 8, 8, LANES), axis=0)
    for place in range(20):
        small_ref[0, place : place + 1] = jnp.sum(sums[place], axis=0, keepdims=True)
    small_ref[0, 20:24] = jnp.zeros((4, LANES), F32)


def act_back_kernel(cols, z0, z1, grad0, grad1, top0, top1, bottom0, bottom1, w_ref, out0, out1, bias_ref, s0, s1):
    tokens = z0.shape[0]
    for grad, top, bottom, scratch in ((grad0, top0, bottom0, s0), (grad1, top1, bottom1, s1)):
        stage_columns(scratch, top[0], grad[...].astype(F32), bottom[0], cols)
    for j, (z, scratch, out) in enumerate(((z0, s0, out0), (z1, s1, out1))):
        total = jnp.zeros((8, LANES), F32)
        for at, size in strips_of(tokens, cols):
            part = taps(scratch, w_ref[j], at, size, cols, True) * silu_slope(z[at : at + size])
            out[at : at + size] = part.astype(BF16)
            total = total + jnp.sum(part.reshape(size // 8, 8, LANES), axis=0)
        bias_ref[0, j : j + 1] = jnp.sum(total, axis=0, keepdims=True)
    bias_ref[0, 2:8] = jnp.zeros((6, LANES), F32)


def call(kernel, grid, in_specs, out_specs, out_shape, flops, moved, scratch=(), **extra):
    return pl.pallas_call(
        kernel,
        grid=grid,
        in_specs=in_specs,
        out_specs=out_specs,
        out_shape=out_shape,
        scratch_shapes=list(scratch),
        compiler_params=pltpu.CompilerParams(vmem_limit_bytes=VMEM_LIMIT),
        cost_estimate=pl.CostEstimate(flops=int(flops), bytes_accessed=int(moved), transcendentals=0),
        **extra,
    )


def struct(shape, dtype):
    return jax.ShapeDtypeStruct(shape, dtype)


class Kernels:
    def __init__(self, micro, tokens, cols, width, hidden, slots):
        self.micro, self.tokens, self.cols = micro, tokens, cols
        self.width, self.hidden, self.slots = width, hidden, slots
        self.groups, self.units = width // LANES, hidden // LANES

    def tile(self, offset=0):
        return pl.BlockSpec((self.tokens, LANES), lambda m, g: (m, g + offset))

    def folded(self):
        return pl.BlockSpec((1, 1, HEAD_DIM + 8, LANES), lambda m, g: (m, g, 0, 0))

    def folded_shape(self):
        return struct((self.micro, self.groups, HEAD_DIM + 8, LANES), F32)

    def states(self, keys_values):
        size = self.micro * self.tokens * self.width
        return call(
            state_kernel, (self.micro, self.groups), [self.tile(), self.tile(self.groups)],
            self.folded(), self.folded_shape(), size * 600, size * 8,
        )(keys_values, keys_values)

    def mix(self, queries, states):
        size = self.micro * self.tokens * self.width
        return call(
            mix_kernel, (self.micro, self.groups), [self.tile(), self.folded()],
            self.tile(), struct(queries.shape, BF16), size * 1500, size * 6,
        )(queries, states)

    def mix_back(self, queries, states, mixed_grad):
        size = self.micro * self.tokens * self.width
        return call(
            mix_back_kernel, (self.micro, self.groups), [self.tile(), self.folded(), self.tile()],
            [self.tile(), self.folded()], [struct(queries.shape, BF16), self.folded_shape()],
            size * 4000, size * 10,
        )(queries, states, mixed_grad)

    def states_back(self, keys_values, state_grad):
        groups = self.groups
        size = self.micro * self.tokens * self.width
        tile = lambda offset: pl.BlockSpec((self.tokens, LANES), lambda j, m, g: (m, g + offset))
        return call(
            state_back_kernel, (2, self.micro, groups),
            [tile(0), tile(groups), pl.BlockSpec((1, 1, HEAD_DIM + 8, LANES), lambda j, m, g: (m, g, 0, 0))],
            pl.BlockSpec((self.tokens, LANES), lambda j, m, g: (m, g + j * groups)),
            struct(keys_values.shape, BF16), size * 1500, size * 20,
        )(keys_values, keys_values, state_grad)

    def text_tile(self, offset):
        return pl.BlockSpec((self.slots, LANES), lambda m, g: (m, g + offset))

    def cross(self, lengths, queries, text):
        size = self.micro * self.tokens * self.width
        smem = pl.BlockSpec(memory_space=pltpu.SMEM)
        peak = pl.BlockSpec((1, 1, 8, LANES), lambda m, g: (m, g, 0, 0))
        return call(
            cross_kernel, (self.micro, self.groups),
            [smem, self.tile(), self.text_tile(0), self.text_tile(self.groups)],
            [self.tile(), peak],
            [struct(queries.shape, BF16), struct((self.micro, self.groups, 8, LANES), F32)],
            size * 20000, size * 6,
        )(lengths, queries, text, text)

    def cross_back(self, lengths, queries, text, attended_grad):
        size = self.micro * self.tokens * self.width
        smem = pl.BlockSpec(memory_space=pltpu.SMEM)
        return call(
            cross_back_kernel, (self.micro, self.groups),
            [smem, self.tile(), self.text_tile(0), self.text_tile(self.groups), self.tile()],
            [self.tile(), self.text_tile(0), self.text_tile(0)],
            [struct(queries.shape, BF16), struct((text.shape[0], self.width), BF16), struct((text.shape[0], self.width), BF16)],
            size * 50000, size * 6,
        )(lengths, queries, text, text, attended_grad)

    def edge(self, offset=0):
        return pl.BlockSpec((1, self.cols, LANES), lambda m, g: (m, 0, g + offset))

    def scratch(self):
        return pltpu.VMEM((3, self.tokens + 2 * self.cols, LANES), F32)

    def conv_specs(self):
        units = self.units
        return (
            [self.tile(), self.tile(units), self.edge(), self.edge(units), self.edge(), self.edge(units)],
            [
                pl.BlockSpec((2, 9, LANES), lambda m, g: (0, 0, g)),
                pl.BlockSpec((2, 1, LANES), lambda m, g: (0, 0, g)),
            ],
        )

    def conv(self, pre, top, bottom, grad, conv_w, conv_b):
        size = self.micro * self.tokens * self.hidden
        data, weights = self.conv_specs()
        one = struct((pre.shape[0], self.hidden), BF16)
        return call(
            functools.partial(conv_kernel, self.cols), (self.micro, self.units),
            data + [self.tile()] + weights,
            [self.tile()] * 3 + [pl.BlockSpec((1, 24, LANES), lambda m, g: (m, 0, g))],
            [one, one, one, struct((self.micro, 24, self.hidden), F32)], size * 40000, size * 16,
            [self.scratch(), self.scratch()],
        )(pre, pre, top, top, bottom, bottom, grad, conv_w, conv_b)

    def act_back(self, pre, grads, tops, bottoms, conv_w):
        size = self.micro * self.tokens * self.hidden
        data, weights = self.conv_specs()
        one = struct((pre.shape[0], self.hidden), BF16)
        return call(
            functools.partial(act_back_kernel, self.cols), (self.micro, self.units),
            data[:2] + [self.tile(), self.tile()] + [self.edge()] * 4 + weights[:1],
            [self.tile(), self.tile(), pl.BlockSpec((1, 8, LANES), lambda m, g: (m, 0, g))],
            [one, one, struct((self.micro, 8, self.hidden), F32)], size * 40000, size * 20,
            [self.scratch(), self.scratch()],
        )(pre, pre, *grads, *tops, *bottoms, conv_w)


def pad_to(values, *sizes):
    return jnp.pad(values, [(0, size - now) for size, now in zip(sizes, values.shape)])


def side_by_side(parts, width):
    return jnp.concatenate([pad_to(part, part.shape[0], width) for part in parts], axis=1)


def halos(rows, cols):
    size = lax.axis_size(SEQ)
    up = [(i, i + 1) for i in range(size - 1)]
    down = [(j, i) for i, j in up]
    return (
        lax.ppermute(rows[:, -cols:], SEQ, up),
        lax.ppermute(rows[:, :cols], SEQ, down),
    )


def shards(latents, text, timesteps, text_lengths, cotangent, table, self_qkv, self_out, cross_q, cross_kv,
           cross_out, up_w, up_b, conv_w, conv_b, down_w):
    micro, _, row_count, cols, features = latents.shape
    tokens = row_count * cols
    own_rows, heads_width = cross_q.shape
    hidden_width = up_b.shape[1]
    text_len = text.shape[2]
    width, hidden, slots = up_to(heads_width, LANES), up_to(hidden_width, 2 * LANES), up_to(text_len, 16)
    rows = up_to(own_rows, 16)
    dp_size, seq_size = lax.axis_size(DP), lax.axis_size(SEQ)
    wide = dp_size * seq_size * rows
    core = lax.axis_index(TP)
    kernels = Kernels(micro, tokens, cols, width, hidden // 2, slots)

    half = hidden // 2

    def units(values, at):
        return pad_to(values[:, at * half : (at + 1) * half], values.shape[0], half)

    def heads_rows(*parts):
        return pad_to(side_by_side(parts, width), rows, len(parts) * width)

    def ffn_rows(at):
        up = jnp.concatenate([units(up_w[0], at), units(up_w[1], at)], axis=1)
        return [pad_to(up, rows, 2 * half)], [pad_to(units(down_w.T, at), rows, half)]

    wire = Wire()
    qkv_rows = gather(wire, [heads_rows(self_qkv[1], self_qkv[2])], [heads_rows(self_qkv[0])])
    token_rows = gather(wire, [heads_rows(cross_q)], [heads_rows(self_out.T)])
    text_rows = gather(wire, [heads_rows(cross_kv[0], cross_kv[1])], [heads_rows(cross_out.T)])

    unit_rows = [gather(wire, *ffn_rows(at)) for at in range(2)]

    slot = jnp.arange(wide)
    valid = slot % rows < own_rows
    channel = jnp.where(valid, slot // rows * own_rows + slot % rows, -1)
    pick = (jnp.arange(features)[:, None] == channel[None, :]).astype(BF16)

    def relative(values):
        return jnp.where(core == 0, values, jnp.flip(values, axis=0))

    lengths = relative(text_lengths[:, 0])
    caption = jnp.pad(relative(text[:, 0]), ((0, 0), (0, slots - text_len), (0, 0))).reshape(micro * slots, features)
    caption = dot(caption, pick, 1, 0).astype(BF16)
    resid_in = dot(lax.dynamic_index_in_dim(latents, core, 0, False).reshape(tokens, features), pick, 1, 0)
    grad_out = dot(lax.dynamic_index_in_dim(cotangent, core, 0, False).reshape(tokens, features), pick, 1, 0)

    frequency = jnp.exp(-math.log(10000.0) * channel.astype(F32) / features)
    time = lax.dynamic_index_in_dim(timesteps[:, 0], core, 0, False).astype(F32)
    waves = 0.5 * jnp.sin(time * frequency[None, :] + jnp.arange(6, dtype=F32)[:, None])
    mod_table = jnp.dot(table, pick.astype(F32), precision=lax.Precision.HIGHEST)
    modulation = jnp.where(valid[None, :], mod_table + waves, 0.0)
    shift_a, scale_a, gate_a, shift_f, scale_f, gate_f = [modulation[i] for i in range(6)]

    def normalise(values):
        center = jnp.where(valid[None, :], values - jnp.sum(values, axis=1, keepdims=True) / features, 0.0)
        spread = jnp.sum(center * center, axis=1, keepdims=True) / features
        inverse = lax.rsqrt(spread + NORM_EPS)
        return center * inverse, inverse

    def normalise_back(values, grad, stretch):
        unit, inverse = normalise(values)
        shift_grad = jnp.sum(grad, axis=0)
        scale_grad = jnp.sum(grad * unit, axis=0)
        scaled = grad * (1.0 + stretch)
        mean = jnp.sum(scaled, axis=1, keepdims=True) / features
        along = jnp.sum(scaled * unit, axis=1, keepdims=True) / features
        return jnp.where(valid[None, :], inverse * (scaled - mean - unit * along), 0.0), shift_grad, scale_grad

    def both(own):
        return jnp.concatenate([own, other_core(own)], axis=0)

    def core_total(parts):
        def product(at):
            return sum(dot(left[at : at + tokens], right, 1, dim) for left, right, dim in parts)

        return other_core(product(tokens).astype(BF16)).astype(F32) + product(0)

    ffn_out_grad = both((gate_f * grad_out).astype(BF16))

    def weight_grad(activation, grad):
        return dot(activation, grad, 0, 0).astype(BF16)

    unit_a, _ = normalise(resid_in)
    normed = both((unit_a * (1.0 + scale_a) + shift_a).astype(BF16))
    w_kv, w_q = wire.need(qkv_rows)
    keys_values = dot(normed, w_kv, 1, 0)
    states = butterfly(kernels.states(keys_values), (SEQ,), jnp.add)
    queries = dot(wire.step(normed), w_q, 1, 0)
    mixed = kernels.mix(queries, wire.step(states))
    w_cq, w_so = wire.need(token_rows)
    self_term = core_total([(mixed, w_so, 1)])
    resid_a = resid_in + gate_a * self_term
    cross_input = both(resid_a.astype(BF16))
    cross_query = dot(cross_input, w_cq, 1, 0).astype(BF16)
    w_ckv, w_co = wire.need(text_rows)
    text_proj = dot(caption, w_ckv, 1, 0).astype(BF16)
    attended, peaks = kernels.cross(lengths, cross_query, wire.step(text_proj))
    head_count = heads_width // HEAD_DIM
    head_peaks = []
    own_peaks = jnp.max(peaks[:, :, : LANES // HEAD_DIM, 0], axis=0).reshape(-1)[:head_count]
    wire.join(butterfly_phases(own_peaks, (SEQ, DP), jnp.maximum, head_peaks))
    resid_b = resid_a + core_total([(wire.step(attended), w_co, 1)])
    unit_f, _ = normalise(resid_b)
    normed_ffn = both((unit_f * (1.0 + scale_f) + shift_f).astype(BF16))

    ffn_terms, backs, smalls, ffn_grads = [], [], [], []
    for at in range(2):
        w_up, w_down = wire.need(unit_rows[at])
        if at == 1:
            early, _ = lax.optimization_barrier((early, w_down))
            ffn_grads.append([part for parts in early for part in scatter(None, [parts], [])])
        bias = jnp.concatenate([units(up_b[0:1], at), units(up_b[1:2], at)], axis=1)
        filters = jnp.stack([units(conv_w[:, j], at) for j in range(2)])
        filter_bias = jnp.stack([units(conv_b[j : j + 1], at) for j in range(2)])
        pre = dot(wire.step(normed_ffn) if at == 0 else normed_ffn, w_up, 1, 0) + bias
        by_micro = pre.reshape(micro, tokens, 2 * half)
        edges = jnp.concatenate([by_micro[:, :cols], by_micro[:, -cols:]], axis=1)
        top, bottom = halos(silu(edges).astype(BF16), cols)
        gated_grad = dot(ffn_out_grad, w_down, 1, 0)
        if at == 0:
            pre, top, bottom = wire.step((pre, top, bottom))
        gated, conv_grad0, conv_grad1, small = kernels.conv(pre, top, bottom, gated_grad, filters, filter_bias)
        edges = [grad.reshape(micro, tokens, half) for grad in (conv_grad0, conv_grad1)]
        edges = jnp.concatenate(
            [jnp.concatenate([grad[:, :cols], grad[:, -cols:]], axis=1) for grad in edges], axis=2
        )
        top_grad, bottom_grad = halos(edges, cols)
        down_parts = weight_grad(ffn_out_grad, gated)
        if at == 0:
            top_grad, bottom_grad = wire.step((top_grad, bottom_grad))
        up_low0, up_low1, bias_grad = kernels.act_back(
            pre, (conv_grad0, conv_grad1), [top_grad[:, :, :half], top_grad[:, :, half:]],
            [bottom_grad[:, :, :half], bottom_grad[:, :, half:]], filters,
        )
        smalls.append(jnp.concatenate([jnp.sum(small, axis=0)[:20], jnp.sum(bias_grad, axis=0)[:2]], axis=0))
        if at == 0:
            up_low0, up_low1 = wire.step((up_low0, up_low1))
        up_low = jnp.concatenate([up_low0, up_low1], axis=1)
        up_parts = weight_grad(normed_ffn, up_low)
        if at == 0:
            early = (up_parts, down_parts)
            normed_ffn, _ = lax.optimization_barrier((normed_ffn, early))
        else:
            ffn_grads.append(scatter(wire, [up_parts], [down_parts]))
            up_low, _ = lax.optimization_barrier((up_low, (up_parts, down_parts)))
        ffn_terms.append((gated, w_down, 1))
        backs.append((up_low, w_up, 1))

    backs[1] = (wire.step(up_low, True), *backs[1][1:])
    normed_ffn_grad = core_total(backs)
    resid_b_part, shift_f_grad, scale_f_grad = normalise_back(resid_b, normed_ffn_grad, scale_f)
    resid_b_grad = grad_out + resid_b_part
    cross_grad = both(wire.step(resid_b_grad, True).astype(BF16))
    attended_grad = dot(cross_grad, w_co, 1, 0).astype(BF16)
    query_grad, key_grad, value_grad = kernels.cross_back(lengths, cross_query, text_proj, wire.step(attended_grad, True))
    (query_grad, key_grad, value_grad), _ = lax.optimization_barrier(((query_grad, key_grad, value_grad), ffn_grads[0][1]))
    query_grad, key_grad, value_grad = wire.step((query_grad, key_grad, value_grad), True)
    cross_out_parts = weight_grad(cross_grad, attended)
    cross_kv_parts = weight_grad(caption, jnp.concatenate([key_grad, value_grad], axis=1))
    text_grads = scatter(None, [cross_kv_parts], [])
    resid_a_grad = resid_b_grad + core_total([(wire.step(query_grad, True), w_cq, 1)])
    cross_q_parts = weight_grad(cross_input, query_grad)
    gate_a_grad = jnp.sum(resid_a_grad * self_term, axis=0)
    self_grad = both((gate_a * resid_a_grad).astype(BF16))
    mixed_grad = dot(wire.step(self_grad, True), w_so, 1, 0)
    mixed_grad, _ = lax.optimization_barrier((mixed_grad, ffn_grads[0][0]))
    q_low, state_grad = kernels.mix_back(queries, states, wire.step(mixed_grad, True))
    self_out_parts = weight_grad(self_grad, mixed)
    state_grad = butterfly(state_grad, (SEQ,), jnp.add)
    small = []
    wire.join(butterfly_phases(jnp.concatenate(smalls, axis=1), (SEQ, DP), jnp.add, small))
    token_grads = scatter(wire, [cross_q_parts, weight_grad(normed, q_low)], [self_out_parts, cross_out_parts])
    kv_low = kernels.states_back(keys_values, wire.step(state_grad, True))
    kv_parts = weight_grad(normed, kv_low)
    kv_low, _ = lax.optimization_barrier((wire.step(kv_low, True), (text_grads, kv_parts)))
    kv_grads = scatter(None, [kv_parts], [])
    normed_grad = core_total([(q_low, w_q, 1), (kv_low, w_kv, 1)])
    resid_part, shift_a_grad, scale_a_grad = normalise_back(resid_in, wire.step(normed_grad, True), scale_a)
    latent_grad = resid_a_grad + resid_part
    ffn_terms = wire.after([left for left, _, _ in ffn_terms])
    ffn_out = core_total([(left, rows_of[1], 1) for left, rows_of in zip(ffn_terms, unit_rows)])
    resid_c = resid_b + gate_f * ffn_out
    gate_f_grad = jnp.sum(grad_out * ffn_out, axis=0)

    def whole(own):
        other = other_core(own)
        pair = jnp.where(core == 0, jnp.stack([own, other]), jnp.stack([other, own]))
        return pair.reshape(micro, 1, row_count, cols, features)

    high, low = split(latent_grad)
    output = whole(dot(resid_c.astype(BF16), pick, 1, 1).astype(BF16))
    latents_grad = whole(dot(high, pick, 1, 1) + dot(low, pick, 1, 1))
    mod_grad = jnp.stack([shift_a_grad, scale_a_grad, gate_a_grad, shift_f_grad, scale_f_grad, gate_f_grad])
    mod_grad = lax.dot_general(
        mod_grad, pick.astype(F32), (((1,), (1,)), ((), ())), precision=lax.Precision.HIGHEST
    )
    table_grads = []
    wire.join(butterfly_phases(butterfly(mod_grad, (TP,), jnp.add), (SEQ, DP), jnp.add, table_grads))
    wire.finish()
    (table_grad,), (head_peaks,), (small,) = table_grads, head_peaks, small
    down_grad = jnp.concatenate([down for _, down in ffn_grads], axis=1)
    up_grad = jnp.concatenate(
        [up[:, j * half : (j + 1) * half] for j in range(2) for up, _ in ffn_grads], axis=1
    )
    (cross_kv_grad,), (cross_q_grad, q_grad, self_out_grad, cross_out_grad) = text_grads, token_grads

    factor = jnp.repeat(jnp.sqrt(CLIP_TAU / jnp.maximum(head_peaks, CLIP_TAU)), HEAD_DIM)

    def cut(grad, count, each, size):
        grad = grad[:own_rows].reshape(own_rows, count, each)[:, :, :size]
        return grad.transpose(1, 0, 2)

    def heads(grad):
        return grad[:own_rows, :heads_width]

    taps_grad = small[:18].reshape(2, 9, hidden)[:, :, :hidden_width].transpose(1, 0, 2)
    return (
        output,
        latents_grad,
        table_grad,
        jnp.concatenate([heads(q_grad)[None], cut(kv_grads[0], 2, width, heads_width)], axis=0),
        heads(self_out_grad).T,
        heads(cross_q_grad),
        cut(cross_kv_grad, 2, width, heads_width),
        heads(cross_out_grad).T,
        cut(up_grad, 2, hidden, hidden_width),
        small[20:22, :hidden_width],
        taps_grad,
        small[18:20, :hidden_width],
        down_grad[:own_rows, :hidden_width].T,
        cross_q.astype(F32) * factor[None, :],
        cross_kv[0].astype(F32) * factor[None, :],
    )


def solution(mesh):
    tokens = P(None, DP, SEQ, None, None)
    stacked, by_column, by_row = P(None, (DP, SEQ), TP), P(TP, (DP, SEQ)), P((DP, SEQ), TP)
    return jax.shard_map(
        shards,
        mesh=mesh,
        in_specs=(
            tokens, P(None, DP, None, None), P(None, DP), P(None, DP), tokens, P(), stacked, by_column, by_row,
            stacked, by_column, stacked, P(None, TP), P(None, None, TP), P(None, TP), by_column,
        ),
        out_specs=(
            tokens, tokens, P(), stacked, by_column, by_row, stacked, by_column, stacked, P(None, TP),
            P(None, None, TP), P(None, TP), by_column, by_row, by_row,
        ),
        check_vma=False,
    )
```
